512 devices in a mesh: pp: 4 (over x), ep: 32 (over y_hi, z), tp: 4 (over y_lo, core).
Axes of the slice: x: 4, y: 8 (y_hi: 4, y_lo: 2; y = y_hi * 2 + y_lo), z: 8, core: 2. Of those that a mesh axis runs over, the one named last changes fastest.
Arguments:
- trunk_in: bfloat16 [4, 4096, 2048], P('pp', 'ep'), may hold values from -6 to 6
- expert_ids: int32 [4, 4096, 8], P('pp', 'ep'), may hold values from 0 to 31, all different within a row; in each aligned block of 128 rows (0 to 127, 128 to 255, ..., all dimensions but the last counted through in order) at most 40 rows name the same one
- gate_scores: float32 [4, 4096, 8], P('pp', 'ep'), may hold values from 0.05 to 1
- trunk_gain: float32 [4, 2048], P('pp'), may hold values from 0.1 to 1.9
- w_gate: bfloat16 [4, 32, 2048, 768], P('pp', 'ep', None, 'tp'), may hold values from -0.125 to 0.125
- w_up: bfloat16 [4, 32, 2048, 768], P('pp', 'ep', None, 'tp'), may hold values from -0.125 to 0.125
- w_down: bfloat16 [4, 32, 768, 2048], P('pp', 'ep', 'tp'), may hold values from -0.21875 to 0.21875
- image_in: bfloat16 [4, 128, 3200], P('pp', ('ep', 'tp')), may hold values from -6 to 6
- image_gain: float32 [4, 3200], P('pp'), may hold values from 0.1 to 1.9
- fc_in: bfloat16 [4, 3200, 12800], P('pp', None, ('ep', 'tp')), may hold values from -0.109375 to 0.109375
- fc_out: bfloat16 [4, 12800, 3200], P('pp', ('ep', 'tp')), may hold values from -0.0546875 to 0.0546875
- layer_scale: float32 [4, 3200], P('pp'), may hold values from 0.5 to 1.5
Outputs:
- trunk_out: bfloat16 [4, 4096, 2048], P('pp', 'ep')
- image_out: bfloat16 [4, 128, 3200], P('pp', ('ep', 'tp'))
The draws below stay inside these ranges and needn't reach their ends.
Inputs may be any that keep to these rules, and one draw needn't show every extreme that they name: `expert_ids`: within each aligned block of 128 rows of one section (the rows of one device), no expert is named by more than 40 rows, a bound that some block reaches.
All inputs are finite; a program needn't handle non-finite values.
Results may differ from the reference program's by a relative error of at most 0.008.
Values may be sent and summed in bfloat16 or wider, within the bound.
No kernel may reach another device: no remote copies, remote signals or barrier semaphores. Data moves between devices by JAX's collectives and lax.ppermute only.
A program may use at most 64 MiB of HBM per device.

```python
import math
import jax
import jax.numpy as jnp
import numpy as np
from jax import lax

D = 2048
FF = 768
DV = 3200
FV = 12800
TOK_DEV = 128
EXPERTS = 32
TOPK = 8
CAP = 40
TOKENS = 4096
IMG = 128
N_PP = 4
N_EP = 32
N_TP = 4


def block_scale(stream_key, dims, cuts, smallest, top_value):
    level, own = 1.0, jax.random.fold_in(stream_key, 6)
    for dim, parts in cuts:
        steps = jnp.exp(jax.random.uniform(jax.random.fold_in(own, dim), (parts,), jnp.float32, smallest / len(cuts), top_value / len(cuts)))
        level = level * jnp.repeat(steps, dims[dim] // parts).reshape([-1 if axis == dim else 1 for axis in range(len(dims))])
    return level


def deal_out(key, own, number, rows, amount, top, most, slope):
    order = jax.random.permutation(key, amount)
    crowded, usual = shares(amount, rows * top, most, slope, True), shares(amount, rows * top, most, slope, False)
    places = jnp.arange(amount)

    def named(tallies, rotation):
        used = int((tallies > 0).sum())
        fixed = max(1, used // 4)
        passed = fixed + (places - fixed + rotation * (used - fixed)) % max(1, amount - fixed)
        return jnp.zeros((amount,), jnp.int32).at[order[jnp.where(places < fixed, places, passed)]].set(jnp.asarray(tallies, jnp.int32))

    tallies = jnp.where(number % 4 == 0, named(crowded, number // 4), named(usual, number - number // 4 - 1))
    mixed = jax.random.permutation(jax.random.fold_in(own, 3), amount)
    donor, sink = mixed[0:amount // 2 * 2:2], mixed[1:amount // 2 * 2:2]
    slack = jnp.minimum(tallies[donor] - 1, most - tallies[sink]) // 2
    slack = jnp.where((donor == order[0]) | (sink == order[0]) | (tallies[sink] == 0), 0, jnp.maximum(slack, 0))
    passed = jax.random.randint(jax.random.fold_in(own, 4), (amount // 2,), 0, 1 << 20) % (slack + 1)
    tallies = tallies.at[donor].add(-passed).at[sink].add(passed)
    members = jnp.searchsorted(jnp.cumsum(tallies), jnp.arange(rows * top), side="right").astype(jnp.int32)
    listing = members.reshape(top, rows).T
    listing = listing[jax.random.permutation(jax.random.fold_in(own, 1), rows)]
    rotation = jax.random.randint(jax.random.fold_in(own, 2), (rows, 1), 0, top)
    return jnp.take_along_axis(listing, (jnp.arange(top)[None, :] + rotation) % top, axis=1)


def shares(amount, total, most, skew, full):
    portions = [(1 << 20) // math.isqrt(grade ** skew) + 1 for grade in range(1, amount + 1)]
    largest = most if full else min(most, max(-(-total // amount), total * portions[0] // sum(portions)))
    least = 1 if total - largest >= amount - 1 else 0
    given, spare = [largest] + [least] * (amount - 1), total - largest - least * (amount - 1)
    while spare > 0:
        candidates = [i for i in range(1, amount) if given[i] < largest] or [i for i in range(1, amount) if given[i] < most]
        mass, left = sum([portions[i] for i in candidates]), spare
        for i in candidates:
            more = min(most - given[i], max(1, left * portions[i] // mass), spare)
            given[i] = given[i] + more
            spare = spare - more
    return np.array(given)


def normal_values(own_key, shape, spread, most, shards=(), kind=jnp.bfloat16):
    array = jax.random.normal(own_key, shape, jnp.float32) * spread
    if len(shards) > 0:
        array = block_scale(own_key, shape, shards, -0.22, 0.18) * array
    return jnp.clip(array, min=-most, max=most).astype(kind)


def setup_inputs(seed: int = 0) -> dict:
    key_list = jax.random.split(jax.random.key(seed), 13)
    trunk_in = normal_values(key_list[0], (N_PP, TOKENS, D), 1.0, 6.0, ((0, 4), (1, 32)))
    expert_ids_keys = jax.random.split(jax.random.fold_in(key_list[1], 1), N_PP * TOKENS // TOK_DEV)
    expert_ids_turns = jax.random.permutation(jax.random.fold_in(key_list[1], 3), N_PP * TOKENS // TOK_DEV)
    expert_ids = jax.vmap(lambda own, number: deal_out(jax.random.fold_in(key_list[1], 2), own, number, TOK_DEV, EXPERTS, TOPK, CAP, 2))(expert_ids_keys, expert_ids_turns).reshape((N_PP, TOKENS, TOPK))
    gate_scores = jnp.clip(jnp.exp(math.log(1.0) - 2.9957323 * jax.random.uniform(key_list[2], (N_PP, TOKENS, TOPK), jnp.float32) ** block_scale(key_list[2], (N_PP, TOKENS, TOPK), ((0, 4), (1, 32)), -0.2, 0.2)), 0.05, 1.0)
    trunk_gain = jnp.clip(1.0 + 0.18 * jax.random.normal(key_list[3], (N_PP, D), jnp.float32), 0.1, 1.9)
    w_gate = normal_values(key_list[4], (N_PP, EXPERTS, D, FF), D ** -0.5, 0.125, ((0, 4), (1, 32), (3, 4)))
    w_up = normal_values(key_list[5], (N_PP, EXPERTS, D, FF), D ** -0.5, 0.125, ((0, 4), (1, 32), (3, 4)))
    w_down = normal_values(key_list[6], (N_PP, EXPERTS, FF, D), FF ** -0.5, 0.21875, ((0, 4), (1, 32), (2, 4)))
    image_in = normal_values(key_list[7], (N_PP, IMG, DV), 1.0, 6.0, ((0, 4), (1, 128)))
    image_gain = jnp.clip(1.0 + 0.18 * jax.random.normal(key_list[8], (N_PP, DV), jnp.float32), 0.1, 1.9)
    fc_in = normal_values(key_list[9], (N_PP, DV, FV), DV ** -0.5, 0.109375, ((0, 4), (2, 128)))
    fc_out = normal_values(key_list[10], (N_PP, FV, DV), FV ** -0.5, 0.0546875, ((0, 4), (1, 128)))
    layer_scale = jnp.clip(0.5 + 1.0 * jax.random.uniform(key_list[11], (N_PP, DV), jnp.float32) ** block_scale(key_list[11], (N_PP, DV), ((0, 4),), -0.2, 0.2), 0.5, 1.5)
    return dict(trunk_in=trunk_in, expert_ids=expert_ids, gate_scores=gate_scores, trunk_gain=trunk_gain, w_gate=w_gate, w_up=w_up, w_down=w_down, image_in=image_in, image_gain=image_gain, fc_in=fc_in, fc_out=fc_out, layer_scale=layer_scale)


def rms_scale(values, gain):
    wide = values.astype(jnp.float32)
    return wide * lax.rsqrt(lax.optimization_barrier(jnp.mean(wide * wide, axis=-1, keepdims=True)) + 1e-06) * gain

def place(dest, n_exp, cap):
    onehot = (dest[:, None] == jnp.arange(n_exp, dtype=jnp.int32)[None, :]).astype(jnp.int32)
    rank = lax.optimization_barrier(jnp.sum((jnp.cumsum(onehot, axis=0) - onehot) * onehot, axis=1))
    return (dest * cap + rank).astype(jnp.int32)

def owners(slot, count, rows, topk):
    entry_token = (jnp.arange(slot.shape[0], dtype=jnp.int32) // topk).astype(jnp.int32)
    return jnp.full((count,), rows, jnp.int32).at[slot].set(entry_token)

def trunk_section(tokens, ids, scores, gain, gate_w, up_w, down_w):
    normed = rms_scale(tokens, gain).astype(jnp.bfloat16)
    blocks = normed.reshape(N_EP, TOK_DEV, D)
    id_blocks = ids.reshape(N_EP, TOK_DEV * TOPK)

    def pack(pair):
        block, chosen = pair
        slot = place(chosen, EXPERTS, CAP)
        table = owners(slot, EXPERTS * CAP, TOK_DEV, TOPK)
        padded = jnp.concatenate([block, jnp.zeros((1, D), jnp.bfloat16)], axis=0)
        return (padded[table].reshape(EXPERTS, CAP, D), slot)
    slots, slot_ids = lax.map(pack, (blocks, id_blocks))
    quarter = FF // N_TP

    def expert(group):
        rows, gw, uw, dw = group
        flat = rows.reshape(-1, D)
        gate = jnp.dot(flat, gw, preferred_element_type=jnp.float32)
        upval = jnp.dot(flat, uw, preferred_element_type=jnp.float32)
        hidden = (jax.nn.silu(gate) * upval).astype(jnp.bfloat16)
        total = jnp.zeros((flat.shape[0], D), jnp.float32)
        for part in range(N_TP):
            piece = jnp.dot(hidden[:, part * quarter:(part + 1) * quarter], dw[part * quarter:(part + 1) * quarter], preferred_element_type=jnp.float32).astype(jnp.bfloat16)
            piece = lax.optimization_barrier(piece)
            total = total + piece.astype(jnp.float32)
        return total.reshape(N_EP, CAP, D)
    outputs = lax.map(expert, (jnp.transpose(slots, (1, 0, 2, 3)), gate_w, up_w, down_w))
    by_source = jnp.transpose(outputs, (1, 0, 2, 3))
    score_blocks = scores.reshape(N_EP, TOK_DEV, TOPK)
    token_blocks = tokens.reshape(N_EP, TOK_DEV, D)

    def combine(group):
        made, slot, score, block = group
        picked = made.reshape(-1, D)[slot].reshape(TOK_DEV, TOPK, D)
        weights = score / lax.optimization_barrier(jnp.sum(score, axis=-1, keepdims=True))
        added = lax.optimization_barrier(jnp.sum(picked * weights[:, :, None], axis=1))
        return (block.astype(jnp.float32) + added).astype(jnp.bfloat16)
    return lax.map(combine, (by_source, slot_ids, score_blocks, token_blocks)).reshape(TOKENS, D)

def encoder_section(image, gain, first, second, scale):
    normed = rms_scale(image, gain).astype(jnp.bfloat16)
    hidden = jax.nn.gelu(jnp.dot(normed, first, preferred_element_type=jnp.float32), approximate=False).astype(jnp.bfloat16)
    summed = jnp.dot(hidden, second, preferred_element_type=jnp.float32)
    return (image.astype(jnp.float32) + scale * summed).astype(jnp.bfloat16)

def reference(trunk_in, expert_ids, gate_scores, trunk_gain, w_gate, w_up, w_down, image_in, image_gain, fc_in, fc_out, layer_scale):
    layers = []
    encoded = []
    for section in range(N_PP):
        layers.append(trunk_section(trunk_in[section], expert_ids[section], gate_scores[section], trunk_gain[section], w_gate[section], w_up[section], w_down[section]))
        encoded.append(encoder_section(image_in[section], image_gain[section], fc_in[section], fc_out[section], layer_scale[section]))
    trunk_out = jnp.roll(jnp.stack(layers), 1, axis=0)
    image_out = jnp.roll(jnp.stack(encoded), -1, axis=0)
    return (trunk_out, image_out)
```

```python
import jax
import jax.numpy as jnp
import numpy as np
from jax import lax
from jax.experimental import pallas as pl
from jax.experimental.pallas import tpu as pltpu
from jax.sharding import Mesh, PartitionSpec as P

BF16 = jnp.bfloat16
F32 = jnp.float32
VM = pl.BlockSpec(memory_space=pltpu.VMEM)
SM = pl.BlockSpec(memory_space=pltpu.SMEM)
CAP = 40
LIMIT = 48 * 1024 * 1024


def call(kernel, outs, scalars=0, flops=0, moved=0):
    def run(*operands):
        specs = [SM] * scalars + [VM] * (len(operands) - scalars)
        return pl.pallas_call(
            kernel,
            out_shape=outs,
            in_specs=specs,
            out_specs=jax.tree.map(lambda _: VM, outs),
            compiler_params=pltpu.CompilerParams(vmem_limit_bytes=LIMIT),
            cost_estimate=pl.CostEstimate(flops=flops, bytes_accessed=moved, transcendentals=0),
        )(*operands)

    return run


def shaped(dims, kind=BF16):
    return jax.ShapeDtypeStruct(dims, kind)


def nt(a, b):
    return lax.dot_general(a, b, (((1,), (1,)), ((), ())), preferred_element_type=F32)


def table_kernel(where, meta, pick, high, low):
    rows, toks = pick.shape
    group = rows // CAP
    topk = meta.shape[0] // 2
    first = where[0] * group
    wanted = (lax.broadcasted_iota(jnp.int32, (group, toks), 0) + first).astype(F32)
    scores = meta[topk:, :]
    total = jnp.sum(scores, axis=0, keepdims=True)
    member = jnp.zeros((group, toks), F32)
    weight = jnp.zeros((group, toks), F32)
    for k in range(topk):
        same = meta[k : k + 1, :] == wanted
        member = jnp.where(same, 1.0, member)
        weight = jnp.where(same, meta[topk + k : topk + k + 1, :] / total, weight)
    earlier = lax.broadcasted_iota(jnp.int32, (toks, toks), 0) < lax.broadcasted_iota(jnp.int32, (toks, toks), 1)
    rank = jnp.dot(member.astype(BF16), earlier.astype(F32).astype(BF16), preferred_element_type=F32)
    rank = jnp.where(member > 0.5, rank, -1.0)
    slots = lax.broadcasted_iota(jnp.int32, (group, CAP, toks), 1).astype(F32)
    hit = jnp.where(rank[:, None, :] == slots, 1.0, 0.0)
    pick[...] = hit.reshape(rows, toks).astype(BF16)
    scaled = (hit * weight[:, None, :]).reshape(rows, toks).T
    top = scaled.astype(BF16)
    high[...] = top
    low[...] = (scaled - top.astype(F32)).astype(BF16)


def pack_kernel(pick, toks, gain, rows):
    wide = toks[...].astype(F32)
    scale = lax.rsqrt(jnp.mean(wide * wide, axis=-1, keepdims=True) + 1e-06)
    normed = (wide * scale * gain[...]).astype(BF16)
    rows[...] = jnp.dot(pick[...], normed, preferred_element_type=F32).astype(BF16)


def expert_kernel(*refs):
    rows, out = refs[0], refs[-1]
    flat = rows[...]
    total = None
    for s in range(4):
        gate_w, up_w, down_w = refs[1 + 3 * s : 4 + 3 * s]
        gate = nt(flat, gate_w[...])
        upval = nt(flat, up_w[...])
        hidden = (gate * jax.nn.sigmoid(gate) * upval).astype(BF16)
        made = jnp.dot(hidden, down_w[...], preferred_element_type=F32)
        total = made if total is None else total + made
    out[...] = total.astype(BF16)


def combine_kernel(where, high, low, made, *pieces):
    n = len(pieces)
    cols = made.shape[1] // n
    for k in range(n):
        q = lax.rem(where[0] + k, n)
        part = made[:, pl.ds(pl.multiple_of(q * cols, cols), cols)]
        summed = jnp.dot(high[...], part, preferred_element_type=F32)
        summed += jnp.dot(low[...], part, preferred_element_type=F32)
        pieces[k][...] = summed.astype(BF16)


def layer_kernel(where, toks, *refs):
    pieces, out = refs[:-1], refs[-1]
    cols = out.shape[1]
    total = toks[:, pl.ds(pl.multiple_of(where[1] * cols, cols), cols)].astype(F32)
    for piece in pieces:
        total += piece[...].astype(F32)
    out[...] = total.astype(BF16)


def join_kernel(where, own, across, other, other_across, out):
    cols = own.shape[1]
    t = where[1]
    yl, core = t // 2, lax.rem(t, 2)
    for ref, quarter in (
        (own, t),
        (across, (1 - yl) * 2 + core),
        (other, yl * 2 + 1 - core),
        (other_across, (1 - yl) * 2 + 1 - core),
    ):
        out[:, pl.ds(pl.multiple_of(quarter * cols, cols), cols)] = ref[...]


def rms_scale(values, gain):
    wide = values.astype(F32)
    return wide * lax.rsqrt(jnp.mean(wide * wide, axis=-1, keepdims=True) + 1e-06) * gain


def body(
    trunk_in,
    expert_ids,
    gate_scores,
    trunk_gain,
    w_gate,
    w_up,
    w_down,
    image_in,
    image_gain,
    fc_in,
    fc_out,
    layer_scale,
):
    n_pp, n_yh, n_z = (lax.axis_size(a) for a in ("pp", "yh", "z"))
    n_tp = 4
    square = ("yh", "yl", "core")
    where = jnp.stack([lax.axis_index("yh"), lax.axis_index(("yl", "core"))]).astype(jnp.int32)

    def swapped(value):
        return lax.ppermute(value, square, [(a * n_tp + b, b * n_tp + a) for a in range(n_yh) for b in range(n_tp)])

    def flipped(value, axis):
        return lax.ppermute(value, axis, [(0, 1), (1, 0)])

    tokens = trunk_in[0]
    width = tokens.shape[1]
    toks = tokens.shape[0]
    meta = jnp.concatenate([expert_ids[0].T.astype(F32), gate_scores[0].T], axis=0)
    meta = swapped(meta)
    sent = swapped(tokens)

    own = [w_gate[0, 0].T, w_up[0, 0].T, w_down[0, 0]]
    across = [flipped(w, "yl") for w in own]
    other = [flipped(w, "core") for w in own]

    n_rows = n_z * CAP
    pick, high, low = call(
        table_kernel,
        (shaped((n_rows, toks)), shaped((toks, n_rows)), shaped((toks, n_rows))),
        scalars=1,
    )(where, meta)
    rows = call(pack_kernel, shaped((n_rows, width)), flops=2 * n_rows * toks * width, moved=2 * n_rows * width)(
        pick, sent, trunk_gain
    )

    image = image_in[0]
    image_normed = rms_scale(image, image_gain[0]).astype(BF16)
    column = lax.all_gather(image_normed, "z", axis=0, tiled=True)
    all_rows = lax.all_gather(column, square, axis=0, tiled=True)

    def over_z(value):
        return lax.all_to_all(value.reshape(n_z, CAP, width), "z", split_axis=0, concat_axis=0, tiled=True).reshape(
            n_rows, width
        )

    arrived = over_z(rows)
    other_across = [flipped(w, "core") for w in across]
    made = call(
        expert_kernel,
        shaped((n_rows, width)),
        flops=6 * n_rows * width * 768,
        moved=12 * 192 * width * 2,
    )(arrived, *own, *across, *other, *other_across)
    returned = over_z(made)

    hidden = jax.nn.gelu(jnp.dot(all_rows, fc_in[0], preferred_element_type=F32), approximate=False).astype(BF16)
    part = jnp.dot(hidden, fc_out[0], preferred_element_type=F32).astype(BF16)
    part = part.reshape(n_yh * n_tp, n_z, part.shape[1])
    column_sum = lax.psum_scatter(part, square, scatter_dimension=0, tiled=True)[0]
    spread = lax.all_to_all(column_sum.astype(F32)[:, None, :], "z", split_axis=0, concat_axis=0, tiled=True)
    summed = jnp.sum(spread, axis=0)
    encoded = (image.astype(F32) + layer_scale[0] * summed).astype(BF16)
    image_out = lax.ppermute(encoded[None], "pp", [(s, (s - 1) % n_pp) for s in range(n_pp)])

    quarter = width // n_tp
    pieces = call(combine_kernel, tuple(shaped((toks, quarter)) for _ in range(n_tp)), scalars=1, flops=4 * n_rows * toks * width)(
        where, high, low, returned
    )
    pieces = [
        lax.ppermute(
            piece,
            square,
            [(a * n_tp + b, b * n_tp + (a + k) % n_tp) for a in range(n_yh) for b in range(n_tp)],
        )
        for k, piece in enumerate(pieces)
    ]
    layer = call(layer_kernel, shaped((toks, quarter)), scalars=1)(where, tokens, *pieces)
    here = lax.ppermute(layer, "pp", [(s, (s + 1) % n_pp) for s in range(n_pp)])
    there = lax.ppermute(
        layer, ("pp", "yl"), [(s * 2 + y, ((s + 1) % n_pp) * 2 + 1 - y) for s in range(n_pp) for y in range(2)]
    )
    here_other, there_other = flipped(here, "core"), flipped(there, "core")
    trunk_out = call(join_kernel, shaped((toks, width)), scalars=1)(where, here, there, here_other, there_other)
    return (trunk_out[None], image_out)


def solution(mesh):
    n_pp, n_ep, n_tp = (mesh.shape[a] for a in ("pp", "ep", "tp"))
    fine = Mesh(
        np.asarray(mesh.devices).reshape(n_pp, n_tp, n_ep // n_tp, n_tp // 2, 2),
        ("pp", "yh", "z", "yl", "core"),
    )
    ep, tp = ("yh", "z"), ("yl", "core")
    return jax.shard_map(
        body,
        mesh=fine,
        in_specs=(
            P("pp", ep, None),
            P("pp", ep, None),
            P("pp", ep, None),
            P("pp", None),
            P("pp", ep, None, tp),
            P("pp", ep, None, tp),
            P("pp", ep, tp, None),
            P("pp", ep + tp, None),
            P("pp", None),
            P("pp", None, ep + tp),
            P("pp", ep + tp, None),
            P("pp", None),
        ),
        out_specs=(P("pp", ep, None), P("pp", ep + tp, None)),
        check_vma=False,
    )
```

```python
import functools

import jax
import jax.numpy as jnp
import numpy as np
from jax import lax
from jax.experimental import pallas as pl
from jax.experimental.pallas import tpu as pltpu
from jax.sharding import Mesh, PartitionSpec as P

BF16 = jnp.bfloat16
F32 = jnp.float32
VM = pl.BlockSpec(memory_space=pltpu.VMEM)
SM = pl.BlockSpec(memory_space=pltpu.SMEM)
CAP = 40
LIMIT = 48 * 1024 * 1024


def call(kernel, outs, scalars=0, flops=0, moved=0):
    def run(*operands):
        specs = [SM] * scalars + [VM] * (len(operands) - scalars)
        return pl.pallas_call(
            kernel,
            out_shape=outs,
            in_specs=specs,
            out_specs=jax.tree.map(lambda _: VM, outs),
            compiler_params=pltpu.CompilerParams(vmem_limit_bytes=LIMIT),
            cost_estimate=pl.CostEstimate(flops=flops, bytes_accessed=moved, transcendentals=0),
        )(*operands)

    return run


def shaped(dims, kind=BF16):
    return jax.ShapeDtypeStruct(dims, kind)


def nt(a, b):
    return lax.dot_general(a, b, (((1,), (1,)), ((), ())), preferred_element_type=F32)


def table_kernel(where, meta, pick, high, low):
    rows, toks = pick.shape
    group = rows // CAP
    topk = meta.shape[0] // 2
    first = where[0] * group
    wanted = (lax.broadcasted_iota(jnp.int32, (group, toks), 0) + first).astype(F32)
    scores = meta[topk:, :]
    total = jnp.sum(scores, axis=0, keepdims=True)
    member = jnp.zeros((group, toks), F32)
    weight = jnp.zeros((group, toks), F32)
    for k in range(topk):
        same = meta[k : k + 1, :] == wanted
        member = jnp.where(same, 1.0, member)
        weight = jnp.where(same, meta[topk + k : topk + k + 1, :] / total, weight)
    earlier = lax.broadcasted_iota(jnp.int32, (toks, toks), 0) < lax.broadcasted_iota(jnp.int32, (toks, toks), 1)
    rank = jnp.dot(member.astype(BF16), earlier.astype(F32).astype(BF16), preferred_element_type=F32)
    rank = jnp.where(member > 0.5, rank, -1.0)
    slots = lax.broadcasted_iota(jnp.int32, (group, CAP, toks), 1).astype(F32)
    hit = jnp.where(rank[:, None, :] == slots, 1.0, 0.0)
    pick[...] = hit.reshape(rows, toks).astype(BF16)
    scaled = (hit * weight[:, None, :]).reshape(rows, toks).T
    top = scaled.astype(BF16)
    high[...] = top
    low[...] = (scaled - top.astype(F32)).astype(BF16)


def pack_kernel(pick, toks, gain, rows):
    wide = toks[...].astype(F32)
    scale = lax.rsqrt(jnp.mean(wide * wide, axis=-1, keepdims=True) + 1e-06)
    normed = (wide * scale * gain[...]).astype(BF16)
    rows[...] = jnp.dot(pick[...], normed, preferred_element_type=F32).astype(BF16)


def expert_kernel(rows, *refs):
    weights, out = refs[:-1], refs[-1]
    flat = rows[...]
    total = None
    for ref in weights:
        n = ref.shape[0] // 3
        gate = nt(flat, ref[:n, :])
        upval = nt(flat, ref[n : 2 * n, :])
        hidden = (gate * jax.nn.sigmoid(gate) * upval).astype(BF16)
        made = jnp.dot(hidden, ref[2 * n :, :], preferred_element_type=F32)
        total = made if total is None else total + made
    out[...] = total.astype(BF16)


def combine_kernel(where, toks, high, low, made, *pieces):
    n = len(pieces)
    cols = made.shape[1] // n
    for k in range(n):
        q = lax.rem(where[0] + k, n)
        block = pl.ds(pl.multiple_of(q * cols, cols), cols)
        part = made[:, block]
        summed = jnp.dot(high[...], part, preferred_element_type=F32)
        summed += jnp.dot(low[...], part, preferred_element_type=F32)
        if k == 0:
            summed += toks[:, block].astype(F32)
        pieces[k][...] = summed.astype(BF16)


def layer_kernel(*refs):
    pieces, out = refs[:-1], refs[-1]
    total = pieces[0][...].astype(F32)
    for piece in pieces[1:]:
        total += piece[...].astype(F32)
    out[...] = total.astype(BF16)


def join_kernel(where, own, across, other, both, out):
    cols = own.shape[1]
    t = where[1]
    yl, core = t // 2, lax.rem(t, 2)
    for ref, quarter in (
        (own, t),
        (across, (1 - yl) * 2 + core),
        (other, yl * 2 + 1 - core),
        (both, (1 - yl) * 2 + 1 - core),
    ):
        out[:, pl.ds(pl.multiple_of(quarter * cols, cols), cols)] = ref[...]


def image_kernel(n_z, where, rows, gain, first, second, mine, theirs):
    n, dv = rows.shape[0], gain.shape[1]
    wide = rows[:, :dv].astype(F32)
    scale = lax.rsqrt(jnp.mean(wide * wide, axis=-1, keepdims=True) + 1e-06)
    normed = (wide * scale * gain[...]).astype(BF16)
    made = nt(normed, first[...])
    hidden = (0.5 * made * (1.0 + lax.erf(made * np.float32(0.5**0.5)))).astype(BF16)
    core = lax.rem(where[1], 2)
    at = lax.broadcasted_iota(jnp.int32, (n // 2, n), 0)
    column = lax.broadcasted_iota(jnp.int32, (n // 2, n), 1)
    for out, side in ((mine, core), (theirs, 1 - core)):
        source = lax.rem(at, n_z) * (n // n_z) + at // n_z * 2 + side
        order = jnp.where(column == source, 1.0, 0.0).astype(BF16)
        half = jnp.dot(order, hidden, preferred_element_type=F32).astype(BF16)
        out[...] = jnp.dot(half, second[...], preferred_element_type=F32).astype(out.dtype)


def body(
    trunk_in,
    expert_ids,
    gate_scores,
    trunk_gain,
    w_gate,
    w_up,
    w_down,
    image_in,
    image_gain,
    fc_in,
    fc_out,
    layer_scale,
):
    n_pp, n_yh, n_z = (lax.axis_size(a) for a in ("pp", "yh", "z"))
    n_tp = lax.axis_size("yl") * lax.axis_size("core")
    n_square = n_yh * n_tp
    square = ("yh", "yl", "core")
    where = jnp.stack([lax.axis_index("yh"), lax.axis_index(("yl", "core"))]).astype(jnp.int32)

    def swapped(value):
        return lax.ppermute(value, square, [(a * n_tp + b, b * n_tp + a) for a in range(n_yh) for b in range(n_tp)])

    def flipped(value, axis):
        n = lax.axis_size(axis)
        return lax.ppermute(value, axis, [(i, n - 1 - i) for i in range(n)])

    def exchanged(value, axis):
        return lax.all_to_all(value, axis, split_axis=0, concat_axis=0, tiled=True)

    own = jnp.concatenate([w_gate[0, 0].T, w_up[0, 0].T, w_down[0, 0]], axis=0)
    across = flipped(own, "yl")
    other = flipped(own, "core")

    tokens = trunk_in[0]
    toks, width = tokens.shape
    sent = swapped(tokens)
    meta = swapped(jnp.concatenate([expert_ids[0].T.astype(F32), gate_scores[0].T], axis=0))

    image = image_in[0]
    dv = image.shape[1]
    image_wide, meta = lax.optimization_barrier((image.astype(F32), meta))
    ring = exchanged(jnp.broadcast_to(image_wide[None], (n_square, 1, dv)), square)
    ring, sent = lax.optimization_barrier((ring, sent))
    ring = jnp.pad(ring.reshape(n_square, dv).astype(BF16), ((0, 0), (0, -dv % 1024)))
    all_rows = lax.all_gather(ring, "z", axis=0, tiled=True)

    n_rows = n_z * CAP
    pick, high, low = call(
        table_kernel,
        (shaped((n_rows, toks)), shaped((toks, n_rows)), shaped((toks, n_rows))),
        scalars=1,
    )(where, meta)
    rows = call(pack_kernel, shaped((n_rows, width)), flops=2 * n_rows * toks * width, moved=2 * n_rows * width)(
        pick, sent, trunk_gain
    )
    arrived = exchanged(rows.reshape(n_z, CAP, width), "z").reshape(n_rows, width)
    n_image = n_z * n_square
    mine, theirs = call(
        functools.partial(image_kernel, n_z),
        (shaped((n_image // 2, dv), F32), shaped((n_image // 2, dv))),
        scalars=1,
        flops=4 * n_image * dv * 100,
        moved=4 * n_image * dv,
    )(where, all_rows, image_gain, fc_in[0].T, fc_out[0])
    across, arrived, theirs = lax.optimization_barrier((across, arrived, theirs))
    both = flipped(across, "core")
    chip = (mine + flipped(theirs, "core").astype(F32)).reshape(n_square // 2, n_z, dv)
    both, chip = lax.optimization_barrier((both, chip))
    column = lax.psum_scatter(chip, ("yh", "yl"), scatter_dimension=0, tiled=True)[0]
    made = call(
        expert_kernel,
        shaped((n_rows, width)),
        flops=6 * n_rows * width * 768,
        moved=12 * 192 * width * 2,
    )(arrived, own, other, across, both)
    returned = exchanged(made.reshape(n_z, CAP, width), "z").reshape(n_rows, width)

    quarter = width // n_tp
    pieces = call(combine_kernel, tuple(shaped((toks, quarter)) for _ in range(n_tp)), scalars=1, flops=4 * n_rows * toks * width)(
        where, sent, high, low, returned
    )
    pieces = [
        lax.ppermute(
            piece,
            ("pp",) + square,
            [
                (s * n_square + a * n_tp + b, (s + 1) % n_pp * n_square + b * n_tp + (a + k) % n_tp)
                for s in range(n_pp)
                for a in range(n_yh)
                for b in range(n_tp)
            ],
        )
        for k, piece in enumerate(pieces)
    ]
    column, pieces = lax.optimization_barrier((column, pieces))
    summed = jnp.sum(exchanged(column[:, None, :], "z"), axis=0)
    encoded = (image.astype(F32) + layer_scale[0] * summed).astype(BF16)
    image_out = lax.ppermute(encoded[None], "pp", [(s, (s - 1) % n_pp) for s in range(n_pp)])

    layer = call(layer_kernel, shaped((toks, quarter)))(*pieces)
    trunk_out = call(join_kernel, shaped((toks, width)), scalars=1)(
        where, layer, flipped(layer, "yl"), flipped(layer, "core"), flipped(layer, ("yl", "core"))
    )
    return (trunk_out[None], image_out)


def solution(mesh):
    n_pp, n_ep, n_tp = (mesh.shape[a] for a in ("pp", "ep", "tp"))
    fine = Mesh(
        np.asarray(mesh.devices).reshape(n_pp, n_tp, n_ep // n_tp, n_tp // 2, 2),
        ("pp", "yh", "z", "yl", "core"),
    )
    ep, tp = ("yh", "z"), ("yl", "core")
    return jax.shard_map(
        body,
        mesh=fine,
        in_specs=(
            P("pp", ep, None),
            P("pp", ep, None),
            P("pp", ep, None),
            P("pp", None),
            P("pp", ep, None, tp),
            P("pp", ep, None, tp),
            P("pp", ep, tp, None),
            P("pp", ep + tp, None),
            P("pp", None),
            P("pp", None, ep + tp),
            P("pp", ep + tp, None),
            P("pp", None),
        ),
        out_specs=(P("pp", ep, None), P("pp", ep + tp, None)),
        check_vma=False,
    )
```

```python
import functools

import jax
import jax.numpy as jnp
import numpy as np
from jax import lax
from jax.experimental import pallas as pl
from jax.experimental.pallas import tpu as pltpu
from jax.sharding import Mesh, PartitionSpec as P

BF16 = jnp.bfloat16
F32 = jnp.float32
VM = pl.BlockSpec(memory_space=pltpu.VMEM)
SM = pl.BlockSpec(memory_space=pltpu.SMEM)
CAP = 40
LIMIT = 48 * 1024 * 1024


def call(kernel, outs, scalars=0, flops=0, moved=0):
    def run(*operands):
        specs = [SM] * scalars + [VM] * (len(operands) - scalars)
        return pl.pallas_call(
            kernel,
            out_shape=outs,
            in_specs=specs,
            out_specs=jax.tree.map(lambda _: VM, outs),
            compiler_params=pltpu.CompilerParams(vmem_limit_bytes=LIMIT),
            cost_estimate=pl.CostEstimate(flops=flops, bytes_accessed=moved, transcendentals=0),
        )(*operands)

    return run


def shaped(dims, kind=BF16):
    return jax.ShapeDtypeStruct(dims, kind)


def nt(a, b):
    return lax.dot_general(a, b, (((1,), (1,)), ((), ())), preferred_element_type=F32)


def table_kernel(where, meta, pick, high, low):
    rows, toks = pick.shape
    group = rows // CAP
    topk = meta.shape[0] // 2
    first = where[0] * group
    wanted = (lax.broadcasted_iota(jnp.int32, (group, toks), 0) + first).astype(F32)
    scores = meta[topk:, :]
    total = jnp.sum(scores, axis=0, keepdims=True)
    member = jnp.zeros((group, toks), F32)
    weight = jnp.zeros((group, toks), F32)
    for k in range(topk):
        same = meta[k : k + 1, :] == wanted
        member = jnp.where(same, 1.0, member)
        weight = jnp.where(same, meta[topk + k : topk + k + 1, :] / total, weight)
    earlier = lax.broadcasted_iota(jnp.int32, (toks, toks), 0) < lax.broadcasted_iota(jnp.int32, (toks, toks), 1)
    rank = jnp.dot(member.astype(BF16), earlier.astype(F32).astype(BF16), preferred_element_type=F32)
    rank = jnp.where(member > 0.5, rank, -1.0)
    slots = lax.broadcasted_iota(jnp.int32, (group, CAP, toks), 1).astype(F32)
    hit = jnp.where(rank[:, None, :] == slots, 1.0, 0.0)
    pick[...] = hit.reshape(rows, toks).astype(BF16)
    scaled = (hit * weight[:, None, :]).reshape(rows, toks).T
    top = scaled.astype(BF16)
    high[...] = top
    low[...] = (scaled - top.astype(F32)).astype(BF16)


def pack_kernel(pick, toks, gain, rows):
    wide = toks[...].astype(F32)
    scale = lax.rsqrt(jnp.mean(wide * wide, axis=-1, keepdims=True) + 1e-06)
    normed = (wide * scale * gain[...]).astype(BF16)
    rows[...] = jnp.dot(pick[...], normed, preferred_element_type=F32).astype(BF16)


def expert_kernel(rows, *refs):
    shards, out = refs[:4], refs[4]
    rows_v, gate_v, up_v, down_v, hidden_v, out_v, row_sem, in_sem, out_sem = refs[5:]
    count = shards[0].shape[0] // 3
    row_copy = pltpu.make_async_copy(rows, rows_v, row_sem)
    row_copy.start()
    copies = []
    for s, shard in enumerate(shards):
        for p, held in enumerate((gate_v, up_v, down_v)):
            copies.append(
                pltpu.make_async_copy(
                    shard.at[pl.ds(p * count, count)], held.at[pl.ds(s * count, count)], in_sem.at[3 * s + p]
                )
            )
    for p in (0, 1, 2):
        for s in range(4):
            copies[3 * s + p].start() if p < 2 else None
    for s in range(4):
        copies[3 * s + 2].start()
    row_copy.wait()
    flat = rows_v[...]
    step = 256
    seen = 0
    for c in range(4 * count // step):
        while seen * count < (c + 1) * step:
            copies[3 * seen].wait()
            copies[3 * seen + 1].wait()
            seen += 1
        block = slice(c * step, (c + 1) * step)
        gate = nt(flat, gate_v[block, :])
        upval = nt(flat, up_v[block, :])
        hidden_v[:, block] = (gate * jax.nn.sigmoid(gate) * upval).astype(BF16)
    for s in range(4):
        copies[3 * s + 2].wait()
    cols = out_v.shape[1] // 4
    leaving = []
    for j in range(4):
        block = slice(j * cols, (j + 1) * cols)
        out_v[:, block] = jnp.dot(hidden_v[...], down_v[:, block], preferred_element_type=F32).astype(BF16)
        copy = pltpu.make_async_copy(
            out_v.at[:, pl.ds(j * cols, cols)], out.at[:, pl.ds(j * cols, cols)], out_sem.at[j]
        )
        copy.start()
        leaving.append(copy)
    for copy in leaving:
        copy.wait()


def experts(rows, shards):
    n, width = rows.shape
    count = shards[0].shape[0] // 3 * 4
    anywhere = pl.BlockSpec(memory_space=pl.ANY)
    return pl.pallas_call(
        expert_kernel,
        out_shape=shaped((n, width)),
        in_specs=[anywhere] * 5,
        out_specs=pl.BlockSpec(memory_space=pltpu.HBM),
        scratch_shapes=[
            pltpu.VMEM((n, width), BF16),
            pltpu.VMEM((count, width), BF16),
            pltpu.VMEM((count, width), BF16),
            pltpu.VMEM((count, width), BF16),
            pltpu.VMEM((n, count), BF16),
            pltpu.VMEM((n, width), BF16),
            pltpu.SemaphoreType.DMA,
            pltpu.SemaphoreType.DMA((12,)),
            pltpu.SemaphoreType.DMA((4,)),
        ],
        compiler_params=pltpu.CompilerParams(vmem_limit_bytes=LIMIT),
        cost_estimate=pl.CostEstimate(flops=6 * n * width * count, bytes_accessed=6 * count * width, transcendentals=0),
    )(rows, *shards)


def combine_kernel(where, toks, high, low, made, kept, given):
    half = made.shape[1] // 2
    a = where[0]
    for out, h in ((kept, a // 2), (given, 1 - a // 2)):
        block = pl.ds(pl.multiple_of(h * half, half), half)
        part = made[:, block]
        summed = jnp.dot(high[...], part, preferred_element_type=F32)
        summed += jnp.dot(low[...], part, preferred_element_type=F32)
        if out is kept:
            summed += jnp.where(lax.rem(a, 2) == 0, toks[:, block].astype(F32), 0.0)
        out[...] = summed.astype(BF16)


def add_kernel(left, right, out):
    out[...] = (left[...].astype(F32) + right[...].astype(F32)).astype(out.dtype)


def join_kernel(where, own, across, out):
    cols = own.shape[1]
    yl = where[1] // 2
    for ref, half in ((own, yl), (across, 1 - yl)):
        out[:, pl.ds(pl.multiple_of(half * cols, cols), cols)] = ref[...]


def spread_kernel(row, out):
    wide = row[...].astype(F32)
    for i in range(out.shape[0]):
        out[i] = wide


def ring_kernel(ring, out):
    out[...] = jnp.concatenate([ring[i] for i in range(ring.shape[0])], axis=0).astype(BF16)


def pair_kernel(own, other, out):
    n = own.shape[0]
    out[:n, :] = own[...]
    out[n:, :] = other[...]


def image_kernel(sizes, where, *refs):
    groups, (gain, first, second, mine, theirs) = refs[:-5], refs[-5:]
    n_yh, n_z = sizes
    wide = jnp.concatenate([group[...] for group in groups], axis=0).astype(F32)
    n = wide.shape[0]
    scale = lax.rsqrt(jnp.mean(wide * wide, axis=-1, keepdims=True) + 1e-06)
    normed = (wide * scale * gain[...]).astype(BF16)
    made = nt(normed, first[...])
    hidden = (0.5 * made * (1.0 + lax.erf(made * np.float32(0.5**0.5)))).astype(BF16)
    yh, yl, core, z_here = where[0], where[1] // 2, lax.rem(where[1], 2), where[2]
    at = lax.broadcasted_iota(jnp.int32, (n // 2, n), 0)
    column = lax.broadcasted_iota(jnp.int32, (n // 2, n), 1)
    z = lax.rem(at, n_z)
    high = lax.rem(at // n_z + yh, n_yh)
    low = lax.rem(at // (n_z * n_yh) + yl, 2)
    apart = lax.rem(z // 2 - z_here // 2 + n_z // 2, n_z // 2)
    group = jnp.where(apart == 0, 0, jnp.where(apart == 3, 1, apart + 1))
    block = group * 2 + lax.rem(z + z_here, 2)
    for out, side in ((mine, core), (theirs, 1 - core)):
        source = ((block * n_yh + high) * 2 + low) * 2 + side
        order = jnp.where(column == source, 1.0, 0.0).astype(BF16)
        half = jnp.dot(order, hidden, preferred_element_type=F32).astype(BF16)
        out[...] = jnp.dot(half, second[...], preferred_element_type=F32).astype(out.dtype)


def fold_kernel(held, came, keep, *sends):
    total = held[...] + came[...].astype(F32)
    n = keep.shape[0]
    keep[...] = total[:n]
    for i, send in enumerate(sends):
        send[...] = total[n + i * send.shape[0] : n + (i + 1) * send.shape[0]].astype(BF16)


def column_kernel(held, *refs):
    out = refs[-1]
    total = held[...]
    for came in refs[:-1]:
        total += came[...].astype(F32)
    for i in range(out.shape[0]):
        out[i] = total[i : i + 1]


def encoded_kernel(spread, image, scale, out):
    total = spread[0]
    for i in range(1, spread.shape[0]):
        total += spread[i]
    out[...] = (image[...].astype(F32) + scale[...] * total).astype(BF16)


def body(
    trunk_in,
    expert_ids,
    gate_scores,
    trunk_gain,
    w_gate,
    w_up,
    w_down,
    image_in,
    image_gain,
    fc_in,
    fc_out,
    layer_scale,
):
    n_pp, n_yh, n_z = (lax.axis_size(a) for a in ("pp", "yh", "z"))
    n_tp = lax.axis_size("yl") * lax.axis_size("core")
    n_square = n_yh * n_tp
    square = ("yh", "yl", "core")
    where = jnp.stack([lax.axis_index("yh"), lax.axis_index(("yl", "core")), lax.axis_index("z")]).astype(jnp.int32)

    def swapped(value):
        return lax.ppermute(value, square, [(a * n_tp + b, b * n_tp + a) for a in range(n_yh) for b in range(n_tp)])

    def shifted(value, axis, by):
        n = lax.axis_size(axis)
        return lax.ppermute(value, axis, [(i, (i + by) % n) for i in range(n)])

    def exchanged(value, axis):
        return lax.all_to_all(value, axis, split_axis=0, concat_axis=0, tiled=True)

    own = jnp.concatenate([w_gate[0, 0].T, w_up[0, 0].T, w_down[0, 0]], axis=0)
    across = shifted(own, "yl", 1)
    other = shifted(own, "core", 1)

    tokens = trunk_in[0]
    toks, width = tokens.shape
    sent = swapped(tokens)
    meta = swapped(jnp.concatenate([expert_ids[0].T.astype(F32), gate_scores[0].T], axis=0))

    image = image_in[0]
    dv = image.shape[1]
    ring = exchanged(call(spread_kernel, shaped((n_square, 1, dv), F32))(image), square)
    ring = call(ring_kernel, shaped((n_square, dv)))(ring)
    ring, sent = lax.optimization_barrier((ring, sent))
    ring_beside = lax.ppermute(ring, "z", [(i, i ^ 1) for i in range(n_z)])
    pair = call(pair_kernel, shaped((2 * n_square, dv)))(ring, ring_beside)
    below, above = shifted(pair, "z", 2), shifted(pair, "z", -2)
    far = shifted(below, "z", 2)

    n_rows = n_z * CAP
    pick, high, low = call(
        table_kernel,
        (shaped((n_rows, toks)), shaped((toks, n_rows)), shaped((toks, n_rows))),
        scalars=1,
    )(where, meta)
    rows = call(pack_kernel, shaped((n_rows, width)), flops=2 * n_rows * toks * width, moved=2 * n_rows * width)(
        pick, sent, trunk_gain
    )
    arrived = exchanged(rows.reshape(n_z, CAP, width), "z").reshape(n_rows, width)
    across, arrived, above, far = lax.optimization_barrier((across, arrived, above, far))
    both = shifted(across, "core", 1)
    made = experts(arrived, (own, other, across, both))
    returned = exchanged(made.reshape(n_z, CAP, width), "z").reshape(n_rows, width)

    n_image = n_z * n_square
    mine, theirs = call(
        functools.partial(image_kernel, (n_yh, n_z)),
        (shaped((n_image // 2, dv), F32), shaped((n_image // 2, dv))),
        scalars=1,
        flops=4 * n_image * dv * 100,
        moved=4 * n_image * dv,
    )(where, pair, below, above, far, image_gain, fc_in[0].T, fc_out[0])
    mine, theirs = call(fold_kernel, (shaped((n_image // 4, dv), F32), shaped((n_image // 4, dv))))(
        mine, shifted(theirs, "core", 1)
    )
    mine, *theirs = call(
        fold_kernel, (shaped((n_z, dv), F32),) + tuple(shaped((n_z, dv)) for _ in range(n_yh - 1))
    )(mine, shifted(theirs, "yl", 1))
    column = call(column_kernel, shaped((n_z, 1, dv), F32))(
        mine, *[shifted(part, "yh", k + 1) for k, part in enumerate(theirs)]
    )

    column, returned = lax.optimization_barrier((column, returned))
    half = width // 2
    pieces = call(combine_kernel, (shaped((toks, half)), shaped((toks, half))), scalars=1, flops=4 * n_rows * toks * width)(
        where, sent, high, low, returned
    )
    pieces = [
        lax.ppermute(
            piece,
            ("pp",) + square,
            [
                (s * n_square + a * n_tp + b, (s + 1) % n_pp * n_square + b * n_tp + (a ^ flip))
                for s in range(n_pp)
                for a in range(n_yh)
                for b in range(n_tp)
            ],
        )
        for flip, piece in zip((0, 2), pieces)
    ]
    spread, pieces = lax.optimization_barrier((exchanged(column, "z"), pieces))
    part = call(add_kernel, shaped((toks, half)))(*pieces)
    layer = call(add_kernel, shaped((toks, half)))(part, shifted(part, "core", 1))
    trunk_out = call(join_kernel, shaped((toks, width)), scalars=1)(where, layer, shifted(layer, "yl", 1))

    encoded = call(encoded_kernel, shaped((1, dv)))(spread, image, layer_scale)
    image_out = shifted(encoded[None], "pp", -1)
    return (trunk_out[None], image_out)


def solution(mesh):
    n_pp, n_ep, n_tp = (mesh.shape[a] for a in ("pp", "ep", "tp"))
    fine = Mesh(
        np.asarray(mesh.devices).reshape(n_pp, n_tp, n_ep // n_tp, n_tp // 2, 2),
        ("pp", "yh", "z", "yl", "core"),
    )
    ep, tp = ("yh", "z"), ("yl", "core")
    return jax.shard_map(
        body,
        mesh=fine,
        in_specs=(
            P("pp", ep, None),
            P("pp", ep, None),
            P("pp", ep, None),
            P("pp", None),
            P("pp", ep, None, tp),
            P("pp", ep, None, tp),
            P("pp", ep, tp, None),
            P("pp", ep + tp, None),
            P("pp", None),
            P("pp", None, ep + tp),
            P("pp", ep + tp, None),
            P("pp", None),
        ),
        out_specs=(P("pp", ep, None), P("pp", ep + tp, None)),
        check_vma=False,
    )
```

```python
import functools

import jax
import jax.numpy as jnp
import numpy as np
from jax import lax
from jax.experimental import pallas as pl
from jax.experimental.pallas import tpu as pltpu
from jax.sharding import Mesh, PartitionSpec as P

BF16 = jnp.bfloat16
F32 = jnp.float32
VM = pl.BlockSpec(memory_space=pltpu.VMEM)
SM = pl.BlockSpec(memory_space=pltpu.SMEM)
CAP = 40
SMALL = 12 * 1024 * 1024
LARGE = 24 * 1024 * 1024


def call(kernel, outs, scalars=0, flops=0, moved=0):
    def run(*operands):
        specs = [SM] * scalars + [VM] * (len(operands) - scalars)
        return pl.pallas_call(
            kernel,
            out_shape=outs,
            in_specs=specs,
            out_specs=jax.tree.map(lambda _: VM, outs),
            compiler_params=pltpu.CompilerParams(vmem_limit_bytes=SMALL),
            cost_estimate=pl.CostEstimate(flops=flops, bytes_accessed=moved, transcendentals=0),
        )(*operands)

    return run


def shaped(dims, kind=BF16):
    return jax.ShapeDtypeStruct(dims, kind)


def nt(a, b):
    return lax.dot_general(a, b, (((1,), (1,)), ((), ())), preferred_element_type=F32)


def table_kernel(where, meta, pick, high, low):
    rows, toks = pick.shape
    group = rows // CAP
    topk = meta.shape[0] // 2
    first = where[0] * group
    wanted = (lax.broadcasted_iota(jnp.int32, (group, toks), 0) + first).astype(F32)
    scores = meta[topk:, :]
    total = jnp.sum(scores, axis=0, keepdims=True)
    member = jnp.zeros((group, toks), F32)
    weight = jnp.zeros((group, toks), F32)
    for k in range(topk):
        same = meta[k : k + 1, :] == wanted
        member = jnp.where(same, 1.0, member)
        weight = jnp.where(same, meta[topk + k : topk + k + 1, :] / total, weight)
    earlier = lax.broadcasted_iota(jnp.int32, (toks, toks), 0) < lax.broadcasted_iota(jnp.int32, (toks, toks), 1)
    rank = jnp.dot(member.astype(BF16), earlier.astype(F32).astype(BF16), preferred_element_type=F32)
    rank = jnp.where(member > 0.5, rank, -1.0)
    slots = lax.broadcasted_iota(jnp.int32, (group, CAP, toks), 1).astype(F32)
    hit = jnp.where(rank[:, None, :] == slots, 1.0, 0.0)
    pick[...] = hit.reshape(rows, toks).astype(BF16)
    scaled = (hit * weight[:, None, :]).reshape(rows, toks).T
    top = scaled.astype(BF16)
    high[...] = top
    low[...] = (scaled - top.astype(F32)).astype(BF16)


def pack_kernel(pick, toks, gain, rows):
    wide = toks[...].astype(F32)
    scale = lax.rsqrt(jnp.mean(wide * wide, axis=-1, keepdims=True) + 1e-06)
    normed = (wide * scale * gain[...]).astype(BF16)
    rows[...] = jnp.dot(pick[...], normed, preferred_element_type=F32).astype(BF16)


def expert_kernel(rows, *refs):
    shards, out = refs[:4], refs[4]
    rows_v, gate_v, up_v, down_v, hidden_v, out_v, row_sem, in_sem, out_sem = refs[5:]
    count = shards[0].shape[0] // 3
    row_copy = pltpu.make_async_copy(rows, rows_v, row_sem)
    row_copy.start()
    copies = []
    for s, shard in enumerate(shards):
        for p, held in enumerate((gate_v, up_v, down_v)):
            copies.append(
                pltpu.make_async_copy(
                    shard.at[pl.ds(p * count, count)], held.at[pl.ds(s * count, count)], in_sem.at[3 * s + p]
                )
            )
    for s in range(4):
        copies[3 * s].start()
        copies[3 * s + 1].start()
    for s in range(4):
        copies[3 * s + 2].start()
    row_copy.wait()
    flat = rows_v[...]
    step = 256
    seen = 0
    for c in range(4 * count // step):
        while seen * count < (c + 1) * step:
            copies[3 * seen].wait()
            copies[3 * seen + 1].wait()
            seen += 1
        block = slice(c * step, (c + 1) * step)
        gate = nt(flat, gate_v[block, :])
        upval = nt(flat, up_v[block, :])
        hidden_v[:, block] = (gate * jax.nn.sigmoid(gate) * upval).astype(BF16)
    for s in range(4):
        copies[3 * s + 2].wait()
    cols = out_v.shape[1] // 4
    leaving = []
    for j in range(4):
        block = slice(j * cols, (j + 1) * cols)
        out_v[:, block] = jnp.dot(hidden_v[...], down_v[:, block], preferred_element_type=F32).astype(BF16)
        copy = pltpu.make_async_copy(
            out_v.at[:, pl.ds(j * cols, cols)], out.at[:, pl.ds(j * cols, cols)], out_sem.at[j]
        )
        copy.start()
        leaving.append(copy)
    for copy in leaving:
        copy.wait()


def experts(rows, shards):
    n, width = rows.shape
    count = shards[0].shape[0] // 3 * 4
    anywhere = pl.BlockSpec(memory_space=pl.ANY)
    return pl.pallas_call(
        expert_kernel,
        out_shape=pltpu.HBM((n, width), BF16),
        in_specs=[anywhere] * 5,
        out_specs=anywhere,
        scratch_shapes=[
            pltpu.VMEM((n, width), BF16),
            pltpu.VMEM((count, width), BF16),
            pltpu.VMEM((count, width), BF16),
            pltpu.VMEM((count, width), BF16),
            pltpu.VMEM((n, count), BF16),
            pltpu.VMEM((n, width), BF16),
            pltpu.SemaphoreType.DMA,
            pltpu.SemaphoreType.DMA((12,)),
            pltpu.SemaphoreType.DMA((4,)),
        ],
        compiler_params=pltpu.CompilerParams(vmem_limit_bytes=LARGE),
        cost_estimate=pl.CostEstimate(flops=6 * n * width * count, bytes_accessed=6 * count * width, transcendentals=0),
    )(rows, *shards)


def combine_kernel(where, toks, high, low, made, kept, given):
    half = made.shape[1] // 2
    a = where[0]
    for out, h in ((kept, a // 2), (given, 1 - a // 2)):
        block = pl.ds(pl.multiple_of(h * half, half), half)
        part = made[:, block]
        summed = jnp.dot(high[...], part, preferred_element_type=F32)
        summed += jnp.dot(low[...], part, preferred_element_type=F32)
        if out is kept:
            summed += jnp.where(lax.rem(a, 2) == 0, toks[:, block].astype(F32), 0.0)
        out[...] = summed.astype(BF16)


def add_kernel(left, right, out):
    out[...] = (left[...].astype(F32) + right[...].astype(F32)).astype(out.dtype)


def join_kernel(where, own, across, out):
    cols = own.shape[1]
    yl = where[1] // 2
    for ref, half in ((own, yl), (across, 1 - yl)):
        out[:, pl.ds(pl.multiple_of(half * cols, cols), cols)] = ref[...]


def spread_kernel(row, out):
    wide = row[...].astype(F32)
    for i in range(out.shape[0]):
        out[i] = wide


def rows_kernel(spread, out):
    out[...] = jnp.concatenate([spread[i] for i in range(spread.shape[0])], axis=0).astype(BF16)


def pair_kernel(own, other, out):
    out[...] = jnp.concatenate([own[...].astype(F32), other[...].astype(F32)], axis=0).astype(BF16)


def image_kernel(n_z, *refs):
    groups, (gain, first, second, mine, theirs) = refs[:-5], refs[-5:]
    wide = [group[...].astype(F32) for group in groups]
    n_yh = len(wide)
    blocks = []
    for core in range(2):
        for low in range(2):
            for ahead in range(n_yh):
                at = (low * 2 + core) * n_z
                blocks.append(wide[(n_yh - ahead) % n_yh][at : at + n_z, :])
    wide = jnp.concatenate(blocks, axis=0)
    scale = lax.rsqrt(jnp.mean(wide * wide, axis=-1, keepdims=True) + 1e-06)
    normed = (wide * scale * gain[...]).astype(BF16)
    made = nt(normed, first[...])
    hidden = (0.5 * made * (1.0 + lax.erf(made * np.float32(0.5**0.5)))).astype(BF16)
    whole = jnp.dot(hidden, second[...], preferred_element_type=F32)
    half = mine.shape[0]
    mine[...] = whole[:half]
    theirs[...] = whole[half:].astype(BF16)


def fold_kernel(held, came, keep, *sends):
    total = held[...] + came[...].astype(F32)
    n = keep.shape[0]
    keep[...] = total[:n]
    for i, send in enumerate(sends):
        send[...] = total[n + i * send.shape[0] : n + (i + 1) * send.shape[0]].astype(BF16)


def column_kernel(held, *refs):
    out = refs[-1]
    total = held[...]
    for came in refs[:-1]:
        total += came[...].astype(F32)
    for i in range(out.shape[0]):
        out[i] = total[i : i + 1]


def encoded_kernel(spread, image, scale, out):
    total = spread[0]
    for i in range(1, spread.shape[0]):
        total += spread[i]
    out[...] = (image[...].astype(F32) + scale[...] * total).astype(BF16)


def body(
    trunk_in,
    expert_ids,
    gate_scores,
    trunk_gain,
    w_gate,
    w_up,
    w_down,
    image_in,
    image_gain,
    fc_in,
    fc_out,
    layer_scale,
):
    n_pp, n_yh, n_z = (lax.axis_size(a) for a in ("pp", "yh", "z"))
    n_tp = lax.axis_size("yl") * lax.axis_size("core")
    n_square = n_yh * n_tp
    square = ("yh", "yl", "core")
    where = jnp.stack([lax.axis_index("yh"), lax.axis_index(("yl", "core"))]).astype(jnp.int32)

    def swapped(value):
        return lax.ppermute(value, square, [(a * n_tp + b, b * n_tp + a) for a in range(n_yh) for b in range(n_tp)])

    def shifted(value, axis, by):
        n = lax.axis_size(axis)
        return lax.ppermute(value, axis, [(i, (i + by) % n) for i in range(n)])

    def exchanged(value, axis):
        return lax.all_to_all(value, axis, split_axis=0, concat_axis=0, tiled=True)

    own = jnp.concatenate([w_gate[0, 0].T, w_up[0, 0].T, w_down[0, 0]], axis=0)
    across = shifted(own, "yl", 1)
    other = shifted(own, "core", 1)

    tokens = trunk_in[0]
    toks, width = tokens.shape
    sent = swapped(tokens)
    meta = swapped(jnp.concatenate([expert_ids[0].T.astype(F32), gate_scores[0].T], axis=0))

    image = image_in[0]
    dv = image.shape[1]
    column = exchanged(call(spread_kernel, shaped((n_z, 1, dv), F32))(image), "z")
    column = call(rows_kernel, shaped((n_z, dv)))(column)
    column, sent = lax.optimization_barrier((column, sent))
    chip = call(pair_kernel, shaped((2 * n_z, dv)))(column, shifted(column, "core", 1))
    chips = call(pair_kernel, shaped((4 * n_z, dv)))(chip, shifted(chip, "yl", 1))

    n_rows = n_z * CAP
    pick, high, low = call(
        table_kernel,
        (shaped((n_rows, toks)), shaped((toks, n_rows)), shaped((toks, n_rows))),
        scalars=1,
    )(where, meta)
    rows = call(pack_kernel, pltpu.HBM((n_rows, width), BF16), flops=2 * n_rows * toks * width, moved=2 * n_rows * width)(
        pick, sent, trunk_gain
    )
    arrived = exchanged(rows.reshape(n_z, CAP, width), "z").reshape(n_rows, width)
    across, arrived, chips = lax.optimization_barrier((across, arrived, chips))
    both = shifted(across, "core", 1)
    others = [shifted(chips, "yh", k) for k in range(1, n_yh)]
    made = experts(arrived, (own, other, across, both))
    made, others = lax.optimization_barrier((made, others))
    returned = exchanged(made.reshape(n_z, CAP, width), "z").reshape(n_rows, width)

    n_image = n_z * n_square
    mine, theirs = call(
        functools.partial(image_kernel, n_z),
        (shaped((n_image // 2, dv), F32), shaped((n_image // 2, dv))),
        flops=4 * n_image * dv * 100,
        moved=4 * n_image * dv,
    )(chips, *others, image_gain, fc_in[0].T, fc_out[0])
    mine, theirs = call(fold_kernel, (shaped((n_image // 4, dv), F32), shaped((n_image // 4, dv))))(
        mine, shifted(theirs, "core", 1)
    )
    mine, *theirs = call(
        fold_kernel, (shaped((n_z, dv), F32),) + tuple(shaped((n_z, dv)) for _ in range(n_yh - 1))
    )(mine, shifted(theirs, "yl", 1))
    column = call(column_kernel, shaped((n_z, 1, dv), F32))(
        mine, *[shifted(part, "yh", k + 1) for k, part in enumerate(theirs)]
    )

    column, returned = lax.optimization_barrier((column, returned))
    half = width // 2
    pieces = call(combine_kernel, (shaped((toks, half)), shaped((toks, half))), scalars=1, flops=4 * n_rows * toks * width)(
        where, sent, high, low, returned
    )
    pieces = [
        lax.ppermute(
            piece,
            ("pp",) + square,
            [
                (s * n_square + a * n_tp + b, (s + 1) % n_pp * n_square + b * n_tp + (a ^ flip))
                for s in range(n_pp)
                for a in range(n_yh)
                for b in range(n_tp)
            ],
        )
        for flip, piece in zip((0, 2), pieces)
    ]
    spread, pieces = lax.optimization_barrier((exchanged(column, "z"), pieces))
    part = call(add_kernel, shaped((toks, half)))(*pieces)
    layer = call(add_kernel, shaped((toks, half)))(part, shifted(part, "core", 1))
    trunk_out = call(join_kernel, shaped((toks, width)), scalars=1)(where, layer, shifted(layer, "yl", 1))

    encoded = call(encoded_kernel, shaped((1, dv)))(spread, image, layer_scale)
    image_out = shifted(encoded[None], "pp", -1)
    return (trunk_out[None], image_out)


def solution(mesh):
    n_pp, n_ep, n_tp = (mesh.shape[a] for a in ("pp", "ep", "tp"))
    fine = Mesh(
        np.asarray(mesh.devices).reshape(n_pp, n_tp, n_ep // n_tp, n_tp // 2, 2),
        ("pp", "yh", "z", "yl", "core"),
    )
    ep, tp = ("yh", "z"), ("yl", "core")
    return jax.shard_map(
        body,
        mesh=fine,
        in_specs=(
            P("pp", ep, None),
            P("pp", ep, None),
            P("pp", ep, None),
            P("pp", None),
            P("pp", ep, None, tp),
            P("pp", ep, None, tp),
            P("pp", ep, tp, None),
            P("pp", ep + tp, None),
            P("pp", None),
            P("pp", None, ep + tp),
            P("pp", ep + tp, None),
            P("pp", None),
        ),
        out_specs=(P("pp", ep, None), P("pp", ep + tp, None)),
        check_vma=False,
    )
```

```python
import functools

import jax
import jax.numpy as jnp
import numpy as np
from jax import lax
from jax.experimental import pallas as pl
from jax.experimental.pallas import tpu as pltpu
from jax.sharding import Mesh, PartitionSpec as P

BF16 = jnp.bfloat16
F32 = jnp.float32
VM = pl.BlockSpec(memory_space=pltpu.VMEM)
SM = pl.BlockSpec(memory_space=pltpu.SMEM)
CAP = 40
SMALL = 12 * 1024 * 1024
LARGE = 24 * 1024 * 1024


def call(kernel, outs, scalars=0, flops=0, moved=0):
    def run(*operands):
        specs = [SM] * scalars + [VM] * (len(operands) - scalars)
        return pl.pallas_call(
            kernel,
            out_shape=outs,
            in_specs=specs,
            out_specs=jax.tree.map(lambda _: VM, outs),
            compiler_params=pltpu.CompilerParams(vmem_limit_bytes=SMALL),
            cost_estimate=pl.CostEstimate(flops=flops, bytes_accessed=moved, transcendentals=0),
        )(*operands)

    return run


def shaped(dims, kind=BF16):
    return jax.ShapeDtypeStruct(dims, kind)


def nt(a, b):
    return lax.dot_general(a, b, (((1,), (1,)), ((), ())), preferred_element_type=F32)


def send_kernel(ids, scores, toks, out):
    topk, count = ids.shape
    width = toks.shape[1]
    given = scores[...]
    weights = given / jnp.sum(given, axis=0, keepdims=True)
    top = weights.astype(BF16).astype(F32)
    parts = [ids[...].astype(F32), top, weights - top, jnp.zeros((out.shape[1] - width - 3 * topk, count), F32)]
    out[:, :width] = toks[...]
    out[:, width:] = jnp.concatenate(parts, axis=0).T.astype(BF16)


def table(group, first, meta, topk):
    meta = meta.astype(F32).T
    toks = meta.shape[1]
    wanted = (lax.broadcasted_iota(jnp.int32, (group, toks), 0) + first).astype(F32)
    member = jnp.zeros((group, toks), F32)
    weight = jnp.zeros((group, toks), F32)
    for k in range(topk):
        same = meta[k : k + 1, :] == wanted
        member = jnp.where(same, 1.0, member)
        weight = jnp.where(same, meta[topk + k : topk + k + 1, :] + meta[2 * topk + k : 2 * topk + k + 1, :], weight)
    earlier = lax.broadcasted_iota(jnp.int32, (toks, toks), 0) < lax.broadcasted_iota(jnp.int32, (toks, toks), 1)
    rank = jnp.dot(member.astype(BF16), earlier.astype(F32).astype(BF16), preferred_element_type=F32)
    rank = jnp.where(member > 0.5, rank, -1.0)
    slots = lax.broadcasted_iota(jnp.int32, (group, CAP, toks), 1).astype(F32)
    return jnp.where(rank[:, None, :] == slots, 1.0, 0.0), weight


def pack_kernel(topk, where, sent, gain, rows):
    n, width = rows.shape
    group = n // CAP
    hit, _ = table(group, where[0] * group, sent[:, width:], topk)
    wide = sent[:, :width].astype(F32)
    scale = lax.rsqrt(jnp.mean(wide * wide, axis=-1, keepdims=True) + 1e-06)
    normed = (wide * scale * gain[...]).astype(BF16)
    pick = hit.reshape(n, hit.shape[2]).astype(BF16)
    rows[...] = jnp.dot(pick, normed, preferred_element_type=F32).astype(BF16)


def weigh_kernel(topk, where, meta, high, low):
    toks, n = high.shape
    group = n // CAP
    hit, weight = table(group, where[0] * group, meta[...], topk)
    scaled = (hit * weight[:, None, :]).reshape(n, toks).T
    top = scaled.astype(BF16)
    high[...] = top
    low[...] = (scaled - top.astype(F32)).astype(BF16)


def hidden_kernel(rows, *refs):
    shards, out = refs[:4], refs[4]
    rows_v, gate_v, up_v, row_sem, in_sem = refs[5:]
    count = shards[0].shape[0] // 2
    row_copy = pltpu.make_async_copy(rows, rows_v, row_sem)
    row_copy.start()
    copies = []
    for s, shard in enumerate(shards):
        place = pl.ds(s * count, count)
        copies.append(pltpu.make_async_copy(shard.at[pl.ds(0, count)], gate_v.at[place], in_sem.at[2 * s]))
        copies.append(pltpu.make_async_copy(shard.at[pl.ds(count, count)], up_v.at[place], in_sem.at[2 * s + 1]))
    for copy in copies:
        copy.start()
    row_copy.wait()
    flat = rows_v[...]
    step = 256
    seen = 0
    for c in range(4 * count // step):
        while seen * count < (c + 1) * step:
            copies[2 * seen].wait()
            copies[2 * seen + 1].wait()
            seen += 1
        block = slice(c * step, (c + 1) * step)
        gate = nt(flat, gate_v[block, :])
        upval = nt(flat, up_v[block, :])
        out[:, block] = (gate * jax.nn.sigmoid(gate) * upval).astype(BF16)


def down_kernel(hidden, *refs):
    shards, out = refs[:4], refs[4]
    down_v, out_v, in_sem, out_sem = refs[5:]
    count = shards[0].shape[0]
    copies = [
        pltpu.make_async_copy(shard, down_v.at[pl.ds(s * count, count)], in_sem.at[s])
        for s, shard in enumerate(shards)
    ]
    for copy in copies:
        copy.start()
    for copy in copies:
        copy.wait()
    cols = out_v.shape[1] // 4
    leaving = []
    for j in range(4):
        block = slice(j * cols, (j + 1) * cols)
        out_v[:, block] = jnp.dot(hidden[...], down_v[:, block], preferred_element_type=F32).astype(BF16)
        copy = pltpu.make_async_copy(
            out_v.at[:, pl.ds(j * cols, cols)], out.at[:, pl.ds(j * cols, cols)], out_sem.at[j]
        )
        copy.start()
        leaving.append(copy)
    for copy in leaving:
        copy.wait()


ANYWHERE = pl.BlockSpec(memory_space=pl.ANY)


def hidden_units(rows, shards):
    n, width = rows.shape
    count = shards[0].shape[0] * 2
    return pl.pallas_call(
        hidden_kernel,
        out_shape=shaped((n, count)),
        in_specs=[ANYWHERE] * 5,
        out_specs=VM,
        scratch_shapes=[
            pltpu.VMEM((n, width), BF16),
            pltpu.VMEM((count, width), BF16),
            pltpu.VMEM((count, width), BF16),
            pltpu.SemaphoreType.DMA,
            pltpu.SemaphoreType.DMA((8,)),
        ],
        compiler_params=pltpu.CompilerParams(vmem_limit_bytes=LARGE),
        cost_estimate=pl.CostEstimate(flops=4 * n * width * count, bytes_accessed=4 * count * width, transcendentals=0),
    )(rows, *shards)


def expert_rows(hidden, shards):
    n, count = hidden.shape
    width = shards[0].shape[1]
    return pl.pallas_call(
        down_kernel,
        out_shape=pltpu.HBM((n, width), BF16),
        in_specs=[VM] + [ANYWHERE] * 4,
        out_specs=ANYWHERE,
        scratch_shapes=[
            pltpu.VMEM((count, width), BF16),
            pltpu.VMEM((n, width), BF16),
            pltpu.SemaphoreType.DMA((4,)),
            pltpu.SemaphoreType.DMA((4,)),
        ],
        compiler_params=pltpu.CompilerParams(vmem_limit_bytes=SMALL),
        cost_estimate=pl.CostEstimate(flops=2 * n * width * count, bytes_accessed=2 * count * width, transcendentals=0),
    )(hidden, *shards)


def combine_kernel(where, toks, high, low, made, kept, given):
    half = made.shape[1] // 2
    a = where[0]
    for out, h in ((kept, a // 2), (given, 1 - a // 2)):
        block = pl.ds(pl.multiple_of(h * half, half), half)
        part = made[:, block]
        summed = jnp.dot(high[...], part, preferred_element_type=F32)
        summed += jnp.dot(low[...], part, preferred_element_type=F32)
        if out is kept:
            summed += jnp.where(lax.rem(a, 2) == 0, toks[:, block].astype(F32), 0.0)
        out[...] = summed.astype(BF16)


def add_kernel(left, right, out):
    out[...] = (left[...].astype(F32) + right[...].astype(F32)).astype(out.dtype)


def join_kernel(where, own, across, out):
    cols = own.shape[1]
    yl = where[1] // 2
    for ref, half in ((own, yl), (across, 1 - yl)):
        out[:, pl.ds(pl.multiple_of(half * cols, cols), cols)] = ref[...]


def spread_kernel(row, out):
    wide = row[...].astype(F32)
    for i in range(out.shape[0]):
        out[i] = wide


def rows_kernel(spread, out):
    out[...] = jnp.concatenate([spread[i] for i in range(spread.shape[0])], axis=0).astype(BF16)


def pair_kernel(own, other, out):
    both = jnp.concatenate([own[...].astype(F32), other[...].astype(F32)], axis=0).astype(BF16)
    dv = both.shape[1]
    out[:, :dv] = both
    if out.shape[1] > dv:
        out[:, dv:] = jnp.zeros((out.shape[0], out.shape[1] - dv), BF16)


def image_kernel(n_yh, rows, gain, first, second, mine, theirs):
    wide = rows[:, : gain.shape[1]].astype(F32)
    n_z = wide.shape[0] // (4 * n_yh)
    blocks = []
    for core in range(2):
        for low in range(2):
            for high in range(n_yh):
                at = ((high * 2 + low) * 2 + core) * n_z
                blocks.append(wide[at : at + n_z, :])
    wide = jnp.concatenate(blocks, axis=0)
    scale = lax.rsqrt(jnp.mean(wide * wide, axis=-1, keepdims=True) + 1e-06)
    normed = (wide * scale * gain[...]).astype(BF16)
    made = nt(normed, first[...])
    hidden = (0.5 * made * (1.0 + lax.erf(made * np.float32(0.5**0.5)))).astype(BF16)
    whole = jnp.dot(hidden, second[...], preferred_element_type=F32)
    half = mine.shape[0]
    mine[...] = whole[:half]
    theirs[...] = whole[half:].astype(BF16)


def fold_kernel(held, came, keep, *sends):
    total = held[...] + came[...].astype(F32)
    n = keep.shape[0]
    keep[...] = total[:n]
    for send in sends:
        send[...] = total[n:].astype(BF16)


def column_kernel(held, out):
    total = held[...]
    for i in range(out.shape[0]):
        out[i] = total[i : i + 1]


def encoded_kernel(spread, image, scale, out):
    total = spread[0]
    for i in range(1, spread.shape[0]):
        total += spread[i]
    out[...] = (image[...].astype(F32) + scale[...] * total).astype(BF16)


def body(
    trunk_in,
    expert_ids,
    gate_scores,
    trunk_gain,
    w_gate,
    w_up,
    w_down,
    image_in,
    image_gain,
    fc_in,
    fc_out,
    layer_scale,
):
    n_pp, n_yh, n_z = (lax.axis_size(a) for a in ("pp", "yh", "z"))
    n_tp = lax.axis_size("yl") * lax.axis_size("core")
    n_square = n_yh * n_tp
    square = ("yh", "yl", "core")
    where = jnp.stack([lax.axis_index("yh"), lax.axis_index(("yl", "core"))]).astype(jnp.int32)

    def swapped(value):
        return lax.ppermute(value, square, [(a * n_tp + b, b * n_tp + a) for a in range(n_yh) for b in range(n_tp)])

    def shifted(value, axis, by):
        n = lax.axis_size(axis)
        return lax.ppermute(value, axis, [(i, (i + by) % n) for i in range(n)])

    def exchanged(value, axis):
        return lax.all_to_all(value, axis, split_axis=0, concat_axis=0, tiled=True)

    tokens = trunk_in[0]
    toks, width = tokens.shape
    topk = expert_ids.shape[2]
    packed = call(send_kernel, shaped((toks, width + 128)))(expert_ids[0].T, gate_scores[0].T, tokens)

    own = jnp.concatenate([w_gate[0, 0].T, w_up[0, 0].T], axis=0)
    sent = swapped(packed)
    own, sent = lax.optimization_barrier((own, sent))
    across = shifted(own, "yl", 1)
    own_down = w_down[0, 0]
    across_down = shifted(own_down, "yl", 1)
    other = shifted(own, "core", 1)
    other_down = shifted(own_down, "core", 1)
    both = shifted(across, "core", 1)

    image = image_in[0]
    dv = image.shape[1]
    column = exchanged(call(spread_kernel, shaped((n_z, 1, dv), F32))(image), "z")
    column = call(rows_kernel, shaped((n_z, dv)))(column)
    column, sent = lax.optimization_barrier((column, sent))

    n_rows = n_z * CAP
    rows = call(functools.partial(pack_kernel, topk), pltpu.HBM((n_rows, width), BF16), scalars=1)(
        where, sent, trunk_gain
    )
    arrived = exchanged(rows.reshape(n_z, CAP, width), "z").reshape(n_rows, width)

    chip = call(pair_kernel, shaped((2 * n_z, dv)))(column, shifted(column, "core", 1))
    arrived, chip = lax.optimization_barrier((arrived, chip))

    hidden = hidden_units(arrived, (own, other, across, both))
    hidden, across_down = lax.optimization_barrier((hidden, across_down))
    both_down = shifted(across_down, "core", 1)
    chips = call(pair_kernel, shaped((4 * n_z, dv + -dv % 1024)))(chip, shifted(chip, "yl", 1))
    all_rows = lax.all_gather(chips, "yh", axis=0, tiled=True)
    made = expert_rows(hidden, (own_down, other_down, across_down, both_down))
    made, chips, meta = lax.optimization_barrier((made, chips, sent[:, width:]))
    returned = exchanged(made.reshape(n_z, CAP, width), "z").reshape(n_rows, width)
    high, low = call(functools.partial(weigh_kernel, topk), (shaped((toks, n_rows)), shaped((toks, n_rows))), scalars=1)(
        where, meta
    )

    n_image = n_z * n_square
    mine, theirs = call(
        functools.partial(image_kernel, n_yh),
        (shaped((n_image // 2, dv), F32), shaped((n_image // 2, dv))),
        flops=4 * n_image * dv * 100,
        moved=4 * n_image * dv,
    )(all_rows, image_gain, fc_in[0].T, fc_out[0])
    mine, theirs = call(fold_kernel, (shaped((n_image // 4, dv), F32), shaped((n_image // 4, dv))))(
        mine, shifted(theirs, "core", 1)
    )
    mine = call(fold_kernel, shaped((n_image // 4, dv), F32))(mine, shifted(theirs, "yl", 1))
    column = lax.psum_scatter(mine.reshape(n_yh, n_z, dv), "yh", scatter_dimension=0, tiled=True)[0]
    column = call(column_kernel, shaped((n_z, 1, dv), F32))(column)

    half = width // 2
    pieces = call(combine_kernel, (shaped((toks, half)), shaped((toks, half))), scalars=1, flops=4 * n_rows * toks * width)(
        where, sent, high, low, returned
    )
    pieces = [
        lax.ppermute(
            piece,
            ("pp",) + square,
            [
                (s * n_square + a * n_tp + b, (s + 1) % n_pp * n_square + b * n_tp + (a ^ flip))
                for s in range(n_pp)
                for a in range(n_yh)
                for b in range(n_tp)
            ],
        )
        for flip, piece in zip((0, 2), pieces)
    ]
    spread, pieces = lax.optimization_barrier((exchanged(column, "z"), pieces))
    part = call(add_kernel, shaped((toks, half)))(*pieces)
    layer = call(add_kernel, shaped((toks, half)))(part, shifted(part, "core", 1))
    trunk_out = call(join_kernel, shaped((toks, width)), scalars=1)(where, layer, shifted(layer, "yl", 1))

    encoded = call(encoded_kernel, shaped((1, dv)))(spread, image, layer_scale)
    image_out = shifted(encoded[None], "pp", -1)
    return (trunk_out[None], image_out)


def solution(mesh):
    n_pp, n_ep, n_tp = (mesh.shape[a] for a in ("pp", "ep", "tp"))
    fine = Mesh(
        np.asarray(mesh.devices).reshape(n_pp, n_tp, n_ep // n_tp, n_tp // 2, 2),
        ("pp", "yh", "z", "yl", "core"),
    )
    ep, tp = ("yh", "z"), ("yl", "core")
    return jax.shard_map(
        body,
        mesh=fine,
        in_specs=(
            P("pp", ep, None),
            P("pp", ep, None),
            P("pp", ep, None),
            P("pp", None),
            P("pp", ep, None, tp),
            P("pp", ep, None, tp),
            P("pp", ep, tp, None),
            P("pp", ep + tp, None),
            P("pp", None),
            P("pp", None, ep + tp),
            P("pp", ep + tp, None),
            P("pp", None),
        ),
        out_specs=(P("pp", ep, None), P("pp", ep + tp, None)),
        check_vma=False,
    )
```

```python
import functools

import jax
import jax.numpy as jnp
import numpy as np
from jax import lax
from jax.experimental import pallas as pl
from jax.experimental.pallas import tpu as pltpu
from jax.sharding import Mesh, PartitionSpec as P

BF16 = jnp.bfloat16
F32 = jnp.float32
VM = pl.BlockSpec(memory_space=pltpu.VMEM)
SM = pl.BlockSpec(memory_space=pltpu.SMEM)
CAP = 40
ROWS = 48
SMALL = 12 * 1024 * 1024
LARGE = 24 * 1024 * 1024


def call(kernel, outs, scalars=0, flops=0, moved=0):
    def run(*operands):
        specs = [SM] * scalars + [VM] * (len(operands) - scalars)
        return pl.pallas_call(
            kernel,
            out_shape=outs,
            in_specs=specs,
            out_specs=jax.tree.map(lambda _: VM, outs),
            compiler_params=pltpu.CompilerParams(vmem_limit_bytes=SMALL),
            cost_estimate=pl.CostEstimate(flops=flops, bytes_accessed=moved, transcendentals=0),
        )(*operands)

    return run


def shaped(dims, kind=BF16):
    return jax.ShapeDtypeStruct(dims, kind)


def nt(a, b):
    return lax.dot_general(a, b, (((1,), (1,)), ((), ())), preferred_element_type=F32)


def table(group, slots, first, meta):
    toks = meta.shape[1]
    topk = meta.shape[0] // 2
    wanted = (lax.broadcasted_iota(jnp.int32, (group, toks), 0) + first).astype(F32)
    scores = meta[topk:, :]
    total = jnp.sum(scores, axis=0, keepdims=True)
    member = jnp.zeros((group, toks), F32)
    weight = jnp.zeros((group, toks), F32)
    for k in range(topk):
        same = meta[k : k + 1, :] == wanted
        member = jnp.where(same, 1.0, member)
        weight = jnp.where(same, meta[topk + k : topk + k + 1, :] / total, weight)
    earlier = lax.broadcasted_iota(jnp.int32, (toks, toks), 0) < lax.broadcasted_iota(jnp.int32, (toks, toks), 1)
    rank = jnp.dot(member.astype(BF16), earlier.astype(F32).astype(BF16), preferred_element_type=F32)
    rank = jnp.where(member > 0.5, rank, -1.0)
    slot = lax.broadcasted_iota(jnp.int32, (group, slots, toks), 1).astype(F32)
    return jnp.where(rank[:, None, :] == slot, 1.0, 0.0), weight


def pack_kernel(where, meta, toks, gain, image, rows):
    n, width = rows.shape
    group = n // ROWS
    hit, _ = table(group, ROWS, where[0] * group, meta[...])
    wide = toks[...].astype(F32)
    scale = lax.rsqrt(jnp.mean(wide * wide, axis=-1, keepdims=True) + 1e-06)
    normed = (wide * scale * gain[...]).astype(BF16)
    dv = image.shape[1]
    picture = image[...].astype(F32)
    spare = jnp.zeros((1, 2 * width - dv), F32)
    picture = jnp.concatenate([picture[:, :width], jnp.concatenate([picture[:, width:], spare], axis=1)], axis=0)
    picture = jnp.concatenate([picture, jnp.zeros((ROWS - CAP - 2, width), F32)], axis=0)
    empty = jnp.zeros((CAP, width), F32)
    made = jnp.dot(hit.reshape(n, hit.shape[2]).astype(BF16), normed, preferred_element_type=F32)
    rows[...] = (made + jnp.concatenate([empty, picture] * group, axis=0)).astype(BF16)


def weigh_kernel(where, meta, high, low):
    toks, n = high.shape
    group = n // CAP
    hit, weight = table(group, CAP, where[0] * group, meta[...])
    scaled = (hit * weight[:, None, :]).reshape(n, toks).T
    top = scaled.astype(BF16)
    high[...] = top
    low[...] = (scaled - top.astype(F32)).astype(BF16)


def expert_kernel(rows, *refs):
    shards, out = refs[:4], refs[4]
    rows_v, gate_v, up_v, down_v, hidden_v, out_v, row_sem, in_sem, out_sem = refs[5:]
    count = shards[0].shape[0] // 3
    row_copy = pltpu.make_async_copy(rows, rows_v, row_sem)
    row_copy.start()
    copies = []
    for s, shard in enumerate(shards):
        for p, held in enumerate((gate_v, up_v, down_v)):
            copies.append(
                pltpu.make_async_copy(
                    shard.at[pl.ds(p * count, count)], held.at[pl.ds(s * count, count)], in_sem.at[3 * s + p]
                )
            )
    for s in range(4):
        copies[3 * s].start()
        copies[3 * s + 1].start()
    for s in range(4):
        copies[3 * s + 2].start()
    row_copy.wait()
    flat = rows_v[...]
    step = 256
    seen = 0
    for c in range(4 * count // step):
        while seen * count < (c + 1) * step:
            copies[3 * seen].wait()
            copies[3 * seen + 1].wait()
            seen += 1
        block = slice(c * step, (c + 1) * step)
        gate = nt(flat, gate_v[block, :]).reshape(-1, ROWS, step)[:, :CAP].reshape(-1, step)
        upval = nt(flat, up_v[block, :]).reshape(-1, ROWS, step)[:, :CAP].reshape(-1, step)
        hidden_v[:, block] = (gate * jax.nn.sigmoid(gate) * upval).astype(BF16)
    for s in range(4):
        copies[3 * s + 2].wait()
    cols = out_v.shape[1] // 4
    leaving = []
    for j in range(4):
        block = slice(j * cols, (j + 1) * cols)
        out_v[:, block] = jnp.dot(hidden_v[...], down_v[:, block], preferred_element_type=F32).astype(BF16)
        copy = pltpu.make_async_copy(
            out_v.at[:, pl.ds(j * cols, cols)], out.at[:, pl.ds(j * cols, cols)], out_sem.at[j]
        )
        copy.start()
        leaving.append(copy)
    for copy in leaving:
        copy.wait()


def experts(rows, shards):
    given, width = rows.shape
    n = given // ROWS * CAP
    count = shards[0].shape[0] // 3 * 4
    anywhere = pl.BlockSpec(memory_space=pl.ANY)
    return pl.pallas_call(
        expert_kernel,
        out_shape=pltpu.HBM((n, width), BF16),
        in_specs=[anywhere] * 5,
        out_specs=anywhere,
        scratch_shapes=[
            pltpu.VMEM((given, width), BF16),
            pltpu.VMEM((count, width), BF16),
            pltpu.VMEM((count, width), BF16),
            pltpu.VMEM((count, width), BF16),
            pltpu.VMEM((n, count), BF16),
            pltpu.VMEM((n, width), BF16),
            pltpu.SemaphoreType.DMA,
            pltpu.SemaphoreType.DMA((12,)),
            pltpu.SemaphoreType.DMA((4,)),
        ],
        compiler_params=pltpu.CompilerParams(vmem_limit_bytes=LARGE),
        cost_estimate=pl.CostEstimate(flops=6 * n * width * count, bytes_accessed=6 * count * width, transcendentals=0),
    )(rows, *shards)


def combine_kernel(where, toks, high, low, made, kept, given):
    half = made.shape[1] // 2
    a = where[0]
    for out, h in ((kept, a // 2), (given, 1 - a // 2)):
        block = pl.ds(pl.multiple_of(h * half, half), half)
        part = made[:, block]
        summed = jnp.dot(high[...], part, preferred_element_type=F32)
        summed += jnp.dot(low[...], part, preferred_element_type=F32)
        if out is kept:
            summed += jnp.where(lax.rem(a, 2) == 0, toks[:, block].astype(F32), 0.0)
        out[...] = summed.astype(BF16)


def add_kernel(left, right, out):
    out[...] = (left[...].astype(F32) + right[...].astype(F32)).astype(out.dtype)


def join_kernel(where, own, across, out):
    cols = own.shape[1]
    yl = where[1] // 2
    for ref, half in ((own, yl), (across, 1 - yl)):
        out[:, pl.ds(pl.multiple_of(half * cols, cols), cols)] = ref[...]


def image_kernel(sizes, where, own, other, gain, first, second, mine, theirs):
    n_yh, n_z = sizes
    wide = jnp.concatenate([own[...].astype(F32), other[...].astype(F32)], axis=0)
    n = wide.shape[0]
    scale = lax.rsqrt(jnp.mean(wide * wide, axis=-1, keepdims=True) + 1e-06)
    normed = (wide * scale * gain[...]).astype(BF16)
    made = nt(normed, first[...])
    hidden = (0.5 * made * (1.0 + lax.erf(made * np.float32(0.5**0.5)))).astype(BF16)
    yh, yl = where[0], where[1] // 2
    at = lax.broadcasted_iota(jnp.int32, (n, n), 0)
    z = lax.rem(at, n_z)
    high = lax.rem(at // n_z + yh, n_yh)
    low = lax.rem(at // (n_z * n_yh) + yl, 2)
    source = ((at // (2 * n_z * n_yh) * n_yh + high) * 2 + low) * n_z + z
    order = jnp.where(lax.broadcasted_iota(jnp.int32, (n, n), 1) == source, 1.0, 0.0).astype(BF16)
    turned = jnp.dot(order, hidden, preferred_element_type=F32).astype(BF16)
    whole = jnp.dot(turned, second[...], preferred_element_type=F32)
    mine[...] = whole[: n // 2]
    theirs[...] = whole[n // 2 :].astype(BF16)


def fold_kernel(held, came, keep, *sends):
    total = held[...] + came[...].astype(F32)
    n = keep.shape[0]
    keep[...] = total[:n]
    for i, send in enumerate(sends):
        send[...] = total[n + i * send.shape[0] : n + (i + 1) * send.shape[0]].astype(BF16)


def column_kernel(held, *refs):
    out = refs[-1]
    total = held[...]
    for came in refs[:-1]:
        total += came[...].astype(F32)
    for i in range(out.shape[0]):
        out[i] = total[i : i + 1]


def encoded_kernel(spread, image, scale, out):
    total = spread[0]
    for i in range(1, spread.shape[0]):
        total += spread[i]
    out[...] = (image[...].astype(F32) + scale[...] * total).astype(BF16)


def body(
    trunk_in,
    expert_ids,
    gate_scores,
    trunk_gain,
    w_gate,
    w_up,
    w_down,
    image_in,
    image_gain,
    fc_in,
    fc_out,
    layer_scale,
):
    n_pp, n_yh, n_z = (lax.axis_size(a) for a in ("pp", "yh", "z"))
    n_tp = lax.axis_size("yl") * lax.axis_size("core")
    n_square = n_yh * n_tp
    square = ("yh", "yl", "core")
    where = jnp.stack([lax.axis_index("yh"), lax.axis_index(("yl", "core"))]).astype(jnp.int32)

    def swapped(value):
        return lax.ppermute(value, square, [(a * n_tp + b, b * n_tp + a) for a in range(n_yh) for b in range(n_tp)])

    def shifted(value, axis, by):
        n = lax.axis_size(axis)
        return lax.ppermute(value, axis, [(i, (i + by) % n) for i in range(n)])

    def exchanged(value, axis):
        return lax.all_to_all(value, axis, split_axis=0, concat_axis=0, tiled=True)

    tokens = trunk_in[0]
    toks, width = tokens.shape
    sent = swapped(tokens)
    meta = swapped(jnp.concatenate([expert_ids[0].T.astype(F32), gate_scores[0].T], axis=0))
    own = jnp.concatenate([w_gate[0, 0].T, w_up[0, 0].T, w_down[0, 0]], axis=0)
    own, sent, meta = lax.optimization_barrier((own, sent, meta))
    across = shifted(own, "yl", 1)
    other = shifted(own, "core", 1)
    both = shifted(across, "core", 1)

    image = image_in[0]
    dv = image.shape[1]
    rows = call(pack_kernel, pltpu.HBM((n_z * ROWS, width), BF16), scalars=1)(where, meta, sent, trunk_gain, image)
    arrived = exchanged(rows.reshape(n_z, ROWS, width), "z")

    column = arrived[:, CAP : CAP + 2, :].reshape(n_z, 2 * width)[:, :dv]
    spread = jnp.broadcast_to(column[None], (n_yh * 2, n_z, dv))
    image_own = exchanged(spread, ("yh", "yl")).reshape(-1, dv)

    made = experts(arrived.reshape(-1, width), (own, other, across, both))
    made, meta = lax.optimization_barrier((made, meta))
    n_rows = n_z * CAP
    returned = exchanged(made.reshape(n_z, CAP, width), "z").reshape(n_rows, width)
    high, low = call(weigh_kernel, (shaped((toks, n_rows)), shaped((toks, n_rows))), scalars=1)(where, meta)

    n_image = n_z * n_square
    mine, theirs = call(
        functools.partial(image_kernel, (n_yh, n_z)),
        (shaped((n_image // 2, dv), F32), shaped((n_image // 2, dv))),
        scalars=1,
        flops=4 * n_image * dv * 100,
        moved=4 * n_image * dv,
    )(where, image_own, shifted(image_own, "core", 1), image_gain, fc_in[0].T, fc_out[0])
    mine, theirs = call(fold_kernel, (shaped((n_image // 4, dv), F32), shaped((n_image // 4, dv))))(
        mine, shifted(theirs, "core", 1)
    )
    mine, *theirs = call(
        fold_kernel, (shaped((n_z, dv), F32),) + tuple(shaped((n_z, dv)) for _ in range(n_yh - 1))
    )(mine, shifted(theirs, "yl", 1))
    column = call(column_kernel, shaped((n_z, 1, dv), F32))(
        mine, *[shifted(part, "yh", k + 1) for k, part in enumerate(theirs)]
    )

    column, returned = lax.optimization_barrier((column, returned))
    half = width // 2
    pieces = call(combine_kernel, (shaped((toks, half)), shaped((toks, half))), scalars=1, flops=4 * n_rows * toks * width)(
        where, sent, high, low, returned
    )
    pieces = [
        lax.ppermute(
            piece,
            ("pp",) + square,
            [
                (s * n_square + a * n_tp + b, (s + 1) % n_pp * n_square + b * n_tp + (a ^ flip))
                for s in range(n_pp)
                for a in range(n_yh)
                for b in range(n_tp)
            ],
        )
        for flip, piece in zip((0, 2), pieces)
    ]
    spread, pieces = lax.optimization_barrier((exchanged(column, "z"), pieces))
    part = call(add_kernel, shaped((toks, half)))(*pieces)
    layer = call(add_kernel, shaped((toks, half)))(part, shifted(part, "core", 1))
    trunk_out = call(join_kernel, shaped((toks, width)), scalars=1)(where, layer, shifted(layer, "yl", 1))

    encoded = call(encoded_kernel, shaped((1, dv)))(spread, image, layer_scale)
    image_out = shifted(encoded[None], "pp", -1)
    return (trunk_out[None], image_out)


def solution(mesh):
    n_pp, n_ep, n_tp = (mesh.shape[a] for a in ("pp", "ep", "tp"))
    fine = Mesh(
        np.asarray(mesh.devices).reshape(n_pp, n_tp, n_ep // n_tp, n_tp // 2, 2),
        ("pp", "yh", "z", "yl", "core"),
    )
    ep, tp = ("yh", "z"), ("yl", "core")
    return jax.shard_map(
        body,
        mesh=fine,
        in_specs=(
            P("pp", ep, None),
            P("pp", ep, None),
            P("pp", ep, None),
            P("pp", None),
            P("pp", ep, None, tp),
            P("pp", ep, None, tp),
            P("pp", ep, tp, None),
            P("pp", ep + tp, None),
            P("pp", None),
            P("pp", None, ep + tp),
            P("pp", ep + tp, None),
            P("pp", None),
        ),
        out_specs=(P("pp", ep, None), P("pp", ep + tp, None)),
        check_vma=False,
    )
```

```python
import functools

import jax
import jax.numpy as jnp
import numpy as np
from jax import lax
from jax.experimental import pallas as pl
from jax.experimental.pallas import tpu as pltpu
from jax.sharding import Mesh, PartitionSpec as P

BF16 = jnp.bfloat16
F32 = jnp.float32
VM = pl.BlockSpec(memory_space=pltpu.VMEM)
SM = pl.BlockSpec(memory_space=pltpu.SMEM)
CAP = 40
ROWS = 56


def served(n):
    table = {}
    for a in range(n):
        for t, c in enumerate((a - 1, a + 2 if a % 2 == 0 else a, a + 1, a if a % 2 == 0 else a + 2)):
            c %= n
            apart = (a - c) % n
            if apart % 2 == 1:
                copy = 2 if apart == 1 else 0
            else:
                copy = 3 if (apart == 2) == (c % 2 == 0) else 1
            table[a, t] = (c, copy)
    return table
SMALL = 12 * 1024 * 1024
LARGE = 24 * 1024 * 1024


def call(kernel, outs, scalars=0, flops=0, moved=0):
    def run(*operands):
        specs = [SM] * scalars + [VM] * (len(operands) - scalars)
        return pl.pallas_call(
            kernel,
            out_shape=outs,
            in_specs=specs,
            out_specs=jax.tree.map(lambda _: VM, outs),
            compiler_params=pltpu.CompilerParams(vmem_limit_bytes=SMALL),
            cost_estimate=pl.CostEstimate(flops=flops, bytes_accessed=moved, transcendentals=0),
        )(*operands)

    return run


def shaped(dims, kind=BF16):
    return jax.ShapeDtypeStruct(dims, kind)


def nt(a, b):
    return lax.dot_general(a, b, (((1,), (1,)), ((), ())), preferred_element_type=F32)


def table(group, slots, first, meta):
    toks = meta.shape[1]
    topk = meta.shape[0] // 2
    wanted = (lax.broadcasted_iota(jnp.int32, (group, toks), 0) + first).astype(F32)
    scores = meta[topk:, :]
    total = jnp.sum(scores, axis=0, keepdims=True)
    member = jnp.zeros((group, toks), F32)
    weight = jnp.zeros((group, toks), F32)
    for k in range(topk):
        same = meta[k : k + 1, :] == wanted
        member = jnp.where(same, 1.0, member)
        weight = jnp.where(same, meta[topk + k : topk + k + 1, :] / total, weight)
    earlier = lax.broadcasted_iota(jnp.int32, (toks, toks), 0) < lax.broadcasted_iota(jnp.int32, (toks, toks), 1)
    rank = jnp.dot(member.astype(BF16), earlier.astype(F32).astype(BF16), preferred_element_type=F32)
    rank = jnp.where(member > 0.5, rank, -1.0)
    slot = lax.broadcasted_iota(jnp.int32, (group, slots, toks), 1).astype(F32)
    return jnp.where(rank[:, None, :] == slot, 1.0, 0.0), weight


def pack_kernel(where, meta, toks, gain, ring, rows):
    n, width = rows.shape
    group = n // ROWS
    hit, _ = table(group, ROWS, where[0] * group, meta[...])
    wide = toks[...].astype(F32)
    scale = lax.rsqrt(jnp.mean(wide * wide, axis=-1, keepdims=True) + 1e-06)
    normed = (wide * scale * gain[...]).astype(BF16)
    images = jnp.concatenate([ring[i] for i in range(ring.shape[0])], axis=0)
    count, dv = images.shape
    spare = jnp.zeros((count, 2 * width - dv), F32)
    empty = jnp.zeros((CAP, width), F32)
    added = jnp.concatenate([empty, images[:, :width], jnp.concatenate([images[:, width:], spare], axis=1)], axis=0)
    made = jnp.dot(hit.reshape(n, hit.shape[2]).astype(BF16), normed, preferred_element_type=F32)
    rows[...] = (made + jnp.concatenate([added] * group, axis=0)).astype(BF16)


def weigh_kernel(where, meta, high, low):
    toks, n = high.shape
    group = n // CAP
    hit, weight = table(group, CAP, where[0] * group, meta[...])
    scaled = (hit * weight[:, None, :]).reshape(n, toks).T
    top = scaled.astype(BF16)
    high[...] = top
    low[...] = (scaled - top.astype(F32)).astype(BF16)


def expert_kernel(rows, *refs):
    shards, out = refs[:4], refs[4]
    rows_v, gate_v, up_v, down_v, hidden_v, out_v, row_sem, in_sem, out_sem = refs[5:]
    count = shards[0].shape[0] // 3
    row_copy = pltpu.make_async_copy(rows, rows_v, row_sem)
    row_copy.start()
    copies = []
    for s, shard in enumerate(shards):
        for p, held in enumerate((gate_v, up_v, down_v)):
            copies.append(
                pltpu.make_async_copy(
                    shard.at[pl.ds(p * count, count)], held.at[pl.ds(s * count, count)], in_sem.at[3 * s + p]
                )
            )
    for s in range(4):
        copies[3 * s].start()
        copies[3 * s + 1].start()
    for s in range(4):
        copies[3 * s + 2].start()
    row_copy.wait()
    flat = rows_v[...]
    step = 256
    seen = 0
    for c in range(4 * count // step):
        while seen * count < (c + 1) * step:
            copies[3 * seen].wait()
            copies[3 * seen + 1].wait()
            seen += 1
        block = slice(c * step, (c + 1) * step)
        gate = nt(flat, gate_v[block, :]).reshape(-1, ROWS, step)[:, :CAP].reshape(-1, step)
        upval = nt(flat, up_v[block, :]).reshape(-1, ROWS, step)[:, :CAP].reshape(-1, step)
        hidden_v[:, block] = (gate * jax.nn.sigmoid(gate) * upval).astype(BF16)
    for s in range(4):
        copies[3 * s + 2].wait()
    cols = out_v.shape[1] // 4
    leaving = []
    for j in range(4):
        block = slice(j * cols, (j + 1) * cols)
        out_v[:, block] = jnp.dot(hidden_v[...], down_v[:, block], preferred_element_type=F32).astype(BF16)
        copy = pltpu.make_async_copy(
            out_v.at[:, pl.ds(j * cols, cols)], out.at[:, pl.ds(j * cols, cols)], out_sem.at[j]
        )
        copy.start()
        leaving.append(copy)
    for copy in leaving:
        copy.wait()


def experts(rows, shards):
    given, width = rows.shape
    n = given // ROWS * CAP
    count = shards[0].shape[0] // 3 * 4
    anywhere = pl.BlockSpec(memory_space=pl.ANY)
    return pl.pallas_call(
        expert_kernel,
        out_shape=pltpu.HBM((n, width), BF16),
        in_specs=[anywhere] * 5,
        out_specs=anywhere,
        scratch_shapes=[
            pltpu.VMEM((given, width), BF16),
            pltpu.VMEM((count, width), BF16),
            pltpu.VMEM((count, width), BF16),
            pltpu.VMEM((count, width), BF16),
            pltpu.VMEM((n, count), BF16),
            pltpu.VMEM((n, width), BF16),
            pltpu.SemaphoreType.DMA,
            pltpu.SemaphoreType.DMA((12,)),
            pltpu.SemaphoreType.DMA((4,)),
        ],
        compiler_params=pltpu.CompilerParams(vmem_limit_bytes=LARGE),
        cost_estimate=pl.CostEstimate(flops=6 * n * width * count, bytes_accessed=6 * count * width, transcendentals=0),
    )(rows, *shards)


def combine_kernel(where, toks, high, low, made, kept, given):
    half = made.shape[1] // 2
    low_side, core = where[2] // 2, lax.rem(where[2], 2)
    for out, h in ((kept, low_side), (given, 1 - low_side)):
        block = pl.ds(pl.multiple_of(h * half, half), half)
        part = made[:, block]
        summed = jnp.dot(high[...], part, preferred_element_type=F32)
        summed += jnp.dot(low[...], part, preferred_element_type=F32)
        if out is kept:
            summed += jnp.where(core == 0, toks[:, block].astype(F32), 0.0)
        out[...] = summed.astype(BF16)


def add_kernel(left, right, out):
    out[...] = (left[...].astype(F32) + right[...].astype(F32)).astype(out.dtype)


def join_kernel(where, own, across, out):
    cols = own.shape[1]
    yl = where[1] // 2
    for ref, half in ((own, yl), (across, 1 - yl)):
        out[:, pl.ds(pl.multiple_of(half * cols, cols), cols)] = ref[...]


def spread_kernel(row, out):
    wide = row[...].astype(F32)
    for i in range(out.shape[0]):
        out[i] = wide


def image_kernel(sizes, where, rows, gain, weigh, first, first_other, second, second_other, mine, theirs):
    n_yh, n_z = sizes
    n = rows.shape[0]
    wide = rows[...].astype(F32)
    scale = lax.rsqrt(jnp.mean(wide * wide, axis=-1, keepdims=True) + 1e-06)
    normed = (wide * scale * gain[...]).astype(BF16)
    yh, yl = where[0], where[1] // 2
    at = lax.broadcasted_iota(jnp.int32, (n, n), 0)
    z = lax.rem(at, n_z)
    high = lax.rem(at // n_z + yh, n_yh)
    low = lax.rem(at // (n_z * n_yh) + yl, 2)
    source = (z * n_yh + high) * 2 + low
    order = jnp.where(lax.broadcasted_iota(jnp.int32, (n, n), 1) == source, 1.0, 0.0).astype(BF16)
    whole = None
    for w_in, w_out in ((first, second), (first_other, second_other)):
        made = nt(normed, w_in[...])
        hidden = (0.5 * made * (1.0 + lax.erf(made * np.float32(0.5**0.5)))).astype(BF16)
        turned = jnp.dot(order, hidden, preferred_element_type=F32).astype(BF16)
        part = jnp.dot(turned, w_out[...], preferred_element_type=F32)
        whole = part if whole is None else whole + part
    whole = whole * weigh[...]
    images = jnp.dot(order, rows[...], preferred_element_type=F32)
    mark = lax.broadcasted_iota(jnp.int32, (n, 1), 0) == where[3]
    whole = whole + jnp.where(mark, images, 0.0)
    mine[...] = whole[: n // 2]
    theirs[...] = whole[n // 2 :].astype(BF16)


def fold_kernel(held, came, keep, *sends):
    total = held[...] + came[...].astype(F32)
    n = keep.shape[0]
    keep[...] = total[:n]
    for i, send in enumerate(sends):
        send[...] = total[n + i * send.shape[0] : n + (i + 1) * send.shape[0]].astype(BF16)


def column_kernel(held, *refs):
    out = refs[-1]
    total = held[...]
    for came in refs[:-1]:
        total += came[...].astype(F32)
    for i in range(out.shape[0]):
        out[i] = total[i : i + 1]


def encoded_kernel(spread, out):
    total = spread[0]
    for i in range(1, spread.shape[0]):
        total += spread[i]
    out[...] = total.astype(BF16)


def body(
    trunk_in,
    expert_ids,
    gate_scores,
    trunk_gain,
    w_gate,
    w_up,
    w_down,
    image_in,
    image_gain,
    fc_in,
    fc_out,
    layer_scale,
):
    n_pp, n_yh, n_z = (lax.axis_size(a) for a in ("pp", "yh", "z"))
    n_tp = lax.axis_size("yl") * lax.axis_size("core")
    n_square = n_yh * n_tp
    square = ("yh", "yl", "core")
    serve = served(n_yh)
    copies = np.array([serve[a, t][1] for a in range(n_yh) for t in range(n_tp)], np.int32)
    yh, t = lax.axis_index("yh"), lax.axis_index(("yl", "core"))
    where = jnp.stack([yh, t, jnp.asarray(copies)[yh * n_tp + t], lax.axis_index("z")]).astype(jnp.int32)

    def fetched(value):
        pairs = [(c * n_tp + copy, a * n_tp + t) for (a, t), (c, copy) in serve.items()]
        return lax.ppermute(value, square, pairs)

    def shifted(value, axis, by):
        n = lax.axis_size(axis)
        return lax.ppermute(value, axis, [(i, (i + by) % n) for i in range(n)])

    def exchanged(value, axis):
        return lax.all_to_all(value, axis, split_axis=0, concat_axis=0, tiled=True)

    tokens = trunk_in[0]
    toks, width = tokens.shape
    sent = fetched(tokens)
    meta = fetched(jnp.concatenate([expert_ids[0].T.astype(F32), gate_scores[0].T], axis=0))
    own = jnp.concatenate([w_gate[0, 0].T, w_up[0, 0].T, w_down[0, 0]], axis=0)
    image = image_in[0]
    dv = image.shape[1]
    ring = exchanged(call(spread_kernel, shaped((n_yh * 2, 1, dv), F32))(image), ("yh", "yl"))
    own, sent, meta, ring = lax.optimization_barrier((own, sent, meta, ring))
    across = shifted(own, "yl", 1)
    other = shifted(own, "core", 1)
    first, second = fc_in[0].T, fc_out[0]
    first_other, second_other = shifted(first, "core", 1), shifted(second, "core", 1)
    across, first_other, second_other = lax.optimization_barrier((across, first_other, second_other))
    both = shifted(across, "core", 1)

    rows = call(pack_kernel, pltpu.HBM((n_z * ROWS, width), BF16), scalars=1)(where, meta, sent, trunk_gain, ring)
    arrived = exchanged(rows.reshape(n_z, ROWS, width), "z")

    made = experts(arrived.reshape(-1, width), (own, other, across, both))
    made, meta = lax.optimization_barrier((made, meta))
    n_rows = n_z * CAP
    returned = exchanged(made.reshape(n_z, CAP, width), "z").reshape(n_rows, width)
    high, low = call(weigh_kernel, (shaped((toks, n_rows)), shaped((toks, n_rows))), scalars=1)(where, meta)

    images = [arrived[:, CAP : CAP + 8, :], arrived[:, CAP + 8 : CAP + 16, : dv - width]]
    images = jnp.concatenate(images, axis=2).reshape(-1, dv)
    n_image = images.shape[0]
    mine, theirs = call(
        functools.partial(image_kernel, (n_yh, n_z)),
        (shaped((n_image // 2, dv), F32), shaped((n_image // 2, dv))),
        scalars=1,
        flops=8 * n_image * dv * 100,
        moved=8 * 100 * dv,
    )(where, images, image_gain, layer_scale, first, first_other, second, second_other)
    mine, *theirs = call(
        fold_kernel, (shaped((n_z, dv), F32),) + tuple(shaped((n_z, dv)) for _ in range(n_yh - 1))
    )(mine, shifted(theirs, "yl", 1))
    parts = [
        lax.ppermute(
            part,
            ("pp", "yh"),
            [(s * n_yh + h, (s - 1) % n_pp * n_yh + (h + k) % n_yh) for s in range(n_pp) for h in range(n_yh)],
        )
        for k, part in enumerate([mine, *theirs])
    ]
    column = call(column_kernel, shaped((n_z, 1, dv), F32))(*parts)

    column, returned = lax.optimization_barrier((column, returned))
    half = width // 2
    pieces = call(combine_kernel, (shaped((toks, half)), shaped((toks, half))), scalars=1, flops=4 * n_rows * toks * width)(
        where, sent, high, low, returned
    )
    pieces = [
        lax.ppermute(
            piece,
            ("pp",) + square,
            [
                (s * n_square + a * n_tp + t, (s + 1) % n_pp * n_square + c * n_tp + (copy ^ flip))
                for s in range(n_pp)
                for (a, t), (c, copy) in serve.items()
            ],
        )
        for flip, piece in zip((0, 2), pieces)
    ]
    spread, pieces = lax.optimization_barrier((exchanged(column, "z"), pieces))
    part = call(add_kernel, shaped((toks, half)))(*pieces)
    layer = call(add_kernel, shaped((toks, half)))(part, shifted(part, "core", 1))
    trunk_out = call(join_kernel, shaped((toks, width)), scalars=1)(where, layer, shifted(layer, "yl", 1))

    image_out = call(encoded_kernel, shaped((1, dv)))(spread)[None]
    return (trunk_out[None], image_out)


def solution(mesh):
    n_pp, n_ep, n_tp = (mesh.shape[a] for a in ("pp", "ep", "tp"))
    fine = Mesh(
        np.asarray(mesh.devices).reshape(n_pp, n_tp, n_ep // n_tp, n_tp // 2, 2),
        ("pp", "yh", "z", "yl", "core"),
    )
    ep, tp = ("yh", "z"), ("yl", "core")
    return jax.shard_map(
        body,
        mesh=fine,
        in_specs=(
            P("pp", ep, None),
            P("pp", ep, None),
            P("pp", ep, None),
            P("pp", None),
            P("pp", ep, None, tp),
            P("pp", ep, None, tp),
            P("pp", ep, tp, None),
            P("pp", ep + tp, None),
            P("pp", None),
            P("pp", None, ep + tp),
            P("pp", ep + tp, None),
            P("pp", None),
        ),
        out_specs=(P("pp", ep, None), P("pp", ep + tp, None)),
        check_vma=False,
    )
```

```python
import functools

import jax
import jax.numpy as jnp
import numpy as np
from jax import lax
from jax.experimental import pallas as pl
from jax.experimental.pallas import tpu as pltpu
from jax.sharding import Mesh, PartitionSpec as P

BF16 = jnp.bfloat16
F32 = jnp.float32
VM = pl.BlockSpec(memory_space=pltpu.VMEM)
SM = pl.BlockSpec(memory_space=pltpu.SMEM)
CAP = 40
ROWS = 56


def served(n):
    blocks = {}
    for a in range(n):
        for t, c in enumerate((a - 1, a + 2 if a % 2 == 0 else a, a + 1, a if a % 2 == 0 else a + 2)):
            blocks[a, t] = (c % n, t ^ 2)
    return blocks
SMALL = 12 * 1024 * 1024
LARGE = 24 * 1024 * 1024


def call(kernel, outs, scalars=0, flops=0, moved=0):
    def run(*operands):
        specs = [SM] * scalars + [VM] * (len(operands) - scalars)
        return pl.pallas_call(
            kernel,
            out_shape=outs,
            in_specs=specs,
            out_specs=jax.tree.map(lambda _: VM, outs),
            compiler_params=pltpu.CompilerParams(vmem_limit_bytes=SMALL),
            cost_estimate=pl.CostEstimate(flops=flops, bytes_accessed=moved, transcendentals=0),
        )(*operands)

    return run


def in_hbm(value):
    return pltpu.with_memory_space_constraint(value, pltpu.HBM)


def shaped(dims, kind=BF16):
    return jax.ShapeDtypeStruct(dims, kind)


def nt(a, b):
    return lax.dot_general(a, b, (((1,), (1,)), ((), ())), preferred_element_type=F32)


def table(group, slots, first, meta):
    toks = meta.shape[1]
    topk = meta.shape[0] // 2
    wanted = (lax.broadcasted_iota(jnp.int32, (group, toks), 0) + first).astype(F32)
    scores = meta[topk:, :]
    total = jnp.sum(scores, axis=0, keepdims=True)
    member = jnp.zeros((group, toks), F32)
    weight = jnp.zeros((group, toks), F32)
    for k in range(topk):
        same = meta[k : k + 1, :] == wanted
        member = jnp.where(same, 1.0, member)
        weight = jnp.where(same, meta[topk + k : topk + k + 1, :] / total, weight)
    earlier = lax.broadcasted_iota(jnp.int32, (toks, toks), 0) < lax.broadcasted_iota(jnp.int32, (toks, toks), 1)
    rank = jnp.dot(member.astype(BF16), earlier.astype(F32).astype(BF16), preferred_element_type=F32)
    rank = jnp.where(member > 0.5, rank, -100.0)
    slot = (lax.broadcasted_iota(jnp.int32, (group, slots, toks), 1) - (slots - CAP)).astype(F32)
    return jnp.where(rank[:, None, :] == slot, 1.0, 0.0), weight


def pack_kernel(where, meta, toks, gain, ring, rows):
    n, width = rows.shape
    group = n // ROWS
    hit, _ = table(group, ROWS, where[0] * group, meta[...])
    wide = toks[...].astype(F32)
    scale = lax.rsqrt(jnp.mean(wide * wide, axis=-1, keepdims=True) + 1e-06)
    normed = (wide * scale * gain[...]).astype(BF16)
    images = jnp.concatenate([ring[i] for i in range(ring.shape[0])], axis=0)
    count, dv = images.shape
    spare = jnp.zeros((count, 2 * width - dv), F32)
    empty = jnp.zeros((CAP, width), F32)
    added = jnp.concatenate([images[:, :width], jnp.concatenate([images[:, width:], spare], axis=1), empty], axis=0)
    made = jnp.dot(hit.reshape(n, hit.shape[2]).astype(BF16), normed, preferred_element_type=F32)
    rows[...] = (made + jnp.concatenate([added] * group, axis=0)).astype(BF16)


def weigh_kernel(where, meta, high, low):
    toks, n = high.shape
    group = n // CAP
    hit, weight = table(group, CAP, where[0] * group, meta[...])
    scaled = (hit * weight[:, None, :]).reshape(n, toks).T
    top = scaled.astype(BF16)
    high[...] = top
    low[...] = (scaled - top.astype(F32)).astype(BF16)


ANYWHERE = pl.BlockSpec(memory_space=pl.ANY)


def expert_kernel(rows, *refs):
    shards, out = refs[:4], refs[4]
    rows_v, gate_v, up_v, down_v, hidden_v, out_v, row_sem, in_sem, out_sem = refs[5:]
    count = shards[0].shape[0] // 3
    row_copy = pltpu.make_async_copy(rows, rows_v, row_sem)
    row_copy.start()
    copies = []
    for s, shard in enumerate(shards):
        for p, held in enumerate((gate_v, up_v, down_v)):
            copies.append(
                pltpu.make_async_copy(
                    shard.at[pl.ds(p * count, count)], held.at[pl.ds(s * count, count)], in_sem.at[3 * s + p]
                )
            )
    for s in range(4):
        copies[3 * s].start()
        copies[3 * s + 1].start()
    for s in range(4):
        copies[3 * s + 2].start()
    row_copy.wait()
    flat = rows_v[...]
    step = 256
    seen = 0
    for c in range(4 * count // step):
        while seen * count < (c + 1) * step:
            copies[3 * seen].wait()
            copies[3 * seen + 1].wait()
            seen += 1
        block = slice(c * step, (c + 1) * step)
        gate = nt(flat, gate_v[block, :]).reshape(-1, ROWS, step)[:, ROWS - CAP :].reshape(-1, step)
        upval = nt(flat, up_v[block, :]).reshape(-1, ROWS, step)[:, ROWS - CAP :].reshape(-1, step)
        hidden_v[:, block] = (gate * jax.nn.sigmoid(gate) * upval).astype(BF16)
    for s in range(4):
        copies[3 * s + 2].wait()
    cols = out_v.shape[1] // 4
    leaving = []
    for j in range(4):
        block = slice(j * cols, (j + 1) * cols)
        out_v[:, block] = jnp.dot(hidden_v[...], down_v[:, block], preferred_element_type=F32).astype(BF16)
        copy = pltpu.make_async_copy(
            out_v.at[:, pl.ds(j * cols, cols)], out.at[:, pl.ds(j * cols, cols)], out_sem.at[j]
        )
        copy.start()
        leaving.append(copy)
    for copy in leaving:
        copy.wait()


def experts(rows, shards):
    given, width = rows.shape
    n = given // ROWS * CAP
    count = shards[0].shape[0] // 3 * 4
    return pl.pallas_call(
        expert_kernel,
        out_shape=pltpu.HBM((n, width), BF16),
        in_specs=[ANYWHERE] * 5,
        out_specs=ANYWHERE,
        scratch_shapes=[
            pltpu.VMEM((given, width), BF16),
            pltpu.VMEM((count, width), BF16),
            pltpu.VMEM((count, width), BF16),
            pltpu.VMEM((count, width), BF16),
            pltpu.VMEM((n, count), BF16),
            pltpu.VMEM((n, width), BF16),
            pltpu.SemaphoreType.DMA,
            pltpu.SemaphoreType.DMA((12,)),
            pltpu.SemaphoreType.DMA((4,)),
        ],
        compiler_params=pltpu.CompilerParams(vmem_limit_bytes=LARGE),
        cost_estimate=pl.CostEstimate(flops=6 * n * width * count, bytes_accessed=6 * count * width, transcendentals=0),
    )(in_hbm(rows), *[in_hbm(shard) for shard in shards])


def combine_kernel(where, toks, high, low, made, kept, given):
    half = made.shape[1] // 2
    low_side, core = 1 - where[1] // 2, lax.rem(where[1], 2)
    for out, h in ((kept, low_side), (given, 1 - low_side)):
        block = pl.ds(pl.multiple_of(h * half, half), half)
        part = made[:, block]
        summed = jnp.dot(high[...], part, preferred_element_type=F32)
        summed += jnp.dot(low[...], part, preferred_element_type=F32)
        if out is kept:
            summed += jnp.where(core == 0, toks[:, block].astype(F32), 0.0)
        out[...] = summed.astype(BF16)


def add_kernel(left, right, out):
    out[...] = (left[...].astype(F32) + right[...].astype(F32)).astype(out.dtype)


def join_kernel(where, own, across, out):
    cols = own.shape[1]
    yl = where[1] // 2
    for ref, half in ((own, yl), (across, 1 - yl)):
        out[:, pl.ds(pl.multiple_of(half * cols, cols), cols)] = ref[...]


def spread_kernel(row, out):
    wide = row[...].astype(F32)
    for i in range(out.shape[0]):
        out[i] = wide


def image_kernel(sizes, where, arrived, gain, weigh, first, first_other, second, second_other, mine, theirs, *scratch):
    n_yh, n_z = sizes
    rows_v, first_v, first_other_v, second_v, second_other_v, sem = scratch
    count = 2 * n_yh
    copies = [
        pltpu.make_async_copy(arrived.at[i, pl.ds(0, 2 * count)], rows_v.at[i], sem.at[i]) for i in range(n_z)
    ]
    held = ((first, first_v), (first_other, first_other_v), (second, second_v), (second_other, second_other_v))
    for i, (source, target) in enumerate(held):
        copies.append(pltpu.make_async_copy(source, target, sem.at[n_z + i]))
    for copy in copies:
        copy.start()
    for copy in copies:
        copy.wait()
    dv = gain.shape[1]
    wide = rows_v[...].astype(F32)
    width = wide.shape[2]
    n = n_z * count
    wide = jnp.concatenate(
        [wide[:, :count].reshape(n, width), wide[:, count:, : dv - width].reshape(n, dv - width)], axis=1
    )
    rows = wide.astype(BF16)
    scale = lax.rsqrt(jnp.mean(wide * wide, axis=-1, keepdims=True) + 1e-06)
    normed = (wide * scale * gain[...]).astype(BF16)
    yh, yl = where[0], where[1] // 2
    at = lax.broadcasted_iota(jnp.int32, (n, n), 0)
    z = lax.rem(at, n_z)
    high = lax.rem(at // n_z + yh, n_yh)
    low = lax.rem(at // (n_z * n_yh) + yl, 2)
    source = (z * n_yh + high) * 2 + low
    order = jnp.where(lax.broadcasted_iota(jnp.int32, (n, n), 1) == source, 1.0, 0.0).astype(BF16)
    whole = None
    for w_in, w_out in ((first_v, second_v), (first_other_v, second_other_v)):
        made = nt(normed, w_in[...])
        hidden = (0.5 * made * (1.0 + lax.erf(made * np.float32(0.5**0.5)))).astype(BF16)
        turned = jnp.dot(order, hidden, preferred_element_type=F32).astype(BF16)
        part = jnp.dot(turned, w_out[...], preferred_element_type=F32)
        whole = part if whole is None else whole + part
    whole = whole * weigh[...]
    images = jnp.dot(order, rows, preferred_element_type=F32)
    mark = lax.broadcasted_iota(jnp.int32, (n, 1), 0) == where[2]
    whole = whole + jnp.where(mark, images, 0.0)
    mine[...] = whole[: n // 2]
    theirs[...] = whole[n // 2 :].astype(BF16)


def encoder_part(where, arrived, gain, weigh, weights, n_yh):
    n_z, _, width = arrived.shape
    hidden, dv = weights[0].shape
    half = n_z * n_yh
    return pl.pallas_call(
        functools.partial(image_kernel, (n_yh, n_z)),
        out_shape=(shaped((half, dv), F32), shaped((half, dv))),
        in_specs=[SM, ANYWHERE, VM, VM] + [ANYWHERE] * 4,
        out_specs=(VM, VM),
        scratch_shapes=[pltpu.VMEM((n_z, 4 * n_yh, width), BF16)]
        + [pltpu.VMEM((hidden, dv), BF16)] * 4
        + [pltpu.SemaphoreType.DMA((n_z + 4,))],
        compiler_params=pltpu.CompilerParams(vmem_limit_bytes=SMALL),
        cost_estimate=pl.CostEstimate(flops=16 * half * dv * hidden, bytes_accessed=8 * hidden * dv, transcendentals=0),
    )(where, in_hbm(arrived), gain, weigh, *[in_hbm(w) for w in weights])


def fold_kernel(held, came, keep, *sends):
    total = held[...] + came[...].astype(F32)
    n = keep.shape[0]
    keep[...] = total[:n]
    for i, send in enumerate(sends):
        send[...] = total[n + i * send.shape[0] : n + (i + 1) * send.shape[0]].astype(BF16)


def column_kernel(held, *refs):
    out = refs[-1]
    total = held[...]
    for came in refs[:-1]:
        total += came[...].astype(F32)
    for i in range(out.shape[0]):
        out[i] = total[i : i + 1]


def encoded_kernel(spread, out):
    total = spread[0]
    for i in range(1, spread.shape[0]):
        total += spread[i]
    out[...] = total.astype(BF16)


def body(
    trunk_in,
    expert_ids,
    gate_scores,
    trunk_gain,
    w_gate,
    w_up,
    w_down,
    image_in,
    image_gain,
    fc_in,
    fc_out,
    layer_scale,
):
    n_pp, n_yh, n_z = (lax.axis_size(a) for a in ("pp", "yh", "z"))
    n_tp = lax.axis_size("yl") * lax.axis_size("core")
    n_square = n_yh * n_tp
    square = ("yh", "yl", "core")
    serve = served(n_yh)
    where = jnp.stack([lax.axis_index("yh"), lax.axis_index(("yl", "core")), lax.axis_index("z")]).astype(jnp.int32)

    def fetched(value):
        pairs = [(c * n_tp + copy, a * n_tp + t) for (a, t), (c, copy) in serve.items()]
        return lax.ppermute(value, square, pairs)

    def shifted(value, axis, by):
        n = lax.axis_size(axis)
        return lax.ppermute(value, axis, [(i, (i + by) % n) for i in range(n)])

    def exchanged(value, axis):
        return lax.all_to_all(value, axis, split_axis=0, concat_axis=0, tiled=True)

    tokens = trunk_in[0]
    toks, width = tokens.shape
    sent = fetched(tokens)
    meta = fetched(jnp.concatenate([expert_ids[0].T.astype(F32), gate_scores[0].T], axis=0))
    own = jnp.concatenate([w_gate[0, 0].T, w_up[0, 0].T, w_down[0, 0]], axis=0)
    image = image_in[0]
    dv = image.shape[1]
    ring = exchanged(call(spread_kernel, shaped((n_yh * 2, 1, dv), F32))(image), ("yh", "yl"))
    own, sent, meta, ring, where = lax.optimization_barrier((own, sent, meta, ring, where))
    across = shifted(own, "yl", 1)
    other = shifted(own, "core", 1)
    first, second = fc_in[0].T, fc_out[0]
    first_other, second_other = shifted(first, "core", 1), shifted(second, "core", 1)
    across, first_other, second_other = lax.optimization_barrier((across, first_other, second_other))
    both = shifted(across, "core", 1)

    rows = call(pack_kernel, pltpu.HBM((n_z * ROWS, width), BF16), scalars=1)(where, meta, sent, trunk_gain, ring)
    arrived = exchanged(rows.reshape(n_z, ROWS, width), "z")

    made = experts(arrived.reshape(-1, width), (own, other, across, both))
    made, meta = lax.optimization_barrier((made, meta))
    n_rows = n_z * CAP
    returned = exchanged(made.reshape(n_z, CAP, width), "z").reshape(n_rows, width)
    high, low = call(weigh_kernel, (shaped((toks, n_rows)), shaped((toks, n_rows))), scalars=1)(where, meta)

    mine, theirs = encoder_part(where, arrived, image_gain, layer_scale, (first, first_other, second, second_other), n_yh)
    mine, *theirs = call(
        fold_kernel, (shaped((n_z, dv), F32),) + tuple(shaped((n_z, dv)) for _ in range(n_yh - 1))
    )(mine, shifted(theirs, "yl", 1))
    parts = [
        lax.ppermute(
            part,
            ("pp", "yh"),
            [(s * n_yh + h, (s - 1) % n_pp * n_yh + (h + k) % n_yh) for s in range(n_pp) for h in range(n_yh)],
        )
        for k, part in enumerate([mine, *theirs])
    ]
    column = call(column_kernel, shaped((n_z, 1, dv), F32))(*parts)

    column, returned = lax.optimization_barrier((column, returned))
    half = width // 2
    pieces = call(combine_kernel, (shaped((toks, half)), shaped((toks, half))), scalars=1, flops=4 * n_rows * toks * width)(
        where, sent, high, low, returned
    )
    pieces = [
        lax.ppermute(
            piece,
            ("pp",) + square,
            [
                (s * n_square + a * n_tp + t, (s + 1) % n_pp * n_square + c * n_tp + (copy ^ flip))
                for s in range(n_pp)
                for (a, t), (c, copy) in serve.items()
            ],
        )
        for flip, piece in zip((0, 2), pieces)
    ]
    spread, pieces = lax.optimization_barrier((exchanged(column, "z"), pieces))
    part = call(add_kernel, shaped((toks, half)))(*pieces)
    layer = call(add_kernel, shaped((toks, half)))(part, shifted(part, "core", 1))
    trunk_out = call(join_kernel, shaped((toks, width)), scalars=1)(where, layer, shifted(layer, "yl", 1))

    image_out = call(encoded_kernel, shaped((1, dv)))(spread)[None]
    return (trunk_out[None], image_out)


def solution(mesh):
    n_pp, n_ep, n_tp = (mesh.shape[a] for a in ("pp", "ep", "tp"))
    fine = Mesh(
        np.asarray(mesh.devices).reshape(n_pp, n_tp, n_ep // n_tp, n_tp // 2, 2),
        ("pp", "yh", "z", "yl", "core"),
    )
    ep, tp = ("yh", "z"), ("yl", "core")
    return jax.shard_map(
        body,
        mesh=fine,
        in_specs=(
            P("pp", ep, None),
            P("pp", ep, None),
            P("pp", ep, None),
            P("pp", None),
            P("pp", ep, None, tp),
            P("pp", ep, None, tp),
            P("pp", ep, tp, None),
            P("pp", ep + tp, None),
            P("pp", None),
            P("pp", None, ep + tp),
            P("pp", ep + tp, None),
            P("pp", None),
        ),
        out_specs=(P("pp", ep, None), P("pp", ep + tp, None)),
        check_vma=False,
    )
```

```python
import functools

import jax
import jax.numpy as jnp
import numpy as np
from jax import lax
from jax.experimental import pallas as pl
from jax.experimental.pallas import tpu as pltpu
from jax.sharding import Mesh, PartitionSpec as P

BF16 = jnp.bfloat16
F32 = jnp.float32
VM = pl.BlockSpec(memory_space=pltpu.VMEM)
SM = pl.BlockSpec(memory_space=pltpu.SMEM)
CAP = 40
ROWS = 56


def served(n):
    blocks = {}
    for a in range(n):
        for t, c in enumerate((a - 1, a + 2 if a % 2 == 0 else a, a + 1, a if a % 2 == 0 else a + 2)):
            blocks[a, t] = (c % n, t ^ 2)
    return blocks
SMALL = 12 * 1024 * 1024
LARGE = 24 * 1024 * 1024


def call(kernel, outs, scalars=0, flops=0, moved=0):
    def run(*operands):
        specs = [SM] * scalars + [VM] * (len(operands) - scalars)
        return pl.pallas_call(
            kernel,
            out_shape=outs,
            in_specs=specs,
            out_specs=jax.tree.map(lambda _: VM, outs),
            compiler_params=pltpu.CompilerParams(vmem_limit_bytes=SMALL),
            cost_estimate=pl.CostEstimate(flops=flops, bytes_accessed=moved, transcendentals=0),
        )(*operands)

    return run


def in_hbm(value):
    return pltpu.with_memory_space_constraint(value, pltpu.HBM)


def shaped(dims, kind=BF16):
    return jax.ShapeDtypeStruct(dims, kind)


def nt(a, b):
    return lax.dot_general(a, b, (((1,), (1,)), ((), ())), preferred_element_type=F32)


def table(group, slots, first, meta):
    toks = meta.shape[1]
    topk = meta.shape[0] // 2
    wanted = (lax.broadcasted_iota(jnp.int32, (group, toks), 0) + first).astype(F32)
    scores = meta[topk:, :]
    total = jnp.sum(scores, axis=0, keepdims=True)
    member = jnp.zeros((group, toks), F32)
    weight = jnp.zeros((group, toks), F32)
    for k in range(topk):
        same = meta[k : k + 1, :] == wanted
        member = jnp.where(same, 1.0, member)
        weight = jnp.where(same, meta[topk + k : topk + k + 1, :] / total, weight)
    earlier = lax.broadcasted_iota(jnp.int32, (toks, toks), 0) < lax.broadcasted_iota(jnp.int32, (toks, toks), 1)
    rank = jnp.dot(member.astype(BF16), earlier.astype(F32).astype(BF16), preferred_element_type=F32)
    rank = jnp.where(member > 0.5, rank, -100.0)
    slot = (lax.broadcasted_iota(jnp.int32, (group, slots, toks), 1) - (slots - CAP)).astype(F32)
    return jnp.where(rank[:, None, :] == slot, 1.0, 0.0), weight


def pack_kernel(where, meta, toks, gain, ring, rows):
    n, width = rows.shape
    group = n // ROWS
    hit, _ = table(group, ROWS, where[0] * group, meta[...])
    wide = toks[...].astype(F32)
    scale = lax.rsqrt(jnp.mean(wide * wide, axis=-1, keepdims=True) + 1e-06)
    normed = (wide * scale * gain[...]).astype(BF16)
    images = jnp.concatenate([ring[i] for i in range(ring.shape[0])], axis=0)
    count, dv = images.shape
    spare = jnp.zeros((count, 2 * width - dv), F32)
    empty = jnp.zeros((CAP, width), F32)
    added = jnp.concatenate([images[:, :width], jnp.concatenate([images[:, width:], spare], axis=1), empty], axis=0)
    made = jnp.dot(hit.reshape(n, hit.shape[2]).astype(BF16), normed, preferred_element_type=F32)
    rows[...] = (made + jnp.concatenate([added] * group, axis=0)).astype(BF16)


def weigh_kernel(where, meta, high, low):
    toks, n = high.shape
    group = n // CAP
    hit, weight = table(group, CAP, where[0] * group, meta[...])
    scaled = (hit * weight[:, None, :]).reshape(n, toks).T
    top = scaled.astype(BF16)
    high[...] = top
    low[...] = (scaled - top.astype(F32)).astype(BF16)


ANYWHERE = pl.BlockSpec(memory_space=pl.ANY)


def expert_kernel(rows, *refs):
    shards, out = refs[:4], refs[4]
    rows_v, gate_v, up_v, down_v, hidden_v, out_v, row_sem, in_sem, out_sem = refs[5:]
    count = shards[0].shape[0] // 3
    row_copy = pltpu.make_async_copy(rows, rows_v, row_sem)
    row_copy.start()
    copies = []
    for s, shard in enumerate(shards):
        for p, held in enumerate((gate_v, up_v, down_v)):
            copies.append(
                pltpu.make_async_copy(
                    shard.at[pl.ds(p * count, count)], held.at[pl.ds(s * count, count)], in_sem.at[3 * s + p]
                )
            )
    for s in (0, 1):
        copies[3 * s].start()
        copies[3 * s + 1].start()
    row_copy.wait()
    for s in (0, 1):
        copies[3 * s].wait()
        copies[3 * s + 1].wait()
    for s in (2, 3):
        copies[3 * s].start()
        copies[3 * s + 1].start()
    flat = rows_v[...]
    step = 256
    seen = 2
    for c in range(4 * count // step):
        if c == 1:
            for s in range(4):
                copies[3 * s + 2].start()
        while seen * count < (c + 1) * step:
            copies[3 * seen].wait()
            copies[3 * seen + 1].wait()
            seen += 1
        block = slice(c * step, (c + 1) * step)
        gate = nt(flat, gate_v[block, :]).reshape(-1, ROWS, step)[:, ROWS - CAP :].reshape(-1, step)
        upval = nt(flat, up_v[block, :]).reshape(-1, ROWS, step)[:, ROWS - CAP :].reshape(-1, step)
        hidden_v[:, block] = (gate * jax.nn.sigmoid(gate) * upval).astype(BF16)
    for s in range(4):
        copies[3 * s + 2].wait()
    cols = out_v.shape[1] // 4
    leaving = []
    for j in range(4):
        block = slice(j * cols, (j + 1) * cols)
        out_v[:, block] = jnp.dot(hidden_v[...], down_v[:, block], preferred_element_type=F32).astype(BF16)
        copy = pltpu.make_async_copy(
            out_v.at[:, pl.ds(j * cols, cols)], out.at[:, pl.ds(j * cols, cols)], out_sem.at[j]
        )
        copy.start()
        leaving.append(copy)
    for copy in leaving:
        copy.wait()


def experts(rows, shards):
    given, width = rows.shape
    n = given // ROWS * CAP
    count = shards[0].shape[0] // 3 * 4
    return pl.pallas_call(
        expert_kernel,
        out_shape=pltpu.HBM((n, width), BF16),
        in_specs=[ANYWHERE] * 5,
        out_specs=ANYWHERE,
        scratch_shapes=[
            pltpu.VMEM((given, width), BF16),
            pltpu.VMEM((count, width), BF16),
            pltpu.VMEM((count, width), BF16),
            pltpu.VMEM((count, width), BF16),
            pltpu.VMEM((n, count), BF16),
            pltpu.VMEM((n, width), BF16),
            pltpu.SemaphoreType.DMA,
            pltpu.SemaphoreType.DMA((12,)),
            pltpu.SemaphoreType.DMA((4,)),
        ],
        compiler_params=pltpu.CompilerParams(vmem_limit_bytes=LARGE),
        cost_estimate=pl.CostEstimate(flops=6 * n * width * count, bytes_accessed=6 * count * width, transcendentals=0),
    )(in_hbm(rows), *[in_hbm(shard) for shard in shards])


def combine_kernel(where, toks, high, low, made, kept, given):
    half = made.shape[1] // 2
    low_side, core = 1 - where[1] // 2, lax.rem(where[1], 2)
    for out, h in ((kept, low_side), (given, 1 - low_side)):
        block = pl.ds(pl.multiple_of(h * half, half), half)
        part = made[:, block]
        summed = jnp.dot(high[...], part, preferred_element_type=F32)
        summed += jnp.dot(low[...], part, preferred_element_type=F32)
        if out is kept:
            summed += jnp.where(core == 0, toks[:, block].astype(F32), 0.0)
        out[...] = summed.astype(BF16)


def add_kernel(left, right, out):
    out[...] = (left[...].astype(F32) + right[...].astype(F32)).astype(out.dtype)


def join_kernel(where, own, across, out):
    cols = own.shape[1]
    yl = where[1] // 2
    for ref, half in ((own, yl), (across, 1 - yl)):
        out[:, pl.ds(pl.multiple_of(half * cols, cols), cols)] = ref[...]


def spread_kernel(row, out):
    wide = row[...].astype(F32)
    for i in range(out.shape[0]):
        out[i] = wide


def image_kernel(sizes, where, arrived, gain, weigh, first, first_other, second, second_other, mine, theirs, *scratch):
    n_yh, n_z = sizes
    rows_v, first_v, first_other_v, second_v, second_other_v, sem = scratch
    count = 2 * n_yh
    copies = [
        pltpu.make_async_copy(arrived.at[i, pl.ds(0, 2 * count)], rows_v.at[i], sem.at[i]) for i in range(n_z)
    ]
    held = ((first, first_v), (first_other, first_other_v), (second, second_v), (second_other, second_other_v))
    for i, (source, target) in enumerate(held):
        copies.append(pltpu.make_async_copy(source, target, sem.at[n_z + i]))
    for copy in copies:
        copy.start()
    for copy in copies:
        copy.wait()
    dv = gain.shape[1]
    wide = rows_v[...].astype(F32)
    width = wide.shape[2]
    n = n_z * count
    wide = jnp.concatenate(
        [wide[:, :count].reshape(n, width), wide[:, count:, : dv - width].reshape(n, dv - width)], axis=1
    )
    rows = wide.astype(BF16)
    scale = lax.rsqrt(jnp.mean(wide * wide, axis=-1, keepdims=True) + 1e-06)
    normed = (wide * scale * gain[...]).astype(BF16)
    yh, yl = where[0], where[1] // 2
    at = lax.broadcasted_iota(jnp.int32, (n, n), 0)
    z = lax.rem(at, n_z)
    high = lax.rem(at // n_z + yh, n_yh)
    low = lax.rem(at // (n_z * n_yh) + yl, 2)
    source = (z * n_yh + high) * 2 + low
    order = jnp.where(lax.broadcasted_iota(jnp.int32, (n, n), 1) == source, 1.0, 0.0).astype(BF16)
    whole = None
    for w_in, w_out in ((first_v, second_v), (first_other_v, second_other_v)):
        made = nt(normed, w_in[...])
        hidden = (0.5 * made * (1.0 + lax.erf(made * np.float32(0.5**0.5)))).astype(BF16)
        turned = jnp.dot(order, hidden, preferred_element_type=F32).astype(BF16)
        part = jnp.dot(turned, w_out[...], preferred_element_type=F32)
        whole = part if whole is None else whole + part
    whole = whole * weigh[...]
    images = jnp.dot(order, rows, preferred_element_type=F32)
    mark = lax.broadcasted_iota(jnp.int32, (n, 1), 0) == where[2]
    whole = whole + jnp.where(mark, images, 0.0)
    mine[...] = whole[: n // 2]
    theirs[...] = whole[n // 2 :].astype(BF16)


def encoder_part(where, arrived, gain, weigh, weights, n_yh):
    n_z, _, width = arrived.shape
    hidden, dv = weights[0].shape
    half = n_z * n_yh
    return pl.pallas_call(
        functools.partial(image_kernel, (n_yh, n_z)),
        out_shape=(shaped((half, dv), F32), shaped((half, dv))),
        in_specs=[SM, ANYWHERE, VM, VM] + [ANYWHERE] * 4,
        out_specs=(VM, VM),
        scratch_shapes=[pltpu.VMEM((n_z, 4 * n_yh, width), BF16)]
        + [pltpu.VMEM((hidden, dv), BF16)] * 4
        + [pltpu.SemaphoreType.DMA((n_z + 4,))],
        compiler_params=pltpu.CompilerParams(vmem_limit_bytes=SMALL),
        cost_estimate=pl.CostEstimate(flops=16 * half * dv * hidden, bytes_accessed=8 * hidden * dv, transcendentals=0),
    )(where, in_hbm(arrived), gain, weigh, *[in_hbm(w) for w in weights])


def fold_kernel(held, came, keep, *sends):
    total = held[...] + came[...].astype(F32)
    n = keep.shape[0]
    keep[...] = total[:n]
    for i, send in enumerate(sends):
        send[...] = total[n + i * send.shape[0] : n + (i + 1) * send.shape[0]].astype(BF16)


def column_kernel(held, *refs):
    out = refs[-1]
    total = held[...]
    for came in refs[:-1]:
        total += came[...].astype(F32)
    for i in range(out.shape[0]):
        out[i] = total[i : i + 1]


def encoded_kernel(spread, out):
    total = spread[0]
    for i in range(1, spread.shape[0]):
        total += spread[i]
    out[...] = total.astype(BF16)


def body(
    trunk_in,
    expert_ids,
    gate_scores,
    trunk_gain,
    w_gate,
    w_up,
    w_down,
    image_in,
    image_gain,
    fc_in,
    fc_out,
    layer_scale,
):
    n_pp, n_yh, n_z = (lax.axis_size(a) for a in ("pp", "yh", "z"))
    n_tp = lax.axis_size("yl") * lax.axis_size("core")
    n_square = n_yh * n_tp
    square = ("yh", "yl", "core")
    serve = served(n_yh)
    where = jnp.stack([lax.axis_index("yh"), lax.axis_index(("yl", "core")), lax.axis_index("z")]).astype(jnp.int32)

    def fetched(value):
        pairs = [(c * n_tp + copy, a * n_tp + t) for (a, t), (c, copy) in serve.items()]
        return lax.ppermute(value, square, pairs)

    def shifted(value, axis, by):
        n = lax.axis_size(axis)
        return lax.ppermute(value, axis, [(i, (i + by) % n) for i in range(n)])

    def exchanged(value, axis):
        return lax.all_to_all(value, axis, split_axis=0, concat_axis=0, tiled=True)

    tokens = trunk_in[0]
    toks, width = tokens.shape
    sent = fetched(tokens)
    meta = fetched(jnp.concatenate([expert_ids[0].T.astype(F32), gate_scores[0].T], axis=0))
    own = jnp.concatenate([w_gate[0, 0].T, w_up[0, 0].T, w_down[0, 0]], axis=0)
    image = image_in[0]
    dv = image.shape[1]
    ring = exchanged(call(spread_kernel, shaped((n_yh * 2, 1, dv), F32))(image), ("yh", "yl"))
    other = shifted(own, "core", 1)
    own, sent, meta, ring, where = lax.optimization_barrier((own, sent, meta, ring, where))
    across = shifted(own, "yl", 1)

    rows = call(pack_kernel, pltpu.HBM((n_z * ROWS, width), BF16), scalars=1)(where, meta, sent, trunk_gain, ring)
    arrived = exchanged(rows.reshape(n_z, ROWS, width), "z")

    first, second = fc_in[0].T, fc_out[0]
    first_other, second_other = shifted(first, "core", 1), shifted(second, "core", 1)
    across, other, first_other, second_other = lax.optimization_barrier((across, other, first_other, second_other))
    both = shifted(across, "core", 1)

    mine, theirs = encoder_part(where, arrived, image_gain, layer_scale, (first, first_other, second, second_other), n_yh)
    both, theirs = lax.optimization_barrier((both, theirs))
    made = experts(arrived.reshape(-1, width), (own, other, across, both))
    made, meta = lax.optimization_barrier((made, meta))
    n_rows = n_z * CAP
    returned = exchanged(made.reshape(n_z, CAP, width), "z").reshape(n_rows, width)
    high, low = call(weigh_kernel, (shaped((toks, n_rows)), shaped((toks, n_rows))), scalars=1)(where, meta)

    mine, *theirs = call(
        fold_kernel, (shaped((n_z, dv), F32),) + tuple(shaped((n_z, dv)) for _ in range(n_yh - 1))
    )(mine, shifted(theirs, "yl", 1))
    parts = [
        lax.ppermute(
            part,
            ("pp", "yh"),
            [(s * n_yh + h, (s - 1) % n_pp * n_yh + (h + k) % n_yh) for s in range(n_pp) for h in range(n_yh)],
        )
        for k, part in enumerate([mine, *theirs])
    ]
    column = call(column_kernel, shaped((n_z, 1, dv), F32))(*parts)

    column, returned = lax.optimization_barrier((column, returned))
    half = width // 2
    pieces = call(combine_kernel, (shaped((toks, half)), shaped((toks, half))), scalars=1, flops=4 * n_rows * toks * width)(
        where, sent, high, low, returned
    )
    pieces = [
        lax.ppermute(
            piece,
            ("pp",) + square,
            [
                (s * n_square + a * n_tp + t, (s + 1) % n_pp * n_square + c * n_tp + (copy ^ flip))
                for s in range(n_pp)
                for (a, t), (c, copy) in serve.items()
            ],
        )
        for flip, piece in zip((0, 2), pieces)
    ]
    part = call(add_kernel, shaped((toks, half)))(*pieces)
    spread, part = lax.optimization_barrier((exchanged(column, "z"), part))
    layer = call(add_kernel, shaped((toks, half)))(part, shifted(part, "core", 1))
    trunk_out = call(join_kernel, shaped((toks, width)), scalars=1)(where, layer, shifted(layer, "yl", 1))

    image_out = call(encoded_kernel, shaped((1, dv)))(spread)[None]
    return (trunk_out[None], image_out)


def solution(mesh):
    n_pp, n_ep, n_tp = (mesh.shape[a] for a in ("pp", "ep", "tp"))
    fine = Mesh(
        np.asarray(mesh.devices).reshape(n_pp, n_tp, n_ep // n_tp, n_tp // 2, 2),
        ("pp", "yh", "z", "yl", "core"),
    )
    ep, tp = ("yh", "z"), ("yl", "core")
    return jax.shard_map(
        body,
        mesh=fine,
        in_specs=(
            P("pp", ep, None),
            P("pp", ep, None),
            P("pp", ep, None),
            P("pp", None),
            P("pp", ep, None, tp),
            P("pp", ep, None, tp),
            P("pp", ep, tp, None),
            P("pp", ep + tp, None),
            P("pp", None),
            P("pp", None, ep + tp),
            P("pp", ep + tp, None),
            P("pp", None),
        ),
        out_specs=(P("pp", ep, None), P("pp", ep + tp, None)),
        check_vma=False,
    )
```

```python
import functools

import jax
import jax.numpy as jnp
import numpy as np
from jax import lax
from jax.experimental import pallas as pl
from jax.experimental.pallas import tpu as pltpu
from jax.sharding import Mesh, PartitionSpec as P

BF16 = jnp.bfloat16
F32 = jnp.float32
VM = pl.BlockSpec(memory_space=pltpu.VMEM)
SM = pl.BlockSpec(memory_space=pltpu.SMEM)
CAP = 40
ROWS = 56


def served(n):
    blocks = {}
    for a in range(n):
        for t, c in enumerate((a - 1, a + 2 if a % 2 == 0 else a, a + 1, a if a % 2 == 0 else a + 2)):
            blocks[a, t] = (c % n, t ^ 2)
    return blocks
SMALL = 12 * 1024 * 1024
LARGE = 24 * 1024 * 1024


def call(kernel, outs, scalars=0, flops=0, moved=0):
    def run(*operands):
        specs = [SM] * scalars + [VM] * (len(operands) - scalars)
        return pl.pallas_call(
            kernel,
            out_shape=outs,
            in_specs=specs,
            out_specs=jax.tree.map(lambda _: VM, outs),
            compiler_params=pltpu.CompilerParams(vmem_limit_bytes=SMALL),
            cost_estimate=pl.CostEstimate(flops=flops, bytes_accessed=moved, transcendentals=0),
        )(*operands)

    return run


def in_hbm(value):
    return pltpu.with_memory_space_constraint(value, pltpu.HBM)


def shaped(dims, kind=BF16):
    return jax.ShapeDtypeStruct(dims, kind)


def nt(a, b):
    return lax.dot_general(a, b, (((1,), (1,)), ((), ())), preferred_element_type=F32)


def table(group, slots, first, meta):
    toks = meta.shape[1]
    topk = meta.shape[0] // 2
    wanted = (lax.broadcasted_iota(jnp.int32, (group, toks), 0) + first).astype(F32)
    scores = meta[topk:, :]
    total = jnp.sum(scores, axis=0, keepdims=True)
    member = jnp.zeros((group, toks), F32)
    weight = jnp.zeros((group, toks), F32)
    for k in range(topk):
        same = meta[k : k + 1, :] == wanted
        member = jnp.where(same, 1.0, member)
        weight = jnp.where(same, meta[topk + k : topk + k + 1, :] / total, weight)
    earlier = lax.broadcasted_iota(jnp.int32, (toks, toks), 0) < lax.broadcasted_iota(jnp.int32, (toks, toks), 1)
    rank = jnp.dot(member.astype(BF16), earlier.astype(F32).astype(BF16), preferred_element_type=F32)
    rank = jnp.where(member > 0.5, rank, -100.0)
    slot = (lax.broadcasted_iota(jnp.int32, (group, slots, toks), 1) - (slots - CAP)).astype(F32)
    return jnp.where(rank[:, None, :] == slot, 1.0, 0.0), weight


def pack_kernel(where, meta, toks, gain, ring, rows):
    n, width = rows.shape
    group = n // ROWS
    hit, _ = table(group, ROWS, where[0] * group, meta[...])
    wide = toks[...].astype(F32)
    scale = lax.rsqrt(jnp.mean(wide * wide, axis=-1, keepdims=True) + 1e-06)
    normed = (wide * scale * gain[...]).astype(BF16)
    images = jnp.concatenate([ring[i] for i in range(ring.shape[0])], axis=0)
    count, dv = images.shape
    spare = jnp.zeros((count, 2 * width - dv), F32)
    empty = jnp.zeros((CAP, width), F32)
    added = jnp.concatenate([images[:, :width], jnp.concatenate([images[:, width:], spare], axis=1), empty], axis=0)
    made = jnp.dot(hit.reshape(n, hit.shape[2]).astype(BF16), normed, preferred_element_type=F32)
    rows[...] = (made + jnp.concatenate([added] * group, axis=0)).astype(BF16)


def weigh_kernel(where, meta, high, low):
    toks, n = high.shape
    group = n // CAP
    hit, weight = table(group, CAP, where[0] * group, meta[...])
    scaled = (hit * weight[:, None, :]).reshape(n, toks).T
    top = scaled.astype(BF16)
    high[...] = top
    low[...] = (scaled - top.astype(F32)).astype(BF16)


ANYWHERE = pl.BlockSpec(memory_space=pl.ANY)


def products(flat, gate_v, up_v):
    gate = nt(flat, gate_v)
    return (gate * jax.nn.sigmoid(gate) * nt(flat, up_v)).astype(BF16)


def gate_up(shards, starts, stops, gate_v, up_v, sem):
    copies, at = [], 0
    for shard, start, stop in zip(shards, starts, stops):
        count = shard.shape[0] // 3
        for p, held in enumerate((gate_v, up_v)):
            source = shard.at[pl.ds(p * count + start, stop - start)]
            copies.append(pltpu.make_async_copy(source, held.at[pl.ds(at, stop - start)], sem.at[len(copies)]))
        at += stop - start
    return copies


def first_kernel(arrived, own, other, across, rows, out, arrived_v, gate_v, up_v, row_sem, in_sem):
    count = own.shape[0] // 3
    row_copy = pltpu.make_async_copy(arrived, arrived_v, row_sem)
    row_copy.start()
    copies = gate_up((own, other, across), (0, 0, 0), (count, count, out.shape[1] - 2 * count), gate_v, up_v, in_sem)
    for copy in copies[:4]:
        copy.start()
    row_copy.wait()
    wide = arrived_v[...].astype(F32)
    flat = wide[:, ROWS - CAP :].reshape(rows.shape).astype(BF16)
    rows[...] = flat
    for copy in copies[:4]:
        copy.wait()
    for copy in copies[4:]:
        copy.start()
    step = 256
    for c in range(out.shape[1] // step):
        if c == 1:
            for copy in copies[4:]:
                copy.wait()
        block = slice(c * step, (c + 1) * step)
        out[:, block] = products(flat, gate_v[block, :], up_v[block, :])


def second_kernel(rows, begun, own, other, across, both, out, gate_v, up_v, down_v, hidden_v, out_v, in_sem, down_sem, out_sem):
    count = own.shape[0] // 3
    done = begun.shape[1]
    copies = gate_up((across, both), (done - 2 * count, 0), (count, count), gate_v, up_v, in_sem)
    downs = [
        pltpu.make_async_copy(shard.at[pl.ds(2 * count, count)], down_v.at[pl.ds(s * count, count)], down_sem.at[s])
        for s, shard in enumerate((own, other, across, both))
    ]
    for copy in copies + downs:
        copy.start()
    hidden_v[:, :done] = begun[...]
    for copy in copies:
        copy.wait()
    hidden_v[:, done:] = products(rows[...], gate_v[...], up_v[...])
    for copy in downs:
        copy.wait()
    cols = out_v.shape[1] // 4
    leaving = []
    for j in range(4):
        block = slice(j * cols, (j + 1) * cols)
        out_v[:, block] = jnp.dot(hidden_v[...], down_v[:, block], preferred_element_type=F32).astype(BF16)
        copy = pltpu.make_async_copy(
            out_v.at[:, pl.ds(j * cols, cols)], out.at[:, pl.ds(j * cols, cols)], out_sem.at[j]
        )
        copy.start()
        leaving.append(copy)
    for copy in leaving:
        copy.wait()


def experts(arrived, own, other, across, both):
    groups, _, width = arrived.shape
    n = groups * CAP
    count = own.shape[0] // 3 * 4
    begun, left = count // 3 * 2, count // 3
    own, other, across = (in_hbm(shard) for shard in (own, other, across))
    rows, hidden = pl.pallas_call(
        first_kernel,
        out_shape=(shaped((n, width)), shaped((n, begun))),
        in_specs=[ANYWHERE] * 4,
        out_specs=(VM, VM),
        scratch_shapes=[
            pltpu.VMEM(arrived.shape, BF16),
            pltpu.VMEM((begun, width), BF16),
            pltpu.VMEM((begun, width), BF16),
            pltpu.SemaphoreType.DMA,
            pltpu.SemaphoreType.DMA((6,)),
        ],
        compiler_params=pltpu.CompilerParams(vmem_limit_bytes=LARGE),
        cost_estimate=pl.CostEstimate(flops=4 * n * width * begun, bytes_accessed=4 * begun * width, transcendentals=0),
    )(in_hbm(arrived), own, other, across)
    return pl.pallas_call(
        second_kernel,
        out_shape=pltpu.HBM((n, width), BF16),
        in_specs=[VM, VM] + [ANYWHERE] * 4,
        out_specs=ANYWHERE,
        scratch_shapes=[
            pltpu.VMEM((left, width), BF16),
            pltpu.VMEM((left, width), BF16),
            pltpu.VMEM((count, width), BF16),
            pltpu.VMEM((n, count), BF16),
            pltpu.VMEM((n, width), BF16),
            pltpu.SemaphoreType.DMA((4,)),
            pltpu.SemaphoreType.DMA((4,)),
            pltpu.SemaphoreType.DMA((4,)),
        ],
        compiler_params=pltpu.CompilerParams(vmem_limit_bytes=LARGE),
        cost_estimate=pl.CostEstimate(flops=2 * n * width * (2 * left + count), bytes_accessed=4 * count * width, transcendentals=0),
    )(rows, hidden, own, other, across, both)


def combine_kernel(where, toks, high, low, made, kept, given):
    half = made.shape[1] // 2
    low_side, core = 1 - where[1] // 2, lax.rem(where[1], 2)
    for out, h in ((kept, low_side), (given, 1 - low_side)):
        block = pl.ds(pl.multiple_of(h * half, half), half)
        part = made[:, block]
        summed = jnp.dot(high[...], part, preferred_element_type=F32)
        summed += jnp.dot(low[...], part, preferred_element_type=F32)
        if out is kept:
            summed += jnp.where(core == 0, toks[:, block].astype(F32), 0.0)
        out[...] = summed.astype(BF16)


def add_kernel(left, right, out):
    out[...] = (left[...].astype(F32) + right[...].astype(F32)).astype(out.dtype)


def join_kernel(where, own, across, out, sem):
    cols = own.shape[1]
    yl = where[1] // 2
    copies = [
        pltpu.make_async_copy(ref, out.at[:, pl.ds(pl.multiple_of(half * cols, cols), cols)], sem.at[i])
        for i, (ref, half) in enumerate(((own, yl), (across, 1 - yl)))
    ]
    for copy in copies:
        copy.start()
    for copy in copies:
        copy.wait()


def joined(where, own, across):
    toks, cols = own.shape
    return pl.pallas_call(
        join_kernel,
        out_shape=pltpu.HBM((toks, 2 * cols), BF16),
        in_specs=[SM, VM, VM],
        out_specs=ANYWHERE,
        scratch_shapes=[pltpu.SemaphoreType.DMA((2,))],
        compiler_params=pltpu.CompilerParams(vmem_limit_bytes=SMALL),
    )(where, own, across)


def spread_kernel(row, out):
    wide = row[...].astype(F32)
    for i in range(out.shape[0]):
        out[i] = wide


def image_kernel(sizes, where, arrived, gain, weigh, first, first_other, second, second_other, mine, theirs, *scratch):
    n_yh, n_z = sizes
    rows_v, first_v, first_other_v, second_v, second_other_v, sem = scratch
    count = 2 * n_yh
    copies = [
        pltpu.make_async_copy(arrived.at[i, pl.ds(0, 2 * count)], rows_v.at[i], sem.at[i]) for i in range(n_z)
    ]
    held = ((first, first_v), (first_other, first_other_v), (second, second_v), (second_other, second_other_v))
    for i, (source, target) in enumerate(held):
        copies.append(pltpu.make_async_copy(source, target, sem.at[n_z + i]))
    for copy in copies:
        copy.start()
    for copy in copies:
        copy.wait()
    dv = gain.shape[1]
    wide = rows_v[...].astype(F32)
    width = wide.shape[2]
    n = n_z * count
    wide = jnp.concatenate(
        [wide[:, :count].reshape(n, width), wide[:, count:, : dv - width].reshape(n, dv - width)], axis=1
    )
    rows = wide.astype(BF16)
    scale = lax.rsqrt(jnp.mean(wide * wide, axis=-1, keepdims=True) + 1e-06)
    normed = (wide * scale * gain[...]).astype(BF16)
    yh, yl = where[0], where[1] // 2
    at = lax.broadcasted_iota(jnp.int32, (n, n), 0)
    z = lax.rem(at, n_z)
    high = lax.rem(at // n_z + yh, n_yh)
    low = lax.rem(at // (n_z * n_yh) + yl, 2)
    source = (z * n_yh + high) * 2 + low
    order = jnp.where(lax.broadcasted_iota(jnp.int32, (n, n), 1) == source, 1.0, 0.0).astype(BF16)
    whole = None
    for w_in, w_out in ((first_v, second_v), (first_other_v, second_other_v)):
        made = nt(normed, w_in[...])
        hidden = (0.5 * made * (1.0 + lax.erf(made * np.float32(0.5**0.5)))).astype(BF16)
        turned = jnp.dot(order, hidden, preferred_element_type=F32).astype(BF16)
        part = jnp.dot(turned, w_out[...], preferred_element_type=F32)
        whole = part if whole is None else whole + part
    whole = whole * weigh[...]
    images = jnp.dot(order, rows, preferred_element_type=F32)
    mark = lax.broadcasted_iota(jnp.int32, (n, 1), 0) == where[2]
    whole = whole + jnp.where(mark, images, 0.0)
    mine[...] = whole[: n // 2]
    theirs[...] = whole[n // 2 :].astype(BF16)


def encoder_part(where, arrived, gain, weigh, weights, n_yh):
    n_z, _, width = arrived.shape
    hidden, dv = weights[0].shape
    half = n_z * n_yh
    return pl.pallas_call(
        functools.partial(image_kernel, (n_yh, n_z)),
        out_shape=(shaped((half, dv), F32), shaped((half, dv))),
        in_specs=[SM, ANYWHERE, VM, VM] + [ANYWHERE] * 4,
        out_specs=(VM, VM),
        scratch_shapes=[pltpu.VMEM((n_z, 4 * n_yh, width), BF16)]
        + [pltpu.VMEM((hidden, dv), BF16)] * 4
        + [pltpu.SemaphoreType.DMA((n_z + 4,))],
        compiler_params=pltpu.CompilerParams(vmem_limit_bytes=SMALL),
        cost_estimate=pl.CostEstimate(flops=16 * half * dv * hidden, bytes_accessed=8 * hidden * dv, transcendentals=0),
    )(where, in_hbm(arrived), gain, weigh, *[in_hbm(w) for w in weights])


def fold_kernel(held, came, keep, *sends):
    total = held[...] + came[...].astype(F32)
    n = keep.shape[0]
    keep[...] = total[:n]
    for i, send in enumerate(sends):
        send[...] = total[n + i * send.shape[0] : n + (i + 1) * send.shape[0]].astype(BF16)


def column_kernel(held, *refs):
    out = refs[-1]
    total = held[...]
    for came in refs[:-1]:
        total += came[...].astype(F32)
    for i in range(out.shape[0]):
        out[i] = total[i : i + 1]


def encoded_kernel(spread, out):
    total = spread[0]
    for i in range(1, spread.shape[0]):
        total += spread[i]
    out[...] = total.astype(BF16)


def body(
    trunk_in,
    expert_ids,
    gate_scores,
    trunk_gain,
    w_gate,
    w_up,
    w_down,
    image_in,
    image_gain,
    fc_in,
    fc_out,
    layer_scale,
):
    n_pp, n_yh, n_z = (lax.axis_size(a) for a in ("pp", "yh", "z"))
    n_tp = lax.axis_size("yl") * lax.axis_size("core")
    n_square = n_yh * n_tp
    square = ("yh", "yl", "core")
    serve = served(n_yh)
    where = jnp.stack([lax.axis_index("yh"), lax.axis_index(("yl", "core")), lax.axis_index("z")]).astype(jnp.int32)

    def fetched(value):
        pairs = [(c * n_tp + copy, a * n_tp + t) for (a, t), (c, copy) in serve.items()]
        return lax.ppermute(value, square, pairs)

    def shifted(value, axis, by):
        n = lax.axis_size(axis)
        return lax.ppermute(value, axis, [(i, (i + by) % n) for i in range(n)])

    def exchanged(value, axis):
        return lax.all_to_all(value, axis, split_axis=0, concat_axis=0, tiled=True)

    tokens = trunk_in[0]
    toks, width = tokens.shape
    sent = fetched(tokens)
    meta = fetched(jnp.concatenate([expert_ids[0].T.astype(F32), gate_scores[0].T], axis=0))
    own = jnp.concatenate([w_gate[0, 0].T, w_up[0, 0].T, w_down[0, 0]], axis=0)
    image = image_in[0]
    dv = image.shape[1]
    ring = exchanged(call(spread_kernel, shaped((n_yh * 2, 1, dv), F32))(image), ("yh", "yl"))
    other = shifted(own, "core", 1)
    own, sent, meta, ring, where = lax.optimization_barrier((own, sent, meta, ring, where))
    across = shifted(own, "yl", 1)

    rows = call(pack_kernel, pltpu.HBM((n_z * ROWS, width), BF16), scalars=1)(where, meta, sent, trunk_gain, ring)
    arrived = exchanged(rows.reshape(n_z, ROWS, width), "z")

    first, second = fc_in[0].T, fc_out[0]
    first_other, second_other = shifted(first, "core", 1), shifted(second, "core", 1)
    across, other, first_other, second_other = lax.optimization_barrier((across, other, first_other, second_other))
    both = shifted(across, "core", 1)

    made = experts(arrived, own, other, across, both)
    made, meta = lax.optimization_barrier((made, meta))
    n_rows = n_z * CAP
    returned = exchanged(made.reshape(n_z, CAP, width), "z").reshape(n_rows, width)
    high, low = call(weigh_kernel, (shaped((toks, n_rows)), shaped((toks, n_rows))), scalars=1)(where, meta)

    mine, theirs = encoder_part(where, arrived, image_gain, layer_scale, (first, first_other, second, second_other), n_yh)
    mine, *theirs = call(
        fold_kernel, (shaped((n_z, dv), F32),) + tuple(shaped((n_z, dv)) for _ in range(n_yh - 1))
    )(mine, shifted(theirs, "yl", 1))
    parts = [
        lax.ppermute(
            part,
            ("pp", "yh"),
            [(s * n_yh + h, (s - 1) % n_pp * n_yh + (h + k) % n_yh) for s in range(n_pp) for h in range(n_yh)],
        )
        for k, part in enumerate([mine, *theirs])
    ]
    column = call(column_kernel, shaped((n_z, 1, dv), F32))(*parts)

    column, returned = lax.optimization_barrier((column, returned))
    half = width // 2
    pieces = call(combine_kernel, (shaped((toks, half)), shaped((toks, half))), scalars=1, flops=4 * n_rows * toks * width)(
        where, sent, high, low, returned
    )
    pieces = [
        lax.ppermute(
            piece,
            ("pp",) + square,
            [
                (s * n_square + a * n_tp + t, (s + 1) % n_pp * n_square + c * n_tp + (copy ^ flip))
                for s in range(n_pp)
                for (a, t), (c, copy) in serve.items()
            ],
        )
        for flip, piece in zip((0, 2), pieces)
    ]
    part = call(add_kernel, shaped((toks, half)))(*pieces)
    spread, part = lax.optimization_barrier((exchanged(column, "z"), part))
    layer = call(add_kernel, shaped((toks, half)))(part, shifted(part, "core", 1))
    trunk_out = joined(where, layer, shifted(layer, "yl", 1))

    image_out = call(encoded_kernel, shaped((1, dv)))(spread)[None]
    return (trunk_out[None], image_out)


def solution(mesh):
    n_pp, n_ep, n_tp = (mesh.shape[a] for a in ("pp", "ep", "tp"))
    fine = Mesh(
        np.asarray(mesh.devices).reshape(n_pp, n_tp, n_ep // n_tp, n_tp // 2, 2),
        ("pp", "yh", "z", "yl", "core"),
    )
    ep, tp = ("yh", "z"), ("yl", "core")
    return jax.shard_map(
        body,
        mesh=fine,
        in_specs=(
            P("pp", ep, None),
            P("pp", ep, None),
            P("pp", ep, None),
            P("pp", None),
            P("pp", ep, None, tp),
            P("pp", ep, None, tp),
            P("pp", ep, tp, None),
            P("pp", ep + tp, None),
            P("pp", None),
            P("pp", None, ep + tp),
            P("pp", ep + tp, None),
            P("pp", None),
        ),
        out_specs=(P("pp", ep, None), P("pp", ep + tp, None)),
        check_vma=False,
    )
```

```python
import functools

import jax
import jax.numpy as jnp
import numpy as np
from jax import lax
from jax.experimental import pallas as pl
from jax.experimental.pallas import tpu as pltpu
from jax.sharding import Mesh, PartitionSpec as P

BF16 = jnp.bfloat16
F32 = jnp.float32
VM = pl.BlockSpec(memory_space=pltpu.VMEM)
SM = pl.BlockSpec(memory_space=pltpu.SMEM)
CAP = 40
ROWS = 56


def served(n):
    blocks = {}
    for a in range(n):
        for t, c in enumerate((a - 1, a + 2 if a % 2 == 0 else a, a + 1, a if a % 2 == 0 else a + 2)):
            blocks[a, t] = (c % n, t ^ 2)
    return blocks
SMALL = 12 * 1024 * 1024
LARGE = 24 * 1024 * 1024


def call(kernel, outs, scalars=0, flops=0, moved=0):
    def run(*operands):
        specs = [SM] * scalars + [VM] * (len(operands) - scalars)
        return pl.pallas_call(
            kernel,
            out_shape=outs,
            in_specs=specs,
            out_specs=jax.tree.map(lambda _: VM, outs),
            compiler_params=pltpu.CompilerParams(vmem_limit_bytes=SMALL),
            cost_estimate=pl.CostEstimate(flops=flops, bytes_accessed=moved, transcendentals=0),
        )(*operands)

    return run


def in_hbm(value):
    return pltpu.with_memory_space_constraint(value, pltpu.HBM)


def shaped(dims, kind=BF16):
    return jax.ShapeDtypeStruct(dims, kind)


def nt(a, b):
    return lax.dot_general(a, b, (((1,), (1,)), ((), ())), preferred_element_type=F32)


def table(group, slots, first, meta):
    toks = meta.shape[1]
    topk = meta.shape[0] // 2
    wanted = (lax.broadcasted_iota(jnp.int32, (group, toks), 0) + first).astype(F32)
    scores = meta[topk:, :]
    total = jnp.sum(scores, axis=0, keepdims=True)
    member = jnp.zeros((group, toks), F32)
    weight = jnp.zeros((group, toks), F32)
    for k in range(topk):
        same = meta[k : k + 1, :] == wanted
        member = jnp.where(same, 1.0, member)
        weight = jnp.where(same, meta[topk + k : topk + k + 1, :] / total, weight)
    earlier = lax.broadcasted_iota(jnp.int32, (toks, toks), 0) < lax.broadcasted_iota(jnp.int32, (toks, toks), 1)
    rank = jnp.dot(member.astype(BF16), earlier.astype(F32).astype(BF16), preferred_element_type=F32)
    rank = jnp.where(member > 0.5, rank, -100.0)
    slot = (lax.broadcasted_iota(jnp.int32, (group, slots, toks), 1) - (slots - CAP)).astype(F32)
    return jnp.where(rank[:, None, :] == slot, 1.0, 0.0), weight


def pack_kernel(where, meta, toks, gain, ring, rows):
    n, width = rows.shape
    group = n // ROWS
    hit, _ = table(group, ROWS, where[0] * group, meta[...])
    wide = toks[...].astype(F32)
    scale = lax.rsqrt(jnp.mean(wide * wide, axis=-1, keepdims=True) + 1e-06)
    normed = (wide * scale * gain[...]).astype(BF16)
    images = jnp.concatenate([ring[i] for i in range(ring.shape[0])], axis=0)
    count, dv = images.shape
    spare = jnp.zeros((count, 2 * width - dv), F32)
    empty = jnp.zeros((CAP, width), F32)
    added = jnp.concatenate([images[:, :width], jnp.concatenate([images[:, width:], spare], axis=1), empty], axis=0)
    made = jnp.dot(hit.reshape(n, hit.shape[2]).astype(BF16), normed, preferred_element_type=F32)
    rows[...] = (made + jnp.concatenate([added] * group, axis=0)).astype(BF16)


def weigh_kernel(where, meta, high, low):
    toks, n = high.shape
    group = n // CAP
    hit, weight = table(group, CAP, where[0] * group, meta[...])
    scaled = (hit * weight[:, None, :]).reshape(n, toks).T
    top = scaled.astype(BF16)
    high[...] = top
    low[...] = (scaled - top.astype(F32)).astype(BF16)


ANYWHERE = pl.BlockSpec(memory_space=pl.ANY)


def products(flat, gate_v, up_v):
    gate = nt(flat, gate_v)
    return (gate * jax.nn.sigmoid(gate) * nt(flat, up_v)).astype(BF16)


def gate_up(shards, starts, stops, gate_v, up_v, sem):
    copies, at = [], 0
    for shard, start, stop in zip(shards, starts, stops):
        count = shard.shape[0] // 3
        for p, held in enumerate((gate_v, up_v)):
            source = shard.at[pl.ds(p * count + start, stop - start)]
            copies.append(pltpu.make_async_copy(source, held.at[pl.ds(at, stop - start)], sem.at[len(copies)]))
        at += stop - start
    return copies


def first_kernel(arrived, own, other, across, rows, out, arrived_v, gate_v, up_v, row_sem, in_sem):
    count = own.shape[0] // 3
    row_copy = pltpu.make_async_copy(arrived, arrived_v, row_sem)
    row_copy.start()
    copies = gate_up((own, other, across), (0, 0, 0), (count, count, out.shape[1] - 2 * count), gate_v, up_v, in_sem)
    for copy in copies[:4]:
        copy.start()
    row_copy.wait()
    wide = arrived_v[...].astype(F32)
    flat = wide[:, ROWS - CAP :].reshape(rows.shape).astype(BF16)
    rows[...] = flat
    for copy in copies[:4]:
        copy.wait()
    for copy in copies[4:]:
        copy.start()
    step = 256
    for c in range(out.shape[1] // step):
        if c == 1:
            for copy in copies[4:]:
                copy.wait()
        block = slice(c * step, (c + 1) * step)
        out[:, block] = products(flat, gate_v[block, :], up_v[block, :])


def second_kernel(rows, begun, own, other, across, both, out, gate_v, up_v, down_v, hidden_v, out_v, in_sem, down_sem, out_sem):
    count = own.shape[0] // 3
    done = begun.shape[1]
    copies = gate_up((across, both), (done - 2 * count, 0), (count, count), gate_v, up_v, in_sem)
    downs = [
        pltpu.make_async_copy(shard.at[pl.ds(2 * count, count)], down_v.at[pl.ds(s * count, count)], down_sem.at[s])
        for s, shard in enumerate((own, other, across, both))
    ]
    for copy in copies + downs:
        copy.start()
    hidden_v[:, :done] = begun[...]
    for copy in copies:
        copy.wait()
    hidden_v[:, done:] = products(rows[...], gate_v[...], up_v[...])
    for copy in downs:
        copy.wait()
    cols = out_v.shape[1] // 4
    leaving = []
    for j in range(4):
        block = slice(j * cols, (j + 1) * cols)
        out_v[:, block] = jnp.dot(hidden_v[...], down_v[:, block], preferred_element_type=F32).astype(BF16)
        copy = pltpu.make_async_copy(
            out_v.at[:, pl.ds(j * cols, cols)], out.at[:, pl.ds(j * cols, cols)], out_sem.at[j]
        )
        copy.start()
        leaving.append(copy)
    for copy in leaving:
        copy.wait()


def experts(arrived, own, other, across, both):
    groups, _, width = arrived.shape
    n = groups * CAP
    count = own.shape[0] // 3 * 4
    begun, left = count // 3 * 2, count // 3
    own, other, across = (in_hbm(shard) for shard in (own, other, across))
    rows, hidden = pl.pallas_call(
        first_kernel,
        out_shape=(shaped((n, width)), shaped((n, begun))),
        in_specs=[ANYWHERE] * 4,
        out_specs=(VM, VM),
        scratch_shapes=[
            pltpu.VMEM(arrived.shape, BF16),
            pltpu.VMEM((begun, width), BF16),
            pltpu.VMEM((begun, width), BF16),
            pltpu.SemaphoreType.DMA,
            pltpu.SemaphoreType.DMA((6,)),
        ],
        compiler_params=pltpu.CompilerParams(vmem_limit_bytes=LARGE),
        cost_estimate=pl.CostEstimate(flops=4 * n * width * begun, bytes_accessed=4 * begun * width, transcendentals=0),
    )(in_hbm(arrived), own, other, across)
    return pl.pallas_call(
        second_kernel,
        out_shape=pltpu.HBM((n, width), BF16),
        in_specs=[VM, VM] + [ANYWHERE] * 4,
        out_specs=ANYWHERE,
        scratch_shapes=[
            pltpu.VMEM((left, width), BF16),
            pltpu.VMEM((left, width), BF16),
            pltpu.VMEM((count, width), BF16),
            pltpu.VMEM((n, count), BF16),
            pltpu.VMEM((n, width), BF16),
            pltpu.SemaphoreType.DMA((4,)),
            pltpu.SemaphoreType.DMA((4,)),
            pltpu.SemaphoreType.DMA((4,)),
        ],
        compiler_params=pltpu.CompilerParams(vmem_limit_bytes=LARGE),
        cost_estimate=pl.CostEstimate(flops=2 * n * width * (2 * left + count), bytes_accessed=4 * count * width, transcendentals=0),
    )(rows, hidden, own, other, across, both)


def combine_kernel(where, toks, high, low, made, kept, given):
    half = made.shape[1] // 2
    low_side, core = 1 - where[1] // 2, lax.rem(where[1], 2)
    for out, h in ((kept, low_side), (given, 1 - low_side)):
        block = pl.ds(pl.multiple_of(h * half, half), half)
        part = made[:, block]
        summed = jnp.dot(high[...], part, preferred_element_type=F32)
        summed += jnp.dot(low[...], part, preferred_element_type=F32)
        if out is kept:
            summed += jnp.where(core == 0, toks[:, block].astype(F32), 0.0)
        out[...] = summed.astype(BF16)


def add_kernel(left, right, out):
    out[...] = (left[...].astype(F32) + right[...].astype(F32)).astype(out.dtype)


def join_kernel(where, own, across, out, sem):
    cols = own.shape[1]
    yl = where[1] // 2
    copies = [
        pltpu.make_async_copy(ref, out.at[:, pl.ds(pl.multiple_of(half * cols, cols), cols)], sem.at[i])
        for i, (ref, half) in enumerate(((own, yl), (across, 1 - yl)))
    ]
    for copy in copies:
        copy.start()
    for copy in copies:
        copy.wait()


def joined(where, own, across):
    toks, cols = own.shape
    return pl.pallas_call(
        join_kernel,
        out_shape=pltpu.HBM((toks, 2 * cols), BF16),
        in_specs=[SM, VM, VM],
        out_specs=ANYWHERE,
        scratch_shapes=[pltpu.SemaphoreType.DMA((2,))],
        compiler_params=pltpu.CompilerParams(vmem_limit_bytes=SMALL),
    )(where, own, across)


def spread_kernel(row, out):
    wide = row[...].astype(F32)
    for i in range(out.shape[0]):
        out[i] = wide


def image_kernel(sizes, where, arrived, gain, weigh, first, first_other, second, second_other, mine, theirs, *scratch):
    n_yh, n_z = sizes
    rows_v, first_v, first_other_v, second_v, second_other_v, sem = scratch
    count = 2 * n_yh
    copies = [
        pltpu.make_async_copy(arrived.at[i, pl.ds(0, 2 * count)], rows_v.at[i], sem.at[i]) for i in range(n_z)
    ]
    held = ((first, first_v), (first_other, first_other_v), (second, second_v), (second_other, second_other_v))
    for i, (source, target) in enumerate(held):
        copies.append(pltpu.make_async_copy(source, target, sem.at[n_z + i]))
    for copy in copies:
        copy.start()
    for copy in copies:
        copy.wait()
    dv = gain.shape[1]
    wide = rows_v[...].astype(F32)
    width = wide.shape[2]
    n = n_z * count
    wide = jnp.concatenate(
        [wide[:, :count].reshape(n, width), wide[:, count:, : dv - width].reshape(n, dv - width)], axis=1
    )
    rows = wide.astype(BF16)
    scale = lax.rsqrt(jnp.mean(wide * wide, axis=-1, keepdims=True) + 1e-06)
    normed = (wide * scale * gain[...]).astype(BF16)
    yh, yl = where[0], where[1] // 2
    at = lax.broadcasted_iota(jnp.int32, (n, n), 0)
    z = lax.rem(at, n_z)
    high = lax.rem(at // n_z + yh, n_yh)
    low = lax.rem(at // (n_z * n_yh) + yl, 2)
    source = (z * n_yh + high) * 2 + low
    order = jnp.where(lax.broadcasted_iota(jnp.int32, (n, n), 1) == source, 1.0, 0.0).astype(BF16)
    whole = None
    for w_in, w_out in ((first_v, second_v), (first_other_v, second_other_v)):
        made = nt(normed, w_in[...])
        hidden = (0.5 * made * (1.0 + lax.erf(made * np.float32(0.5**0.5)))).astype(BF16)
        turned = jnp.dot(order, hidden, preferred_element_type=F32).astype(BF16)
        part = jnp.dot(turned, w_out[...], preferred_element_type=F32)
        whole = part if whole is None else whole + part
    whole = whole * weigh[...]
    images = jnp.dot(order, rows, preferred_element_type=F32)
    mark = lax.broadcasted_iota(jnp.int32, (n, 1), 0) == where[2]
    whole = whole + jnp.where(mark, images, 0.0)
    mine[...] = whole[: n // 2]
    theirs[...] = whole[n // 2 :].astype(BF16)


def encoder_part(where, arrived, gain, weigh, weights, n_yh):
    n_z, _, width = arrived.shape
    hidden, dv = weights[0].shape
    half = n_z * n_yh
    return pl.pallas_call(
        functools.partial(image_kernel, (n_yh, n_z)),
        out_shape=(shaped((half, dv), F32), shaped((half, dv))),
        in_specs=[SM, ANYWHERE, VM, VM] + [ANYWHERE] * 4,
        out_specs=(VM, VM),
        scratch_shapes=[pltpu.VMEM((n_z, 4 * n_yh, width), BF16)]
        + [pltpu.VMEM((hidden, dv), BF16)] * 4
        + [pltpu.SemaphoreType.DMA((n_z + 4,))],
        compiler_params=pltpu.CompilerParams(vmem_limit_bytes=SMALL),
        cost_estimate=pl.CostEstimate(flops=16 * half * dv * hidden, bytes_accessed=8 * hidden * dv, transcendentals=0),
    )(where, in_hbm(arrived), gain, weigh, *[in_hbm(w) for w in weights])


def fold_kernel(held, came, keep, *sends):
    total = held[...] + came[...].astype(F32)
    n = keep.shape[0]
    keep[...] = total[:n]
    for i, send in enumerate(sends):
        send[...] = total[n + i * send.shape[0] : n + (i + 1) * send.shape[0]].astype(BF16)


def column_kernel(held, *refs):
    out = refs[-1]
    total = held[...]
    for came in refs[:-1]:
        total += came[...].astype(F32)
    for i in range(out.shape[0]):
        out[i] = total[i : i + 1]


def encoded_kernel(spread, out):
    total = spread[0]
    for i in range(1, spread.shape[0]):
        total += spread[i]
    out[...] = total.astype(BF16)


def body(
    trunk_in,
    expert_ids,
    gate_scores,
    trunk_gain,
    w_gate,
    w_up,
    w_down,
    image_in,
    image_gain,
    fc_in,
    fc_out,
    layer_scale,
):
    n_pp, n_yh, n_z = (lax.axis_size(a) for a in ("pp", "yh", "z"))
    n_tp = lax.axis_size("yl") * lax.axis_size("core")
    n_square = n_yh * n_tp
    square = ("yh", "yl", "core")
    serve = served(n_yh)
    where = jnp.stack([lax.axis_index("yh"), lax.axis_index(("yl", "core")), lax.axis_index("z")]).astype(jnp.int32)

    def fetched(value):
        pairs = [(c * n_tp + copy, a * n_tp + t) for (a, t), (c, copy) in serve.items()]
        return lax.ppermute(value, square, pairs)

    def shifted(value, axis, by):
        n = lax.axis_size(axis)
        return lax.ppermute(value, axis, [(i, (i + by) % n) for i in range(n)])

    def exchanged(value, axis):
        return lax.all_to_all(value, axis, split_axis=0, concat_axis=0, tiled=True)

    tokens = trunk_in[0]
    toks, width = tokens.shape
    sent = fetched(tokens)
    meta = fetched(jnp.concatenate([expert_ids[0].T.astype(F32), gate_scores[0].T], axis=0))
    own = jnp.concatenate([w_gate[0, 0].T, w_up[0, 0].T, w_down[0, 0]], axis=0)
    image = image_in[0]
    dv = image.shape[1]
    ring = exchanged(call(spread_kernel, shaped((n_yh * 2, 1, dv), F32))(image), ("yh", "yl"))
    other = shifted(own, "core", 1)
    own, sent, meta, ring, where = lax.optimization_barrier((own, sent, meta, ring, where))
    across = shifted(own, "yl", 1)

    rows = call(pack_kernel, pltpu.HBM((n_z * ROWS, width), BF16), scalars=1)(where, meta, sent, trunk_gain, ring)
    arrived = exchanged(rows.reshape(n_z, ROWS, width), "z")

    first, second = fc_in[0].T, fc_out[0]
    first_other, second_other = shifted(first, "core", 1), shifted(second, "core", 1)
    n_rows = n_z * CAP
    meta, second_other = lax.optimization_barrier((meta, second_other))
    high, low = call(weigh_kernel, (shaped((toks, n_rows)), shaped((toks, n_rows))), scalars=1)(where, meta)
    across, other, first_other, second_other, high, low = lax.optimization_barrier(
        (across, other, first_other, second_other, high, low)
    )
    both = shifted(across, "core", 1)

    made = experts(arrived, own, other, across, both)
    returned = exchanged(made.reshape(n_z, CAP, width), "z").reshape(n_rows, width)
    mine, theirs = encoder_part(where, arrived, image_gain, layer_scale, (first, first_other, second, second_other), n_yh)
    mine, *theirs = call(
        fold_kernel, (shaped((n_z, dv), F32),) + tuple(shaped((n_z, dv)) for _ in range(n_yh - 1))
    )(mine, shifted(theirs, "yl", 1))
    parts = [mine] + [shifted(part, "yh", k + 1) for k, part in enumerate(theirs)]
    column = call(column_kernel, shaped((n_z, 1, dv), F32))(*parts)

    column, returned = lax.optimization_barrier((column, returned))
    half = width // 2
    pieces = call(combine_kernel, (shaped((toks, half)), shaped((toks, half))), scalars=1, flops=4 * n_rows * toks * width)(
        where, sent, high, low, returned
    )
    pieces = [
        lax.ppermute(
            piece,
            ("pp",) + square,
            [
                (s * n_square + a * n_tp + t, (s + 1) % n_pp * n_square + c * n_tp + (copy ^ flip))
                for s in range(n_pp)
                for (a, t), (c, copy) in serve.items()
            ],
        )
        for flip, piece in zip((0, 2), pieces)
    ]
    part = call(add_kernel, shaped((toks, half)))(*pieces)
    spread, part = lax.optimization_barrier((exchanged(column, "z"), part))
    layer = call(add_kernel, shaped((toks, half)))(part, shifted(part, "core", 1))
    trunk_out = joined(where, layer, shifted(layer, "yl", 1))

    encoded = call(encoded_kernel, shaped((1, dv)))(spread)
    image_out = shifted(encoded[None], "pp", -1)
    return (trunk_out[None], image_out)


def solution(mesh):
    n_pp, n_ep, n_tp = (mesh.shape[a] for a in ("pp", "ep", "tp"))
    fine = Mesh(
        np.asarray(mesh.devices).reshape(n_pp, n_tp, n_ep // n_tp, n_tp // 2, 2),
        ("pp", "yh", "z", "yl", "core"),
    )
    ep, tp = ("yh", "z"), ("yl", "core")
    return jax.shard_map(
        body,
        mesh=fine,
        in_specs=(
            P("pp", ep, None),
            P("pp", ep, None),
            P("pp", ep, None),
            P("pp", None),
            P("pp", ep, None, tp),
            P("pp", ep, None, tp),
            P("pp", ep, tp, None),
            P("pp", ep + tp, None),
            P("pp", None),
            P("pp", None, ep + tp),
            P("pp", ep + tp, None),
            P("pp", None),
        ),
        out_specs=(P("pp", ep, None), P("pp", ep + tp, None)),
        check_vma=False,
    )
```

```python
import functools

import jax
import jax.numpy as jnp
import numpy as np
from jax import lax
from jax.experimental import pallas as pl
from jax.experimental.pallas import tpu as pltpu
from jax.sharding import Mesh, PartitionSpec as P

BF16 = jnp.bfloat16
F32 = jnp.float32
VM = pl.BlockSpec(memory_space=pltpu.VMEM)
SM = pl.BlockSpec(memory_space=pltpu.SMEM)
ANYWHERE = pl.BlockSpec(memory_space=pl.ANY)
CAP = 40
ROWS = 56


def served(n):
    blocks = {}
    for a in range(n):
        for t, c in enumerate((a - 1, a + 2 if a % 2 == 0 else a, a + 1, a if a % 2 == 0 else a + 2)):
            blocks[a, t] = (c % n, t ^ 2)
    return blocks
SMALL = 12 * 1024 * 1024
LARGE = 24 * 1024 * 1024


def call(kernel, outs, scalars=0, flops=0, moved=0):
    def run(*operands):
        specs = [SM] * scalars + [VM] * (len(operands) - scalars)
        return pl.pallas_call(
            kernel,
            out_shape=outs,
            in_specs=specs,
            out_specs=jax.tree.map(lambda _: VM, outs),
            compiler_params=pltpu.CompilerParams(vmem_limit_bytes=SMALL),
            cost_estimate=pl.CostEstimate(flops=flops, bytes_accessed=moved, transcendentals=0),
        )(*operands)

    return run


def in_hbm(value):
    return pltpu.with_memory_space_constraint(value, pltpu.HBM)


def shaped(dims, kind=BF16):
    return jax.ShapeDtypeStruct(dims, kind)


def nt(a, b):
    return lax.dot_general(a, b, (((1,), (1,)), ((), ())), preferred_element_type=F32)


def table(group, first, meta):
    toks = meta.shape[1]
    topk = meta.shape[0] // 2
    wanted = (lax.broadcasted_iota(jnp.int32, (group, toks), 0) + first).astype(F32)
    scores = meta[topk:, :]
    total = jnp.sum(scores, axis=0, keepdims=True)
    member = jnp.zeros((group, toks), F32)
    weight = jnp.zeros((group, toks), F32)
    for k in range(topk):
        same = meta[k : k + 1, :] == wanted
        member = jnp.where(same, 1.0, member)
        weight = jnp.where(same, meta[topk + k : topk + k + 1, :] / total, weight)
    earlier = lax.broadcasted_iota(jnp.int32, (toks, toks), 0) < lax.broadcasted_iota(jnp.int32, (toks, toks), 1)
    rank = jnp.dot(member.astype(BF16), earlier.astype(F32).astype(BF16), preferred_element_type=F32)
    rank = jnp.where(member > 0.5, rank, -1.0)
    slot = lax.broadcasted_iota(jnp.int32, (group, CAP, toks), 1).astype(F32)
    return jnp.where(rank[:, None, :] == slot, 1.0, 0.0), weight


def pack_kernel(where, meta, toks, gain, ring, rows, rows_v, sem):
    group, _, width = rows.shape
    hit, _ = table(group, where[0] * group, meta[...])
    wide = toks[...].astype(F32)
    scale = lax.rsqrt(jnp.mean(wide * wide, axis=-1, keepdims=True) + 1e-06)
    normed = (wide * scale * gain[...]).astype(BF16)
    images = jnp.concatenate([ring[i] for i in range(ring.shape[0])], axis=0)
    count, dv = images.shape
    spare = jnp.zeros((count, 2 * width - dv), F32)
    images = jnp.concatenate([images[:, :width], jnp.concatenate([images[:, width:], spare], axis=1)], axis=0)
    made = jnp.dot(hit.reshape(group * CAP, -1).astype(BF16), normed, preferred_element_type=F32)
    copies = []
    for i in range(group):
        rows_v[i] = jnp.concatenate([images, made[i * CAP : (i + 1) * CAP]], axis=0).astype(BF16)
        copies.append(pltpu.make_async_copy(rows_v.at[i], rows.at[i], sem.at[i]))
        copies[-1].start()
    for copy in copies:
        copy.wait()


def packed(where, meta, toks, gain, ring, group):
    dims = (group, ROWS, toks.shape[1])
    return pl.pallas_call(
        pack_kernel,
        out_shape=pltpu.HBM(dims, BF16),
        in_specs=[SM, VM, VM, VM, VM],
        out_specs=ANYWHERE,
        scratch_shapes=[pltpu.VMEM(dims, BF16), pltpu.SemaphoreType.DMA((group,))],
        compiler_params=pltpu.CompilerParams(vmem_limit_bytes=SMALL),
    )(where, meta, toks, gain, ring)


def weigh_kernel(where, meta, high, low):
    toks, n = high.shape
    group = n // CAP
    hit, weight = table(group, where[0] * group, meta[...])
    scaled = (hit * weight[:, None, :]).reshape(n, toks).T
    top = scaled.astype(BF16)
    high[...] = top
    low[...] = (scaled - top.astype(F32)).astype(BF16)


def products(flat, gate_v, up_v):
    gate = nt(flat, gate_v)
    return (gate * jax.nn.sigmoid(gate) * nt(flat, up_v)).astype(BF16)


def gate_up(shards, starts, stops, gate_v, up_v, sem):
    copies, at = [], 0
    for shard, start, stop in zip(shards, starts, stops):
        count = shard.shape[0] // 3
        for p, held in enumerate((gate_v, up_v)):
            source = shard.at[pl.ds(p * count + start, stop - start)]
            copies.append(pltpu.make_async_copy(source, held.at[pl.ds(at, stop - start)], sem.at[len(copies)]))
        at += stop - start
    return copies


def first_kernel(arrived, own, other, across, rows, out, arrived_v, gate_v, up_v, row_sem, in_sem):
    count = own.shape[0] // 3
    row_copy = pltpu.make_async_copy(arrived, arrived_v, row_sem)
    row_copy.start()
    copies = gate_up((own, other, across), (0, 0, 0), (count, count, out.shape[1] - 2 * count), gate_v, up_v, in_sem)
    for copy in copies[:4]:
        copy.start()
    row_copy.wait()
    wide = arrived_v[...].astype(F32)
    flat = wide[:, ROWS - CAP :].reshape(rows.shape).astype(BF16)
    rows[...] = flat
    for copy in copies[:4]:
        copy.wait()
    for copy in copies[4:]:
        copy.start()
    step = 256
    for c in range(out.shape[1] // step):
        if c == 1:
            for copy in copies[4:]:
                copy.wait()
        block = slice(c * step, (c + 1) * step)
        out[:, block] = products(flat, gate_v[block, :], up_v[block, :])


def second_kernel(rows, begun, own, other, across, both, out, gate_v, up_v, down_v, hidden_v, out_v, in_sem, down_sem, out_sem):
    count = own.shape[0] // 3
    done = begun.shape[1]
    copies = gate_up((across, both), (done - 2 * count, 0), (count, count), gate_v, up_v, in_sem)
    downs = [
        pltpu.make_async_copy(shard.at[pl.ds(2 * count, count)], down_v.at[pl.ds(s * count, count)], down_sem.at[s])
        for s, shard in enumerate((own, other, across, both))
    ]
    for copy in copies + downs:
        copy.start()
    hidden_v[:, :done] = begun[...]
    for copy in copies:
        copy.wait()
    hidden_v[:, done:] = products(rows[...], gate_v[...], up_v[...])
    for copy in downs:
        copy.wait()
    cols = out_v.shape[1] // 4
    leaving = []
    for j in range(4):
        block = slice(j * cols, (j + 1) * cols)
        out_v[:, block] = jnp.dot(hidden_v[...], down_v[:, block], preferred_element_type=F32).astype(BF16)
        copy = pltpu.make_async_copy(
            out_v.at[:, pl.ds(j * cols, cols)], out.at[:, pl.ds(j * cols, cols)], out_sem.at[j]
        )
        copy.start()
        leaving.append(copy)
    for copy in leaving:
        copy.wait()


def experts(arrived, own, other, across, both):
    groups, _, width = arrived.shape
    n = groups * CAP
    count = own.shape[0] // 3 * 4
    begun, left = count // 3 * 2, count // 3
    own, other, across = (in_hbm(shard) for shard in (own, other, across))
    rows, hidden = pl.pallas_call(
        first_kernel,
        out_shape=(shaped((n, width)), shaped((n, begun))),
        in_specs=[ANYWHERE] * 4,
        out_specs=(VM, VM),
        scratch_shapes=[
            pltpu.VMEM(arrived.shape, BF16),
            pltpu.VMEM((begun, width), BF16),
            pltpu.VMEM((begun, width), BF16),
            pltpu.SemaphoreType.DMA,
            pltpu.SemaphoreType.DMA((6,)),
        ],
        compiler_params=pltpu.CompilerParams(vmem_limit_bytes=LARGE),
        cost_estimate=pl.CostEstimate(flops=4 * n * width * begun, bytes_accessed=4 * begun * width, transcendentals=0),
    )(in_hbm(arrived), own, other, across)
    return pl.pallas_call(
        second_kernel,
        out_shape=pltpu.HBM((n, width), BF16),
        in_specs=[VM, VM] + [ANYWHERE] * 4,
        out_specs=ANYWHERE,
        scratch_shapes=[
            pltpu.VMEM((left, width), BF16),
            pltpu.VMEM((left, width), BF16),
            pltpu.VMEM((count, width), BF16),
            pltpu.VMEM((n, count), BF16),
            pltpu.VMEM((n, width), BF16),
            pltpu.SemaphoreType.DMA((4,)),
            pltpu.SemaphoreType.DMA((4,)),
            pltpu.SemaphoreType.DMA((4,)),
        ],
        compiler_params=pltpu.CompilerParams(vmem_limit_bytes=LARGE),
        cost_estimate=pl.CostEstimate(flops=2 * n * width * (2 * left + count), bytes_accessed=4 * count * width, transcendentals=0),
    )(rows, hidden, own, other, across, both)


def combine_kernel(where, toks, high, low, made, kept, given):
    half = made.shape[1] // 2
    low_side, core = 1 - where[1] // 2, lax.rem(where[1], 2)
    for out, h in ((kept, low_side), (given, 1 - low_side)):
        block = pl.ds(pl.multiple_of(h * half, half), half)
        part = made[:, block]
        summed = jnp.dot(high[...], part, preferred_element_type=F32)
        summed += jnp.dot(low[...], part, preferred_element_type=F32)
        if out is kept:
            summed += jnp.where(core == 0, toks[:, block].astype(F32), 0.0)
        out[...] = summed.astype(BF16)


def add_kernel(left, right, out):
    out[...] = (left[...].astype(F32) + right[...].astype(F32)).astype(out.dtype)


def join_kernel(where, own, across, out, sem):
    cols = own.shape[1]
    yl = where[1] // 2
    copies = [
        pltpu.make_async_copy(ref, out.at[:, pl.ds(pl.multiple_of(half * cols, cols), cols)], sem.at[i])
        for i, (ref, half) in enumerate(((own, yl), (across, 1 - yl)))
    ]
    for copy in copies:
        copy.start()
    for copy in copies:
        copy.wait()


def joined(where, own, across):
    toks, cols = own.shape
    return pl.pallas_call(
        join_kernel,
        out_shape=pltpu.HBM((toks, 2 * cols), BF16),
        in_specs=[SM, VM, VM],
        out_specs=ANYWHERE,
        scratch_shapes=[pltpu.SemaphoreType.DMA((2,))],
        compiler_params=pltpu.CompilerParams(vmem_limit_bytes=SMALL),
    )(where, own, across)


def spread_kernel(row, out):
    wide = row[...].astype(F32)
    for i in range(out.shape[0]):
        out[i] = wide


def image_kernel(sizes, where, arrived, gain, weigh, first, first_other, second, second_other, mine, theirs, *scratch):
    n_yh, n_z = sizes
    rows_v, first_v, first_other_v, second_v, second_other_v, sem = scratch
    count = 2 * n_yh
    copies = [
        pltpu.make_async_copy(arrived.at[i, pl.ds(0, 2 * count)], rows_v.at[i], sem.at[i]) for i in range(n_z)
    ]
    held = ((first, first_v), (first_other, first_other_v), (second, second_v), (second_other, second_other_v))
    for i, (source, target) in enumerate(held):
        copies.append(pltpu.make_async_copy(source, target, sem.at[n_z + i]))
    for copy in copies:
        copy.start()
    for copy in copies:
        copy.wait()
    dv = gain.shape[1]
    wide = rows_v[...].astype(F32)
    width = wide.shape[2]
    n = n_z * count
    wide = jnp.concatenate(
        [wide[:, :count].reshape(n, width), wide[:, count:, : dv - width].reshape(n, dv - width)], axis=1
    )
    rows = wide.astype(BF16)
    scale = lax.rsqrt(jnp.mean(wide * wide, axis=-1, keepdims=True) + 1e-06)
    normed = (wide * scale * gain[...]).astype(BF16)
    yh, yl = where[0], where[1] // 2
    at = lax.broadcasted_iota(jnp.int32, (n, n), 0)
    z = lax.rem(at, n_z)
    high = lax.rem(at // n_z + yh, n_yh)
    low = lax.rem(at // (n_z * n_yh) + yl, 2)
    source = (z * n_yh + high) * 2 + low
    order = jnp.where(lax.broadcasted_iota(jnp.int32, (n, n), 1) == source, 1.0, 0.0).astype(BF16)
    whole = None
    for w_in, w_out in ((first_v, second_v), (first_other_v, second_other_v)):
        made = nt(normed, w_in[...])
        hidden = (0.5 * made * (1.0 + lax.erf(made * np.float32(0.5**0.5)))).astype(BF16)
        turned = jnp.dot(order, hidden, preferred_element_type=F32).astype(BF16)
        part = jnp.dot(turned, w_out[...], preferred_element_type=F32)
        whole = part if whole is None else whole + part
    whole = whole * weigh[...]
    images = jnp.dot(order, rows, preferred_element_type=F32)
    mark = lax.broadcasted_iota(jnp.int32, (n, 1), 0) == where[2]
    whole = whole + jnp.where(mark, images, 0.0)
    mine[...] = whole[: n // 2]
    theirs[...] = whole[n // 2 :].astype(BF16)


def encoder_part(where, arrived, gain, weigh, weights, n_yh):
    n_z, _, width = arrived.shape
    hidden, dv = weights[0].shape
    half = n_z * n_yh
    return pl.pallas_call(
        functools.partial(image_kernel, (n_yh, n_z)),
        out_shape=(shaped((half, dv), F32), shaped((half, dv))),
        in_specs=[SM, ANYWHERE, VM, VM] + [ANYWHERE] * 4,
        out_specs=(VM, VM),
        scratch_shapes=[pltpu.VMEM((n_z, 4 * n_yh, width), BF16)]
        + [pltpu.VMEM((hidden, dv), BF16)] * 4
        + [pltpu.SemaphoreType.DMA((n_z + 4,))],
        compiler_params=pltpu.CompilerParams(vmem_limit_bytes=SMALL),
        cost_estimate=pl.CostEstimate(flops=16 * half * dv * hidden, bytes_accessed=8 * hidden * dv, transcendentals=0),
    )(where, in_hbm(arrived), gain, weigh, *[in_hbm(w) for w in weights])


def fold_kernel(held, came, keep, *sends):
    total = held[...] + came[...].astype(F32)
    n = keep.shape[0]
    keep[...] = total[:n]
    for i, send in enumerate(sends):
        send[...] = total[n + i * send.shape[0] : n + (i + 1) * send.shape[0]].astype(BF16)


def column_kernel(held, *refs):
    out = refs[-1]
    total = held[...]
    for came in refs[:-1]:
        total += came[...].astype(F32)
    for i in range(out.shape[0]):
        out[i] = total[i : i + 1]


def encoded_kernel(spread, out):
    total = spread[0]
    for i in range(1, spread.shape[0]):
        total += spread[i]
    out[...] = total.astype(BF16)


def body(
    trunk_in,
    expert_ids,
    gate_scores,
    trunk_gain,
    w_gate,
    w_up,
    w_down,
    image_in,
    image_gain,
    fc_in,
    fc_out,
    layer_scale,
):
    n_pp, n_yh, n_z = (lax.axis_size(a) for a in ("pp", "yh", "z"))
    n_tp = lax.axis_size("yl") * lax.axis_size("core")
    n_square = n_yh * n_tp
    square = ("yh", "yl", "core")
    serve = served(n_yh)
    where = jnp.stack([lax.axis_index("yh"), lax.axis_index(("yl", "core")), lax.axis_index("z")]).astype(jnp.int32)

    def fetched(value):
        pairs = [(c * n_tp + copy, a * n_tp + t) for (a, t), (c, copy) in serve.items()]
        return lax.ppermute(value, square, pairs)

    def shifted(value, axis, by):
        n = lax.axis_size(axis)
        return lax.ppermute(value, axis, [(i, (i + by) % n) for i in range(n)])

    def exchanged(value, axis):
        return lax.all_to_all(value, axis, split_axis=0, concat_axis=0, tiled=True)

    tokens = trunk_in[0]
    toks, width = tokens.shape
    sent = fetched(tokens)
    meta = fetched(jnp.concatenate([expert_ids[0].T.astype(F32), gate_scores[0].T], axis=0))
    own = jnp.concatenate([w_gate[0, 0].T, w_up[0, 0].T, w_down[0, 0]], axis=0)
    image = image_in[0]
    dv = image.shape[1]
    ring = exchanged(call(spread_kernel, shaped((n_yh * 2, 1, dv), F32))(image), ("yh", "yl"))
    other = shifted(own, "core", 1)
    own, sent, meta, ring, where = lax.optimization_barrier((own, sent, meta, ring, where))
    across = shifted(own, "yl", 1)

    arrived = exchanged(packed(where, meta, sent, trunk_gain, ring, n_z), "z")

    first, second = fc_in[0].T, fc_out[0]
    first_other, second_other = shifted(first, "core", 1), shifted(second, "core", 1)
    n_rows = n_z * CAP
    meta, second_other = lax.optimization_barrier((meta, second_other))
    high, low = call(weigh_kernel, (shaped((toks, n_rows)), shaped((toks, n_rows))), scalars=1)(where, meta)
    across, other, first_other, second_other, high, low = lax.optimization_barrier(
        (across, other, first_other, second_other, high, low)
    )
    both = shifted(across, "core", 1)

    made = experts(arrived, own, other, across, both)
    returned = exchanged(made.reshape(n_z, CAP, width), "z").reshape(n_rows, width)
    mine, theirs = encoder_part(where, arrived, image_gain, layer_scale, (first, first_other, second, second_other), n_yh)
    mine, *theirs = call(
        fold_kernel, (shaped((n_z, dv), F32),) + tuple(shaped((n_z, dv)) for _ in range(n_yh - 1))
    )(mine, shifted(theirs, "yl", 1))
    parts = [mine] + [shifted(part, "yh", k + 1) for k, part in enumerate(theirs)]
    column = call(column_kernel, shaped((n_z, 1, dv), F32))(*parts)

    column, returned = lax.optimization_barrier((column, returned))
    half = width // 2
    pieces = call(combine_kernel, (shaped((toks, half)), shaped((toks, half))), scalars=1, flops=4 * n_rows * toks * width)(
        where, sent, high, low, returned
    )
    pieces = [
        lax.ppermute(
            piece,
            ("pp",) + square,
            [
                (s * n_square + a * n_tp + t, (s + 1) % n_pp * n_square + c * n_tp + (copy ^ flip))
                for s in range(n_pp)
                for (a, t), (c, copy) in serve.items()
            ],
        )
        for flip, piece in zip((0, 2), pieces)
    ]
    part = call(add_kernel, shaped((toks, half)))(*pieces)
    spread, part = lax.optimization_barrier((exchanged(column, "z"), part))
    layer = call(add_kernel, shaped((toks, half)))(part, shifted(part, "core", 1))
    trunk_out = joined(where, layer, shifted(layer, "yl", 1))

    encoded = call(encoded_kernel, shaped((1, dv)))(spread)
    image_out = shifted(encoded[None], "pp", -1)
    return (trunk_out[None], image_out)


def solution(mesh):
    n_pp, n_ep, n_tp = (mesh.shape[a] for a in ("pp", "ep", "tp"))
    fine = Mesh(
        np.asarray(mesh.devices).reshape(n_pp, n_tp, n_ep // n_tp, n_tp // 2, 2),
        ("pp", "yh", "z", "yl", "core"),
    )
    ep, tp = ("yh", "z"), ("yl", "core")
    return jax.shard_map(
        body,
        mesh=fine,
        in_specs=(
            P("pp", ep, None),
            P("pp", ep, None),
            P("pp", ep, None),
            P("pp", None),
            P("pp", ep, None, tp),
            P("pp", ep, None, tp),
            P("pp", ep, tp, None),
            P("pp", ep + tp, None),
            P("pp", None),
            P("pp", None, ep + tp),
            P("pp", ep + tp, None),
            P("pp", None),
        ),
        out_specs=(P("pp", ep, None), P("pp", ep + tp, None)),
        check_vma=False,
    )
```

```python
import functools

import jax
import jax.numpy as jnp
import numpy as np
from jax import lax
from jax.experimental import pallas as pl
from jax.experimental.pallas import tpu as pltpu
from jax.sharding import Mesh, PartitionSpec as P

BF16 = jnp.bfloat16
F32 = jnp.float32
VM = pl.BlockSpec(memory_space=pltpu.VMEM)
SM = pl.BlockSpec(memory_space=pltpu.SMEM)
ANYWHERE = pl.BlockSpec(memory_space=pl.ANY)
CAP = 40
ROWS = 56


def served(n):
    blocks = {}
    for a in range(n):
        for t, c in enumerate((a - 1, a + 2 if a % 2 == 0 else a, a + 1, a if a % 2 == 0 else a + 2)):
            blocks[a, t] = (c % n, t ^ 2)
    return blocks
SMALL = 12 * 1024 * 1024
LARGE = 24 * 1024 * 1024


def call(kernel, outs, scalars=0, flops=0, moved=0):
    def run(*operands):
        specs = [SM] * scalars + [VM] * (len(operands) - scalars)
        return pl.pallas_call(
            kernel,
            out_shape=outs,
            in_specs=specs,
            out_specs=jax.tree.map(lambda _: VM, outs),
            compiler_params=pltpu.CompilerParams(vmem_limit_bytes=SMALL),
            cost_estimate=pl.CostEstimate(flops=flops, bytes_accessed=moved, transcendentals=0),
        )(*operands)

    return run


def in_hbm(value):
    return pltpu.with_memory_space_constraint(value, pltpu.HBM)


def shaped(dims, kind=BF16):
    return jax.ShapeDtypeStruct(dims, kind)


def nt(a, b):
    return lax.dot_general(a, b, (((1,), (1,)), ((), ())), preferred_element_type=F32)


def table(group, first, meta):
    toks = meta.shape[1]
    topk = meta.shape[0] // 2
    wanted = (lax.broadcasted_iota(jnp.int32, (group, toks), 0) + first).astype(F32)
    scores = meta[topk:, :]
    total = jnp.sum(scores, axis=0, keepdims=True)
    member = jnp.zeros((group, toks), F32)
    weight = jnp.zeros((group, toks), F32)
    for k in range(topk):
        same = meta[k : k + 1, :] == wanted
        member = jnp.where(same, 1.0, member)
        weight = jnp.where(same, meta[topk + k : topk + k + 1, :] / total, weight)
    earlier = lax.broadcasted_iota(jnp.int32, (toks, toks), 0) < lax.broadcasted_iota(jnp.int32, (toks, toks), 1)
    rank = jnp.dot(member.astype(BF16), earlier.astype(F32).astype(BF16), preferred_element_type=F32)
    rank = jnp.where(member > 0.5, rank, -1.0)
    slot = lax.broadcasted_iota(jnp.int32, (group, CAP, toks), 1).astype(F32)
    return jnp.where(rank[:, None, :] == slot, 1.0, 0.0), weight


def pack_kernel(where, meta, toks, gain, ring, rows, rows_v, sem):
    group, _, width = rows.shape
    hit, _ = table(group, where[0] * group, meta[...])
    wide = toks[...].astype(F32)
    scale = lax.rsqrt(jnp.mean(wide * wide, axis=-1, keepdims=True) + 1e-06)
    normed = (wide * scale * gain[...]).astype(BF16)
    images = jnp.concatenate([ring[i] for i in range(ring.shape[0])], axis=0)
    count, dv = images.shape
    spare = jnp.zeros((count, 2 * width - dv), F32)
    images = jnp.concatenate([images[:, :width], jnp.concatenate([images[:, width:], spare], axis=1)], axis=0)
    made = jnp.dot(hit.reshape(group * CAP, -1).astype(BF16), normed, preferred_element_type=F32)
    copies = []
    for i in range(group):
        rows_v[i] = jnp.concatenate([images, made[i * CAP : (i + 1) * CAP]], axis=0).astype(BF16)
        copies.append(pltpu.make_async_copy(rows_v.at[i], rows.at[i], sem.at[i]))
        copies[-1].start()
    for copy in copies:
        copy.wait()


def packed(where, meta, toks, gain, ring, group):
    dims = (group, ROWS, toks.shape[1])
    return pl.pallas_call(
        pack_kernel,
        out_shape=pltpu.HBM(dims, BF16),
        in_specs=[SM, VM, VM, VM, VM],
        out_specs=ANYWHERE,
        scratch_shapes=[pltpu.VMEM(dims, BF16), pltpu.SemaphoreType.DMA((group,))],
        compiler_params=pltpu.CompilerParams(vmem_limit_bytes=SMALL),
    )(where, meta, toks, gain, ring)


def weigh_kernel(where, meta, high, low):
    toks, n = high.shape
    group = n // CAP
    hit, weight = table(group, where[0] * group, meta[...])
    scaled = (hit * weight[:, None, :]).reshape(n, toks).T
    top = scaled.astype(BF16)
    high[...] = top
    low[...] = (scaled - top.astype(F32)).astype(BF16)


def products(flat, gate_v, up_v):
    gate = nt(flat, gate_v)
    return (gate * jax.nn.sigmoid(gate) * nt(flat, up_v)).astype(BF16)


def gate_up(shards, starts, stops, gate_v, up_v, sem):
    copies, at = [], 0
    for shard, start, stop in zip(shards, starts, stops):
        count = shard.shape[0] // 3
        for p, held in enumerate((gate_v, up_v)):
            source = shard.at[pl.ds(p * count + start, stop - start)]
            copies.append(pltpu.make_async_copy(source, held.at[pl.ds(at, stop - start)], sem.at[len(copies)]))
        at += stop - start
    return copies


def first_kernel(arrived, own, other, across, rows, out, arrived_v, gate_v, up_v, row_sem, in_sem):
    count = own.shape[0] // 3
    row_copy = pltpu.make_async_copy(arrived, arrived_v, row_sem)
    row_copy.start()
    copies = gate_up((own, other, across), (0, 0, 0), (count, count, out.shape[1] - 2 * count), gate_v, up_v, in_sem)
    for copy in copies[:4]:
        copy.start()
    row_copy.wait()
    wide = arrived_v[...].astype(F32)
    flat = wide[:, ROWS - CAP :].reshape(rows.shape).astype(BF16)
    rows[...] = flat
    for copy in copies[:4]:
        copy.wait()
    for copy in copies[4:]:
        copy.start()
    step = 256
    for c in range(out.shape[1] // step):
        if c == 1:
            for copy in copies[4:]:
                copy.wait()
        block = slice(c * step, (c + 1) * step)
        out[:, block] = products(flat, gate_v[block, :], up_v[block, :])


def second_kernel(rows, begun, own, other, across, both, out, gate_v, up_v, down_v, hidden_v, out_v, in_sem, down_sem, out_sem):
    count = own.shape[0] // 3
    done = begun.shape[1]
    copies = gate_up((across, both), (done - 2 * count, 0), (count, count), gate_v, up_v, in_sem)
    downs = [
        pltpu.make_async_copy(shard.at[pl.ds(2 * count, count)], down_v.at[pl.ds(s * count, count)], down_sem.at[s])
        for s, shard in enumerate((own, other, across, both))
    ]
    for copy in copies + downs:
        copy.start()
    hidden_v[:, :done] = begun[...]
    for copy in copies:
        copy.wait()
    hidden_v[:, done:] = products(rows[...], gate_v[...], up_v[...])
    for copy in downs:
        copy.wait()
    cols = out_v.shape[1] // 4
    leaving = []
    for j in range(4):
        block = slice(j * cols, (j + 1) * cols)
        out_v[:, block] = jnp.dot(hidden_v[...], down_v[:, block], preferred_element_type=F32).astype(BF16)
        copy = pltpu.make_async_copy(
            out_v.at[:, pl.ds(j * cols, cols)], out.at[:, pl.ds(j * cols, cols)], out_sem.at[j]
        )
        copy.start()
        leaving.append(copy)
    for copy in leaving:
        copy.wait()


def experts(arrived, own, other, across, both):
    groups, _, width = arrived.shape
    n = groups * CAP
    count = own.shape[0] // 3 * 4
    begun, left = count // 3 * 2, count // 3
    other, across = in_hbm(other), in_hbm(across)
    rows, hidden = pl.pallas_call(
        first_kernel,
        out_shape=(shaped((n, width)), shaped((n, begun))),
        in_specs=[ANYWHERE] * 4,
        out_specs=(VM, VM),
        scratch_shapes=[
            pltpu.VMEM(arrived.shape, BF16),
            pltpu.VMEM((begun, width), BF16),
            pltpu.VMEM((begun, width), BF16),
            pltpu.SemaphoreType.DMA,
            pltpu.SemaphoreType.DMA((6,)),
        ],
        compiler_params=pltpu.CompilerParams(vmem_limit_bytes=LARGE),
        cost_estimate=pl.CostEstimate(flops=4 * n * width * begun, bytes_accessed=4 * begun * width, transcendentals=0),
    )(in_hbm(arrived), own, other, across)
    return pl.pallas_call(
        second_kernel,
        out_shape=pltpu.HBM((n, width), BF16),
        in_specs=[VM, VM] + [ANYWHERE] * 4,
        out_specs=ANYWHERE,
        scratch_shapes=[
            pltpu.VMEM((left, width), BF16),
            pltpu.VMEM((left, width), BF16),
            pltpu.VMEM((count, width), BF16),
            pltpu.VMEM((n, count), BF16),
            pltpu.VMEM((n, width), BF16),
            pltpu.SemaphoreType.DMA((4,)),
            pltpu.SemaphoreType.DMA((4,)),
            pltpu.SemaphoreType.DMA((4,)),
        ],
        compiler_params=pltpu.CompilerParams(vmem_limit_bytes=LARGE),
        cost_estimate=pl.CostEstimate(flops=2 * n * width * (2 * left + count), bytes_accessed=4 * count * width, transcendentals=0),
    )(rows, hidden, own, other, across, both)


def combine_kernel(where, toks, high, low, made, kept, given):
    half = made.shape[1] // 2
    low_side, core = 1 - where[1] // 2, lax.rem(where[1], 2)
    for out, h in ((kept, low_side), (given, 1 - low_side)):
        block = pl.ds(pl.multiple_of(h * half, half), half)
        part = made[:, block]
        summed = jnp.dot(high[...], part, preferred_element_type=F32)
        summed += jnp.dot(low[...], part, preferred_element_type=F32)
        if out is kept:
            summed += jnp.where(core == 0, toks[:, block].astype(F32), 0.0)
        out[...] = summed.astype(BF16)


def add_kernel(left, right, out):
    out[...] = (left[...].astype(F32) + right[...].astype(F32)).astype(out.dtype)


def join_kernel(where, own, across, out, sem):
    cols = own.shape[1]
    yl = where[1] // 2
    copies = [
        pltpu.make_async_copy(ref, out.at[:, pl.ds(pl.multiple_of(half * cols, cols), cols)], sem.at[i])
        for i, (ref, half) in enumerate(((own, yl), (across, 1 - yl)))
    ]
    for copy in copies:
        copy.start()
    for copy in copies:
        copy.wait()


def joined(where, own, across):
    toks, cols = own.shape
    return pl.pallas_call(
        join_kernel,
        out_shape=pltpu.HBM((toks, 2 * cols), BF16),
        in_specs=[SM, VM, VM],
        out_specs=ANYWHERE,
        scratch_shapes=[pltpu.SemaphoreType.DMA((2,))],
        compiler_params=pltpu.CompilerParams(vmem_limit_bytes=SMALL),
    )(where, own, across)


def spread_kernel(row, out):
    wide = row[...].astype(F32)
    for i in range(out.shape[0]):
        out[i] = wide


def image_kernel(sizes, where, arrived, gain, weigh, first, first_other, second, second_other, mine, theirs, *scratch):
    n_yh, n_z = sizes
    rows_v, first_v, first_other_v, second_v, second_other_v, sem = scratch
    count = 2 * n_yh
    copies = [
        pltpu.make_async_copy(arrived.at[i, pl.ds(0, 2 * count)], rows_v.at[i], sem.at[i]) for i in range(n_z)
    ]
    held = ((first, first_v), (first_other, first_other_v), (second, second_v), (second_other, second_other_v))
    for i, (source, target) in enumerate(held):
        copies.append(pltpu.make_async_copy(source, target, sem.at[n_z + i]))
    for copy in copies:
        copy.start()
    for copy in copies:
        copy.wait()
    dv = gain.shape[1]
    wide = rows_v[...].astype(F32)
    width = wide.shape[2]
    n = n_z * count
    wide = jnp.concatenate(
        [wide[:, :count].reshape(n, width), wide[:, count:, : dv - width].reshape(n, dv - width)], axis=1
    )
    rows = wide.astype(BF16)
    scale = lax.rsqrt(jnp.mean(wide * wide, axis=-1, keepdims=True) + 1e-06)
    normed = (wide * scale * gain[...]).astype(BF16)
    yh, yl = where[0], where[1] // 2
    at = lax.broadcasted_iota(jnp.int32, (n, n), 0)
    z = lax.rem(at, n_z)
    high = lax.rem(at // n_z + yh, n_yh)
    low = lax.rem(at // (n_z * n_yh) + yl, 2)
    source = (z * n_yh + high) * 2 + low
    order = jnp.where(lax.broadcasted_iota(jnp.int32, (n, n), 1) == source, 1.0, 0.0).astype(BF16)
    whole = None
    for w_in, w_out in ((first_v, second_v), (first_other_v, second_other_v)):
        made = nt(normed, w_in[...])
        hidden = (0.5 * made * (1.0 + lax.erf(made * np.float32(0.5**0.5)))).astype(BF16)
        turned = jnp.dot(order, hidden, preferred_element_type=F32).astype(BF16)
        part = jnp.dot(turned, w_out[...], preferred_element_type=F32)
        whole = part if whole is None else whole + part
    whole = whole * weigh[...]
    images = jnp.dot(order, rows, preferred_element_type=F32)
    mark = lax.broadcasted_iota(jnp.int32, (n, 1), 0) == where[2]
    whole = whole + jnp.where(mark, images, 0.0)
    mine[...] = whole[: n // 2]
    theirs[...] = whole[n // 2 :].astype(BF16)


def encoder_part(where, arrived, gain, weigh, weights, n_yh):
    n_z, _, width = arrived.shape
    hidden, dv = weights[0].shape
    half = n_z * n_yh
    return pl.pallas_call(
        functools.partial(image_kernel, (n_yh, n_z)),
        out_shape=(shaped((half, dv), F32), shaped((half, dv))),
        in_specs=[SM, ANYWHERE, VM, VM] + [ANYWHERE] * 4,
        out_specs=(VM, VM),
        scratch_shapes=[pltpu.VMEM((n_z, 4 * n_yh, width), BF16)]
        + [pltpu.VMEM((hidden, dv), BF16)] * 4
        + [pltpu.SemaphoreType.DMA((n_z + 4,))],
        compiler_params=pltpu.CompilerParams(vmem_limit_bytes=SMALL),
        cost_estimate=pl.CostEstimate(flops=16 * half * dv * hidden, bytes_accessed=8 * hidden * dv, transcendentals=0),
    )(where, in_hbm(arrived), gain, weigh, *[in_hbm(w) for w in weights])


def fold_kernel(held, came, keep, *sends):
    total = held[...] + came[...].astype(F32)
    n = keep.shape[0]
    keep[...] = total[:n]
    for i, send in enumerate(sends):
        send[...] = total[n + i * send.shape[0] : n + (i + 1) * send.shape[0]].astype(BF16)


def column_kernel(held, *refs):
    out = refs[-1]
    total = held[...]
    for came in refs[:-1]:
        total += came[...].astype(F32)
    for i in range(out.shape[0]):
        out[i] = total[i : i + 1]


def encoded_kernel(spread, out):
    total = spread[0]
    for i in range(1, spread.shape[0]):
        total += spread[i]
    out[...] = total.astype(BF16)


def body(
    trunk_in,
    expert_ids,
    gate_scores,
    trunk_gain,
    w_gate,
    w_up,
    w_down,
    image_in,
    image_gain,
    fc_in,
    fc_out,
    layer_scale,
):
    n_pp, n_yh, n_z = (lax.axis_size(a) for a in ("pp", "yh", "z"))
    n_tp = lax.axis_size("yl") * lax.axis_size("core")
    n_square = n_yh * n_tp
    square = ("yh", "yl", "core")
    serve = served(n_yh)
    where = jnp.stack([lax.axis_index("yh"), lax.axis_index(("yl", "core")), lax.axis_index("z")]).astype(jnp.int32)

    def fetched(value):
        pairs = [(c * n_tp + copy, a * n_tp + t) for (a, t), (c, copy) in serve.items()]
        return lax.ppermute(value, square, pairs)

    def shifted(value, axis, by):
        n = lax.axis_size(axis)
        return lax.ppermute(value, axis, [(i, (i + by) % n) for i in range(n)])

    def exchanged(value, axis):
        return lax.all_to_all(value, axis, split_axis=0, concat_axis=0, tiled=True)

    tokens = trunk_in[0]
    toks, width = tokens.shape
    sent = fetched(tokens)
    image = image_in[0]
    dv = image.shape[1]
    ring = call(spread_kernel, shaped((n_yh * 2, 1, dv), F32))(image)
    ids, ring = lax.optimization_barrier((expert_ids, ring))
    ring = exchanged(ring, ("yh", "yl"))
    meta = fetched(jnp.concatenate([ids[0].T.astype(F32), gate_scores[0].T], axis=0))
    own = jnp.concatenate([w_gate[0, 0].T, w_up[0, 0].T, w_down[0, 0]], axis=0)
    other = shifted(own, "core", 1)
    own, sent, meta, ring, where = lax.optimization_barrier((own, sent, meta, ring, where))
    across = shifted(own, "yl", 1)

    arrived = exchanged(packed(where, meta, sent, trunk_gain, ring, n_z), "z")

    first, second = fc_in[0].T, fc_out[0]
    first_other, second_other = shifted(first, "core", 1), shifted(second, "core", 1)
    n_rows = n_z * CAP
    meta, second_other = lax.optimization_barrier((meta, second_other))
    high, low = call(weigh_kernel, (shaped((toks, n_rows)), shaped((toks, n_rows))), scalars=1)(where, meta)
    across, other, first_other, second_other, high, low = lax.optimization_barrier(
        (across, other, first_other, second_other, high, low)
    )
    both = shifted(across, "core", 1)

    made = experts(arrived, own, other, across, both)
    returned = exchanged(made.reshape(n_z, CAP, width), "z").reshape(n_rows, width)
    mine, theirs = encoder_part(where, arrived, image_gain, layer_scale, (first, first_other, second, second_other), n_yh)
    mine, *theirs = call(
        fold_kernel, (shaped((n_z, dv), F32),) + tuple(shaped((n_z, dv)) for _ in range(n_yh - 1))
    )(mine, shifted(theirs, "yl", 1))
    parts = [mine] + [shifted(part, "yh", k + 1) for k, part in enumerate(theirs)]
    column = call(column_kernel, shaped((n_z, 1, dv), F32))(*parts)

    column, returned = lax.optimization_barrier((column, returned))
    half = width // 2
    pieces = call(combine_kernel, (shaped((toks, half)), shaped((toks, half))), scalars=1, flops=4 * n_rows * toks * width)(
        where, sent, high, low, returned
    )
    pieces = [
        lax.ppermute(
            piece,
            ("pp",) + square,
            [
                (s * n_square + a * n_tp + t, (s + 1) % n_pp * n_square + c * n_tp + (copy ^ flip))
                for s in range(n_pp)
                for (a, t), (c, copy) in serve.items()
            ],
        )
        for flip, piece in zip((0, 2), pieces)
    ]
    part = call(add_kernel, shaped((toks, half)))(*pieces)
    spread, part = lax.optimization_barrier((exchanged(column, "z"), part))
    layer = call(add_kernel, shaped((toks, half)))(part, shifted(part, "core", 1))
    trunk_out = joined(where, layer, shifted(layer, "yl", 1))

    encoded = call(encoded_kernel, shaped((1, dv)))(spread)
    image_out = shifted(encoded[None], "pp", -1)
    return (trunk_out[None], image_out)


def solution(mesh):
    n_pp, n_ep, n_tp = (mesh.shape[a] for a in ("pp", "ep", "tp"))
    fine = Mesh(
        np.asarray(mesh.devices).reshape(n_pp, n_tp, n_ep // n_tp, n_tp // 2, 2),
        ("pp", "yh", "z", "yl", "core"),
    )
    ep, tp = ("yh", "z"), ("yl", "core")
    return jax.shard_map(
        body,
        mesh=fine,
        in_specs=(
            P("pp", ep, None),
            P("pp", ep, None),
            P("pp", ep, None),
            P("pp", None),
            P("pp", ep, None, tp),
            P("pp", ep, None, tp),
            P("pp", ep, tp, None),
            P("pp", ep + tp, None),
            P("pp", None),
            P("pp", None, ep + tp),
            P("pp", ep + tp, None),
            P("pp", None),
        ),
        out_specs=(P("pp", ep, None), P("pp", ep + tp, None)),
        check_vma=False,
    )
```
